32 devices in a mesh: tilt: 4 (over z), pos: 8 (over y, x, core).
Axes of the slice: x: 2, y: 2, z: 4, core: 2. Of those that a mesh axis runs over, the one named last changes fastest.
Arguments:
- intensity: bfloat16 [4, 128, 256, 256], P('tilt', 'pos'), may hold values from 0 to 1
- positions: int32 [4, 128, 2], P('tilt', 'pos'), may hold values from 0 to 512, as said below
- counts: int32 [4, 8], P('tilt', 'pos'), may hold values from 8 to 16, as said below
- object_field: bfloat16 [4, 2, 768, 768], P('tilt', None, 'pos'), may hold values from 0.5 to 1.5
- probe: float32 [2, 256, 256], replicated, may hold values from -3 to 3
Outputs:
- object_grad: float32 [4, 2, 768, 768], P('tilt', None, 'pos')
- probe_grad: float32 [2, 256, 256], replicated
The draws below stay inside these ranges and needn't reach their ends.
Inputs may be any that keep to these rules, and one draw needn't show every extreme that they name: The batch pairs each flat tilt t < 2 with the steep tilt t + 2: for every position index p, counts[t, p] + counts[t + 2, p] = 24 and counts[t, p] <= 12. `positions`: the row offset of a slot of position index p lies between max(0, (p - 2) * 96) and min(512, (p + 256 // 96 + 1) * 96 - 256); column offsets lie between 0 and 512.
All inputs are finite; a program needn't handle non-finite values.
Results may differ from the reference program's by a relative error of at most 0.0017.
The reference program's roundings to bfloat16 on the way count: a program that leaves them out, or rounds other values in their place, can miss the bound.
Values may be sent and summed in bfloat16 or wider, within the bound.
A program may use at most 128 MiB of HBM per device.

```python
import math
import jax
import jax.numpy as jnp
from jax import lax

W = 256
FMAX = 16
CMIN = 8
OBJ_DEV = 96
TILTS = 4
OBJ = 768
SLOTS = 128
N_POS = 8


def draw_counts(key, part):
    paired = TILTS // 2
    offset = jax.random.randint(jax.random.fold_in(key, 17), (paired, N_POS), 0, 3).astype(jnp.int32)
    offset = offset.at[0].set(0)
    flat = CMIN + offset
    steep = FMAX - offset
    return jnp.concatenate([flat, steep], 0).astype(jnp.int32)


def draw_positions(key, part):
    slot = jnp.arange(SLOTS, dtype=jnp.int32)
    owner = slot // FMAX
    reach = W // OBJ_DEV
    lowest = jnp.maximum((owner - reach) * OBJ_DEV, 0)
    highest = jnp.minimum((owner + reach + 1) * OBJ_DEV - W, OBJ - W)
    rows = jax.random.randint(jax.random.fold_in(key, 3), (TILTS, SLOTS), lowest[None, :], highest[None, :] + 1).astype(jnp.int32)
    columns = jax.random.randint(jax.random.fold_in(key, 5), (TILTS, SLOTS), 0, OBJ - W + 1).astype(jnp.int32)
    rows = rows.at[:, 0].set(0)
    rows = rows.at[:, SLOTS - 1].set(OBJ - W)
    columns = columns.at[:, 0].set(0)
    columns = columns.at[:, SLOTS - 1].set(OBJ - W)
    return jnp.stack([rows, columns], -1).astype(jnp.int32)


def shard_levels(own_key, dims, split, low, top_value):
    gain, own = 1.0, jax.random.fold_in(own_key, 6)
    for axis_at, parts in split:
        steps = jnp.exp(jax.random.uniform(jax.random.fold_in(own, axis_at), (parts,), jnp.float32, low / len(split), top_value / len(split)))
        gain = gain * jnp.repeat(steps, dims[axis_at] // parts).reshape([-1 if axis == axis_at else 1 for axis in range(len(dims))])
    return gain


def noise(stream_key, shape, deviation, bound, kind=jnp.bfloat16):
    array = deviation * jax.random.normal(stream_key, shape, jnp.float32)
    return jnp.clip(array, min=-bound, max=bound).astype(kind)


def setup_inputs(seed: int = 0) -> dict:
    seeds = jax.random.split(jax.random.key(seed), 6)
    intensity = jnp.clip(1.0 * jax.random.uniform(seeds[0], (TILTS, SLOTS, W, W), jnp.float32) ** shard_levels(seeds[0], (TILTS, SLOTS, W, W), ((0, 4), (1, 8)), -0.2, 0.2), 0.0, 1.0).astype(jnp.bfloat16)
    positions = draw_positions(jax.random.fold_in(seeds[5], 71), 0)
    counts = draw_counts(jax.random.fold_in(seeds[5], 71), 0)
    object_field = jnp.clip(0.5 + 1.0 * jax.random.uniform(seeds[3], (TILTS, 2, OBJ, OBJ), jnp.float32) ** shard_levels(seeds[3], (TILTS, 2, OBJ, OBJ), ((0, 4), (2, 8)), -0.2, 0.2), 0.5, 1.5).astype(jnp.bfloat16)
    probe = noise(seeds[4], (2, W, W), 0.5, 3.0, jnp.float32)
    return dict(intensity=intensity, positions=positions, counts=counts, object_field=object_field, probe=probe)


def dft_tables(length):
    index = jnp.arange(length, dtype=jnp.int32)
    phase = (index[:, None] * index[None, :] % length).astype(jnp.float32) * (2.0 * math.pi / length)
    cosine = jnp.cos(phase) / math.sqrt(length)
    sine = jnp.sin(phase) / math.sqrt(length)
    forward_table = jnp.stack([jnp.stack([cosine, -sine]), jnp.stack([sine, cosine])]).astype(jnp.bfloat16)
    inverse_table = jnp.stack([jnp.stack([cosine, sine]), jnp.stack([-sine, cosine])]).astype(jnp.bfloat16)
    return (forward_table, inverse_table)

def widen(field):
    return lax.optimization_barrier(field).astype(jnp.float32)

def along_columns(field, table):
    return jnp.einsum('fcry,cdyk->fdrk', widen(field), widen(table))

def along_rows(field, table):
    return jnp.einsum('fcyk,cdyr->fdrk', widen(field), widen(table))

def frame_grads(frames, patches, probe, forward_table, inverse_table, live):
    probe_re, probe_im = (probe[0], probe[1])
    patch_re = patches[:, 0].astype(jnp.float32)
    patch_im = patches[:, 1].astype(jnp.float32)
    exit_wave = jnp.stack([probe_re * patch_re - probe_im * patch_im, probe_re * patch_im + probe_im * patch_re], 1).astype(jnp.bfloat16)
    half = along_columns(exit_wave, forward_table).astype(jnp.bfloat16)
    far = along_rows(half, forward_table)
    misfit = far[:, 0] * far[:, 0] + far[:, 1] * far[:, 1] - frames.astype(jnp.float32)
    back = (far * misfit[:, None]).astype(jnp.bfloat16)
    middle = along_rows(back, inverse_table).astype(jnp.bfloat16)
    wave = along_columns(middle, inverse_table)
    wave_re, wave_im = (wave[:, 0], wave[:, 1])
    grads = jnp.stack([probe_re * wave_re + probe_im * wave_im, probe_re * wave_im - probe_im * wave_re], 1).astype(jnp.bfloat16)
    grads = jnp.where(live[:, None, None, None], grads, jnp.zeros_like(grads))
    weight = live.astype(jnp.float32)[:, None, None]
    numer_re = lax.optimization_barrier(jnp.sum((patch_re * wave_re + patch_im * wave_im) * weight, axis=0))
    numer_im = lax.optimization_barrier(jnp.sum((patch_re * wave_im - patch_im * wave_re) * weight, axis=0))
    denom = lax.optimization_barrier(jnp.sum((patch_re * patch_re + patch_im * patch_im) * weight, axis=0))
    return (grads, jnp.stack([numer_re, numer_im]), denom)

def place_patches(total, pieces, places):
    zero = jnp.zeros((), jnp.int32)

    def add_one(index, total):
        start = (zero, places[index, 0].astype(jnp.int32), places[index, 1].astype(jnp.int32))
        current = lax.dynamic_slice(total, start, (2, W, W))
        return lax.dynamic_update_slice(total, current + pieces[index].astype(jnp.float32), start)
    return lax.fori_loop(0, pieces.shape[0], add_one, total)

def reference(intensity, positions, counts, object_field, probe):
    forward_table, inverse_table = dft_tables(W)
    lane = jnp.arange(FMAX, dtype=jnp.int32)
    zero = jnp.zeros((), jnp.int32)

    def one_tilt(carry, inputs):
        numer, denom = carry
        frames, places, column, image = inputs

        def cut(place):
            return lax.dynamic_slice(image, (zero, place[0].astype(jnp.int32), place[1].astype(jnp.int32)), (2, W, W))

        def one_block(state, block):
            total, numer, denom = state
            block_frames, block_places, block_count = block
            patches = jax.vmap(cut)(block_places)
            live = lane < block_count
            grads, numer_b, denom_b = frame_grads(block_frames, patches, probe, forward_table, inverse_table, live)
            total = place_patches(total, grads, block_places)
            return ((total, numer + numer_b, denom + denom_b), None)
        blocks = (frames.reshape(N_POS, FMAX, W, W), places.reshape(N_POS, FMAX, 2), column)
        start = (jnp.zeros((2, OBJ, OBJ), jnp.float32), numer, denom)
        (total, numer, denom), _ = lax.scan(one_block, start, blocks)
        return ((numer, denom), total)
    start = (jnp.zeros((2, W, W), jnp.float32), jnp.zeros((W, W), jnp.float32))
    (numer, denom), object_grad = lax.scan(one_tilt, start, (intensity, positions, counts, object_field))
    return (object_grad, numer / denom[None])
```

```python
import functools

import jax
import jax.numpy as jnp
import numpy as np
from jax import lax
from jax.experimental import pallas as pl
from jax.experimental.pallas import tpu as pltpu
from jax.sharding import PartitionSpec as P

LANES = 128


def dft_tables(length):
    index = np.arange(length, dtype=np.int64)
    phase = (index[:, None] * index[None, :] % length).astype(np.float64) * (
        2.0 * np.pi / length
    )
    cosine = np.cos(phase) / np.sqrt(length)
    sine = np.sin(phase) / np.sqrt(length)
    forward = np.block([[cosine, -sine], [sine, cosine]])
    inverse = np.block([[cosine, sine], [-sine, cosine]])
    return (
        jnp.asarray(forward.astype(np.float32)).astype(jnp.bfloat16),
        jnp.asarray(inverse.astype(np.float32)).astype(jnp.bfloat16),
    )


def frames_kernel(
    reach,
    tilts,
    pos_any,
    count_ref,
    frames_ref,
    band,
    probe_ref,
    fwd_ref,
    inv_ref,
    total,
    chunks_ref,
    sums_ref,
    pos_ref,
    pos_sem,
):
    fetch = pltpu.make_async_copy(pos_any, pos_ref, pos_sem)
    fetch.start()
    rows = band.shape[2] // (2 * reach + 1)
    width = probe_ref.shape[-1]
    wide = width // LANES

    total[...] = jnp.zeros_like(total)
    sums_ref[...] = jnp.zeros_like(sums_ref)
    first = (lax.axis_index("pos") - reach) * rows
    fetch.wait()

    lane = lax.broadcasted_iota(jnp.int32, (width, LANES), 1)

    def some_frames(at):
        pr, pi = probe_ref[0], probe_ref[1]
        spots, patches, exits = [], [], []
        for i in at:
            r = pos_ref[0, i] - first
            q = pos_ref[1, i]
            qb, qs = q // LANES, lax.rem(q, LANES)
            spots.append((r, qb, qs))
            near = lane < LANES - qs
            back_shift = lax.rem(LANES - qs, LANES)
            patch = []
            for c in range(2):
                rolled = [
                    pltpu.roll(band[c, qb + j, pl.ds(r, width), :], back_shift, 1)
                    for j in range(wide + 1)
                ]
                patch.append(
                    jnp.concatenate(
                        [jnp.where(near, rolled[j], rolled[j + 1]) for j in range(wide)], 1
                    )
                )
            xr, xi = patch
            patches.append((xr, xi))
            exits.append(
                jnp.concatenate(
                    [
                        (pr * xr - pi * xi).astype(jnp.bfloat16),
                        (pr * xi + pi * xr).astype(jnp.bfloat16),
                    ],
                    1,
                )
            )
        halves = jnp.dot(
            jnp.concatenate(exits, 0), fwd_ref[...], preferred_element_type=jnp.float32
        ).astype(jnp.bfloat16)
        mids = []
        for n, i in enumerate(at):
            half = halves[n * width : (n + 1) * width]
            half = jnp.concatenate([half[:, :width], half[:, width:]], 0)
            far = jnp.dot(inv_ref[...], half, preferred_element_type=jnp.float32)
            fr, fi = far[:width], far[width:]
            misfit = fr * fr + fi * fi - frames_ref[i].astype(jnp.float32)
            back = jnp.concatenate(
                [(fr * misfit).astype(jnp.bfloat16), (fi * misfit).astype(jnp.bfloat16)], 0
            )
            mid = jnp.dot(fwd_ref[...], back, preferred_element_type=jnp.float32).astype(
                jnp.bfloat16
            )
            mids.append(jnp.concatenate([mid[:width], mid[width:]], 1))
        waves = jnp.dot(
            jnp.concatenate(mids, 0), inv_ref[...], preferred_element_type=jnp.float32
        )
        sums = [0.0, 0.0, 0.0]
        for n, i in enumerate(at):
            xr, xi = patches[n]
            wave = waves[n * width : (n + 1) * width]
            wr, wi = wave[:, :width], wave[:, width:]
            sums[0] += xr * wr + xi * wi
            sums[1] += xr * wi - xi * wr
            sums[2] += xr * xr + xi * xi
            r, qb, qs = spots[n]
            far_side = lane >= qs
            for c in range(2):
                grad = pr * wr + pi * wi if c == 0 else pr * wi - pi * wr
                grad = grad.astype(jnp.bfloat16).astype(jnp.float32)
                rolled = [
                    pltpu.roll(grad[:, j * LANES : (j + 1) * LANES], qs, 1)
                    for j in range(wide)
                ]
                zero = jnp.zeros_like(rolled[0])
                for j in range(wide + 1):
                    here = rolled[j] if j < wide else zero
                    before = rolled[j - 1] if j > 0 else zero
                    total[c, qb + j, pl.ds(r, width), :] += jnp.where(far_side, here, before)
        for k in range(3):
            sums_ref[k] += sums[k]

    count = count_ref[0, 0]

    @pl.loop(0, count // 2)
    def _(i):
        some_frames([2 * i, 2 * i + 1])

    @pl.when(lax.rem(count, 2) == 1)
    def _():
        some_frames([count - 1])

    pairs, chips, _, _ = chunks_ref.shape
    chunk = chunks_ref.shape[2] // (3 * tilts)
    for e in range(pairs):
        for c in range(chips):
            for t in range(tilts):
                start = ((e * chips + c) * tilts + t) * chunk
                for k in range(3):
                    chunks_ref[e, c, pl.ds((t * 3 + k) * chunk, chunk), :] = sums_ref[
                        k, start : start + chunk, :
                    ]


def frame_sums(reach, tilts, parts, positions, count, frames, band, probe, forward, inverse):
    vmem = pl.BlockSpec(memory_space=pltpu.VMEM)
    smem = pl.BlockSpec(memory_space=pltpu.SMEM)
    return pl.pallas_call(
        functools.partial(frames_kernel, reach, tilts),
        out_shape=[
            jax.ShapeDtypeStruct(band.shape, jnp.float32),
            jax.ShapeDtypeStruct(parts, jnp.float32),
        ],
        in_specs=[vmem, smem] + [vmem] * 5,
        out_specs=[vmem] * 2,
        scratch_shapes=[
            pltpu.VMEM((3,) + probe.shape[1:], jnp.float32),
            pltpu.SMEM(positions.shape, jnp.int32),
            pltpu.SemaphoreType.DMA,
        ],
        compiler_params=pltpu.CompilerParams(vmem_limit_bytes=24 * 1024 * 1024),
    )(positions, count, frames, band, probe, forward, inverse)


def greet(tilts, devices):
    t, p = lax.axis_index("tilt"), lax.axis_index("pos")
    barrier = pltpu.get_barrier_semaphore()
    for k in range(1, devices):
        pl.semaphore_signal(
            barrier,
            inc=1,
            device_id=(t, lax.rem(p + k, devices)),
            device_id_type=pl.DeviceIdType.MESH,
        )
    for k in range(1, tilts):
        pl.semaphore_signal(
            barrier,
            inc=1,
            device_id=(lax.rem(t + k, tilts), p),
            device_id_type=pl.DeviceIdType.MESH,
        )
    pl.semaphore_wait(barrier, devices - 1 + tilts - 1)


def send(src, dst, sem_out, sem_in, tilt, pos):
    return pltpu.make_async_remote_copy(
        src_ref=src,
        dst_ref=dst,
        send_sem=sem_out,
        recv_sem=sem_in,
        device_id=(tilt, pos),
        device_id_type=pl.DeviceIdType.MESH,
    )


def relayed(devices):
    return devices == 8


def gather_kernel(
    devices,
    field_any,
    frames_any,
    probe_any,
    fwd_any,
    inv_any,
    pos_any,
    band,
    frames_ref,
    probe_ref,
    fwd_ref,
    inv_ref,
    pos_ref,
    own,
    slots,
    stage,
    out_sem,
    in_sem,
    relay_out,
    relay_in,
    local_sem,
):
    t, p = lax.axis_index("tilt"), lax.axis_index("pos")
    chip, chips = p // 2, devices // 2
    rows = own.shape[1]
    groups = own.shape[2] // LANES

    own_copy = pltpu.make_async_copy(field_any.at[0], own, local_sem.at[0])
    own_copy.start()
    loads = [
        pltpu.make_async_copy(src, dst, local_sem.at[1 + n])
        for n, (src, dst) in enumerate(
            [
                (pos_any, pos_ref),
                (probe_any, probe_ref),
                (fwd_any, fwd_ref),
                (inv_any, inv_ref),
                (frames_any.at[0], frames_ref),
            ]
        )
    ]
    greet(1, devices)
    own_copy.wait()

    def place(src, b):
        for c in range(2):
            for g in range(groups):
                band[c, g, pl.ds(b * rows, rows), :] = src[
                    c, :, g * LANES : (g + 1) * LANES
                ].astype(jnp.float32)

    def role(odd):
        partner = p - 1 if odd else p + 1
        has_left, has_right = chip > 0, chip < chips - 1
        near, far = (3, 4) if odd else (1, 0)
        onward = 4 if odd else 0
        from_partner = 1 if odd else 3
        opposite = 0 if odd else 4
        outer, inner = (has_right, has_left) if odd else (has_left, has_right)
        slot_left, slot_right = (4, 1) if odd else (3, 0)
        pos_left, pos_right = 2 * chip - 1, 2 * chip + 2

        def copy(src, slot, c, out, pos):
            return send(
                src.at[c], slots.at[slot, c], out_sem.at[out, c], in_sem.at[slot, c], t, pos
            )

        to_left = [copy(own, slot_left, c, 1, pos_left) for c in range(2)]
        to_right = [copy(own, slot_right, c, 2, pos_right) for c in range(2)]
        to_partner = [copy(own, 3 if odd else 1, c, 0, partner) for c in range(2)]
        forward = [copy(slots.at[near], onward, c, 3, partner) for c in range(2)]

        def arrived(slot, c):
            copy(own, slot, c, 0, partner).wait_recv()

        if relayed(devices):
            across = lax.rem(p + 4, 8)
            to_stage = send(own.at[1], stage, relay_out.at[0], relay_in.at[0], t, across)
            staged_right = send(
                stage, slots.at[slot_right, 1], relay_out.at[1], in_sem.at[slot_right, 1], t, 4
            )
            staged_left = send(
                stage, slots.at[slot_left, 1], relay_out.at[2], in_sem.at[slot_left, 1], t, 3
            )
            middle = (chip == 1) | (chip == 2)
            pl.when(middle)(to_stage.start)
            pl.when(has_left)(to_left[0].start)
            pl.when(has_right)(to_right[0].start)
            pl.when(has_left & (chip != 2))(to_left[1].start)
            pl.when(has_right & (chip != 1))(to_right[1].start)
        else:
            for c in range(2):
                pl.when(has_left)(to_left[c].start)
                pl.when(has_right)(to_right[c].start)
        for c in range(2):
            to_partner[c].start()
        for load in loads:
            load.start()
        for c in range(2):
            band[c, groups] = jnp.zeros(band.shape[2:], jnp.float32)
        place(own, 2)
        for c in range(2):
            arrived(from_partner, c)
        place(slots.at[from_partner], from_partner)
        if relayed(devices):

            @pl.when(chip == 0)
            def _():
                to_stage.wait_recv()
                staged_left.start()

            @pl.when(chip == 3)
            def _():
                to_stage.wait_recv()
                staged_right.start()

        @pl.when(outer)
        def _():
            for c in range(2):
                arrived(near, c)
                forward[c].start()
            place(slots.at[near], near)
            for c in range(2):
                arrived(far, c)
            place(slots.at[far], far)

        @pl.when(inner)
        def _():
            for c in range(2):
                arrived(opposite, c)
            place(slots.at[opposite], opposite)

        for load in loads:
            load.wait()
        pl.when(has_left)(to_left[0].wait_send)
        pl.when(has_right)(to_right[0].wait_send)
        if relayed(devices):
            pl.when(middle)(to_stage.wait_send)
            pl.when(has_left & (chip != 2))(to_left[1].wait_send)
            pl.when(has_right & (chip != 1))(to_right[1].wait_send)
            pl.when(chip == 0)(staged_left.wait_send)
            pl.when(chip == 3)(staged_right.wait_send)
        else:
            pl.when(has_left)(to_left[1].wait_send)
            pl.when(has_right)(to_right[1].wait_send)
        for c in range(2):
            to_partner[c].wait_send()
            pl.when(outer)(forward[c].wait_send)

    pl.when(lax.rem(p, 2) == 0)(lambda: role(False))
    pl.when(lax.rem(p, 2) == 1)(lambda: role(True))


def gather(devices, field, frames, probe, forward, inverse, positions):
    hbm = pl.BlockSpec(memory_space=pltpu.HBM)
    vmem = pl.BlockSpec(memory_space=pltpu.VMEM)
    _, planes, rows, columns = field.shape
    block = (planes, rows, columns)
    groups = columns // LANES
    dma = pltpu.SemaphoreType.DMA
    return pl.pallas_call(
        functools.partial(gather_kernel, devices),
        out_shape=[
            jax.ShapeDtypeStruct((planes, groups + 1, 5 * rows, LANES), jnp.float32),
            jax.ShapeDtypeStruct(frames.shape[1:], frames.dtype),
            jax.ShapeDtypeStruct(probe.shape, probe.dtype),
            jax.ShapeDtypeStruct(forward.shape, forward.dtype),
            jax.ShapeDtypeStruct(inverse.shape, inverse.dtype),
            jax.ShapeDtypeStruct(positions.shape, positions.dtype),
        ],
        in_specs=[hbm] * 6,
        out_specs=[vmem] * 6,
        scratch_shapes=[
            pltpu.VMEM(block, field.dtype),
            pltpu.VMEM((5,) + block, field.dtype),
            pltpu.VMEM((rows, columns), field.dtype),
            dma((4, 2)),
            dma((5, 2)),
            dma((3,)),
            dma((1,)),
            dma((6,)),
        ],
        compiler_params=pltpu.CompilerParams(
            collective_id=1, has_side_effects=True, vmem_limit_bytes=16 * 1024 * 1024
        ),
    )(field, frames, probe, forward, inverse, positions)


def exchange_kernel(tilts, devices, *refs):
    grads, sums, object_ref, probe_ref = refs[:4]
    mine, extra, from_left, from_right, near, distant, stage = refs[4:11]
    half, got0, got1, plane, column, got2, result = refs[11:18]
    obj_out, obj_in, stage_out, stage_in = refs[18:22]
    out0, in0, out1, in1, out2, in2, out3, in3, out4, in4, out5, in5 = refs[22:]
    t, p = lax.axis_index("tilt"), lax.axis_index("pos")
    chip, chips = p // 2, devices // 2
    e = lax.rem(p, 2)
    partner = p + 1 - 2 * e
    groups, rows = mine.shape[1:3]
    chunk = column.shape[0] // 2
    relay = relayed(devices)
    greet(tilts, devices)

    def block(b):
        return grads.at[:, pl.ds(0, groups), pl.ds(b * rows, rows), :]

    swap = send(sums.at[1 - e], got0, out0.at[0], in0.at[0], t, partner)

    def objects(odd, step):
        has = chip < chips - 1 if odd else chip > 0
        way = 1 if odd else -1
        middle = (chip == 1) if odd else (chip == 2)
        corner = (chip == 3) if odd else (chip == 0)
        lands = from_left if odd else from_right
        side = 0 if odd else 1
        across = lax.rem(p + 4, 8)

        def out(src, n, c, pos):
            return send(src.at[c], lands.at[c], obj_out.at[n, c], obj_in.at[side, c], t, pos)

        far = [out(distant, 0, c, p + 2 * way) for c in range(2)]
        close = [out(near, 1, c, p + way) for c in range(2)]
        to_extra = send(
            block(0 if odd else 4), extra, obj_out.at[2, 0], obj_in.at[2, 0], t, partner
        )
        to_mine = send(block(1 if odd else 3), mine, obj_out.at[2, 1], obj_in.at[2, 1], t, partner)
        if relay:
            up = [
                send(src.at[1], stage.at[n], stage_out.at[n], stage_in.at[n], t, across)
                for n, src in enumerate([distant, near])
            ]
            onto = [(5, 4), (2, 3)][side]
            on = [
                send(stage.at[n], lands.at[1], stage_out.at[2 + n], obj_in.at[side, 1], t, onto[n])
                for n in range(2)
            ]
        if step == 0:
            to_extra.start()
            b = 4 if odd else 0
            for c in range(2):
                distant[c] = grads[c, 0:groups, pl.ds(b * rows, rows), :].astype(distant.dtype)
            pl.when(has)(far[0].start)
            if relay:
                pl.when(middle)(up[0].start)
        elif step == 1:
            if relay:
                pl.when(has & ~middle)(far[1].start)
            else:
                pl.when(has)(far[1].start)
            to_mine.start()
            to_extra.wait_recv()
            b = 3 if odd else 1
            for c in range(2):
                near[c] = (
                    grads[c, 0:groups, pl.ds(b * rows, rows), :] + extra[c]
                ).astype(near.dtype)
            pl.when(has)(close[0].start)
            if relay:
                pl.when(middle)(up[1].start)
                pl.when(has & ~middle)(close[1].start)

                @pl.when(corner)
                def _():
                    up[0].wait_recv()
                    on[0].start()
            else:
                pl.when(has)(close[1].start)
        elif step == 2:
            if relay:

                @pl.when(corner)
                def _():
                    up[1].wait_recv()
                    on[1].start()
        else:
            to_mine.wait_recv()
            to_extra.wait_send()
            to_mine.wait_send()
            pl.when(has)(far[0].wait_send)
            pl.when(has)(close[0].wait_send)
            if relay:
                for n, direct in enumerate([far[1], close[1]]):
                    pl.when(has & ~middle)(direct.wait_send)
                    pl.when(middle)(up[n].wait_send)
                    pl.when(corner)(on[n].wait_send)
            else:
                pl.when(has)(far[1].wait_send)
                pl.when(has)(close[1].wait_send)

    def both(step):
        pl.when(e == 0)(lambda: objects(False, step))
        pl.when(e == 1)(lambda: objects(True, step))

    swap.start()
    both(0)
    swap.wait_recv()
    half[...] = (sums[e] + got0[...]).astype(half.dtype)
    round1 = []
    for k in range(1, chips):
        other = lax.rem(chip + k, chips)
        round1.append(
            send(half.at[other], got1.at[k - 1], out1.at[k - 1], in1.at[k - 1], t, 2 * other + e)
        )
        round1[-1].start()
    both(1)
    total = sums[e, chip] + got0[chip]
    for k in range(1, chips):
        round1[k - 1].wait_recv()
        total = total + got1[k - 1].astype(jnp.float32)
    for s in range(tilts):
        plane[s] = total[s * 3 * chunk : (s + 1) * 3 * chunk]
    round2 = []
    for k in range(1, tilts):
        other = lax.rem(t + k, tilts)
        round2.append(
            send(plane.at[other], got2.at[k - 1], out2.at[k - 1], in2.at[k - 1], other, p)
        )
        round2[-1].start()
    both(2)
    total = plane[t]
    for k in range(1, tilts):
        round2[k - 1].wait_recv()
        total = total + got2[k - 1]
    below = total[2 * chunk :]
    column[...] = total[: 2 * chunk] / jnp.concatenate([below, below], 0)
    result[e, chip, t] = column[...]
    round3 = []
    for k in range(1, tilts):
        other = lax.rem(t + k, tilts)
        round3.append(
            send(column, result.at[e, chip, t], out3.at[k - 1], in3.at[k - 1], other, p)
        )
        round3[-1].start()
    for k in range(1, tilts):
        round3[k - 1].wait_recv()
    round4 = []
    for k in range(1, chips):
        other = lax.rem(chip + k, chips)
        round4.append(
            send(
                result.at[e, chip],
                result.at[e, chip],
                out4.at[k - 1],
                in4.at[k - 1],
                t,
                2 * other + e,
            )
        )
        round4[-1].start()
    for k in range(1, chips):
        round4[k - 1].wait_recv()
    back = send(result.at[e], result.at[e], out5.at[0], in5.at[0], t, partner)
    back.start()

    both(3)
    for c in range(2):
        for g in range(groups):
            object_ref[0, c, :, g * LANES : (g + 1) * LANES] = (
                grads[c, g, pl.ds(2 * rows, rows), :] + mine[c, g]
            )
    for side, has, landed in [(0, chip > 0, from_left), (1, chip < chips - 1, from_right)]:

        @pl.when(has)
        def _():
            for c in range(2):
                send(
                    near.at[c], landed.at[c], obj_out.at[1, c], obj_in.at[side, c], t, partner
                ).wait_recv()
                for g in range(groups):
                    object_ref[0, c, :, g * LANES : (g + 1) * LANES] += landed[c, g].astype(
                        jnp.float32
                    )

    back.wait_recv()
    for i in range(2):
        for c in range(chips):
            for s in range(tilts):
                start = ((i * chips + c) * tilts + s) * chunk
                for k in range(2):
                    probe_ref[k, start : start + chunk, :] = result[
                        i, c, s, k * chunk : (k + 1) * chunk, :
                    ]
    swap.wait_send()
    for copy in round1 + round2 + round3 + round4:
        copy.wait_send()
    back.wait_send()


def exchange(tilts, devices, width, rows, grads, sums):
    vmem = pl.BlockSpec(memory_space=pltpu.VMEM)
    planes, groups = grads.shape[0], grads.shape[1] - 1
    _, chips, part, _ = sums.shape
    third = part // tilts
    block = (planes, groups, rows, LANES)
    dma = pltpu.SemaphoreType.DMA
    f32, bf16 = jnp.float32, jnp.bfloat16
    return pl.pallas_call(
        functools.partial(exchange_kernel, tilts, devices),
        out_shape=[
            jax.ShapeDtypeStruct((1, planes, rows, groups * LANES), f32),
            jax.ShapeDtypeStruct((2, width, width), f32),
        ],
        in_specs=[vmem] * 2,
        out_specs=[vmem] * 2,
        scratch_shapes=[pltpu.VMEM(block, f32)] * 2
        + [pltpu.VMEM(block, bf16)] * 4
        + [
            pltpu.VMEM((2,) + block[1:], bf16),
            pltpu.VMEM((chips, part, width), bf16),
            pltpu.VMEM((chips, part, width), f32),
            pltpu.VMEM((chips - 1, part, width), bf16),
            pltpu.VMEM((tilts, third, width), f32),
            pltpu.VMEM((2 * third // 3, width), f32),
            pltpu.VMEM((tilts - 1, third, width), f32),
            pltpu.VMEM((2, chips, tilts, 2 * third // 3, width), f32),
        ]
        + [dma((3, 2)), dma((3, 2)), dma((4,)), dma((2,))]
        + [dma((1,))] * 2
        + [dma((chips - 1,))] * 2
        + [dma((tilts - 1,))] * 4
        + [dma((chips - 1,))] * 2
        + [dma((1,))] * 2,
        compiler_params=pltpu.CompilerParams(
            collective_id=2, has_side_effects=True, vmem_limit_bytes=20 * 1024 * 1024
        ),
    )(grads, sums)


def local(tilts, devices, intensity, positions, counts, object_field, probe):
    width = probe.shape[-1]
    rows = object_field.shape[2]
    reach = width // rows
    assert reach == 2 and devices % 2 == 0
    forward, inverse = dft_tables(width)
    band, frames, probe_v, forward, inverse, places = gather(
        devices, object_field, intensity, probe, forward, inverse, positions[0].T
    )
    parts = (2, devices // 2, 3 * width // devices, width)
    grads, sums = frame_sums(
        reach, tilts, parts, places, counts, frames, band, probe_v, forward, inverse
    )
    return tuple(exchange(tilts, devices, width, rows, grads, sums))


def solution(mesh):
    placed = (
        P("tilt", "pos", None, None),
        P("tilt", "pos", None),
        P("tilt", "pos"),
        P("tilt", None, "pos", None),
        P(),
    )
    return jax.shard_map(
        functools.partial(local, mesh.shape["tilt"], mesh.shape["pos"]),
        mesh=mesh,
        in_specs=placed,
        out_specs=(P("tilt", None, "pos", None), P()),
        check_vma=False,
    )
```

```python
import functools

import jax
import jax.numpy as jnp
import numpy as np
from jax import lax
from jax.experimental import pallas as pl
from jax.experimental.pallas import tpu as pltpu
from jax.sharding import PartitionSpec as P

LANES = 128


def dft_tables(length):
    index = np.arange(length, dtype=np.int64)
    phase = (index[:, None] * index[None, :] % length).astype(np.float64) * (
        2.0 * np.pi / length
    )
    cosine = np.cos(phase) / np.sqrt(length)
    sine = np.sin(phase) / np.sqrt(length)
    forward = np.block([[cosine, -sine], [sine, cosine]])
    inverse = np.block([[cosine, sine], [-sine, cosine]])
    return (
        jnp.asarray(forward.astype(np.float32)).astype(jnp.bfloat16),
        jnp.asarray(inverse.astype(np.float32)).astype(jnp.bfloat16),
    )


def frames_kernel(
    reach,
    tilts,
    pos_any,
    count_ref,
    frames_ref,
    band,
    probe_ref,
    fwd_ref,
    inv_ref,
    total,
    chunks_ref,
    sums_ref,
    pos_ref,
    pos_sem,
):
    fetch = pltpu.make_async_copy(pos_any, pos_ref, pos_sem)
    fetch.start()
    rows = band.shape[2] // (2 * reach + 1)
    width = probe_ref.shape[-1]
    wide = width // LANES

    total[...] = jnp.zeros_like(total)
    sums_ref[...] = jnp.zeros_like(sums_ref)
    first = (lax.axis_index("pos") - reach) * rows
    fetch.wait()

    lane = lax.broadcasted_iota(jnp.int32, (width, LANES), 1)

    def some_frames(at):
        pr, pi = probe_ref[0], probe_ref[1]
        spots, patches, exits = [], [], []
        for i in at:
            r = pos_ref[0, i] - first
            q = pos_ref[1, i]
            qb, qs = q // LANES, lax.rem(q, LANES)
            spots.append((r, qb, qs))
            near = lane < LANES - qs
            back_shift = lax.rem(LANES - qs, LANES)
            patch = []
            for c in range(2):
                rolled = [
                    pltpu.roll(band[c, qb + j, pl.ds(r, width), :], back_shift, 1)
                    for j in range(wide + 1)
                ]
                patch.append(
                    jnp.concatenate(
                        [jnp.where(near, rolled[j], rolled[j + 1]) for j in range(wide)], 1
                    )
                )
            xr, xi = patch
            patches.append((xr, xi))
            exits.append(
                jnp.concatenate(
                    [
                        (pr * xr - pi * xi).astype(jnp.bfloat16),
                        (pr * xi + pi * xr).astype(jnp.bfloat16),
                    ],
                    1,
                )
            )
        halves = jnp.dot(
            jnp.concatenate(exits, 0), fwd_ref[...], preferred_element_type=jnp.float32
        ).astype(jnp.bfloat16)
        mids = []
        for n, i in enumerate(at):
            half = halves[n * width : (n + 1) * width]
            half = jnp.concatenate([half[:, :width], half[:, width:]], 0)
            far = jnp.dot(inv_ref[...], half, preferred_element_type=jnp.float32)
            fr, fi = far[:width], far[width:]
            misfit = fr * fr + fi * fi - frames_ref[i].astype(jnp.float32)
            back = jnp.concatenate(
                [(fr * misfit).astype(jnp.bfloat16), (fi * misfit).astype(jnp.bfloat16)], 0
            )
            mid = jnp.dot(fwd_ref[...], back, preferred_element_type=jnp.float32).astype(
                jnp.bfloat16
            )
            mids.append(jnp.concatenate([mid[:width], mid[width:]], 1))
        waves = jnp.dot(
            jnp.concatenate(mids, 0), inv_ref[...], preferred_element_type=jnp.float32
        )
        sums = [0.0, 0.0, 0.0]
        for n, i in enumerate(at):
            xr, xi = patches[n]
            wave = waves[n * width : (n + 1) * width]
            wr, wi = wave[:, :width], wave[:, width:]
            sums[0] += xr * wr + xi * wi
            sums[1] += xr * wi - xi * wr
            sums[2] += xr * xr + xi * xi
            r, qb, qs = spots[n]
            far_side = lane >= qs
            for c in range(2):
                grad = pr * wr + pi * wi if c == 0 else pr * wi - pi * wr
                grad = grad.astype(jnp.bfloat16).astype(jnp.float32)
                rolled = [
                    pltpu.roll(grad[:, j * LANES : (j + 1) * LANES], qs, 1)
                    for j in range(wide)
                ]
                zero = jnp.zeros_like(rolled[0])
                for j in range(wide + 1):
                    here = rolled[j] if j < wide else zero
                    before = rolled[j - 1] if j > 0 else zero
                    total[c, qb + j, pl.ds(r, width), :] += jnp.where(far_side, here, before)
        for k in range(3):
            sums_ref[k] += sums[k]

    count = count_ref[0, 0]

    @pl.loop(0, count // 2)
    def _(i):
        some_frames([2 * i, 2 * i + 1])

    @pl.when(lax.rem(count, 2) == 1)
    def _():
        some_frames([count - 1])

    pairs, chips, _, _ = chunks_ref.shape
    chunk = chunks_ref.shape[2] // (3 * tilts)
    for e in range(pairs):
        for c in range(chips):
            for t in range(tilts):
                start = ((e * chips + c) * tilts + t) * chunk
                for k in range(3):
                    chunks_ref[e, c, pl.ds((t * 3 + k) * chunk, chunk), :] = sums_ref[
                        k, start : start + chunk, :
                    ]


def frame_sums(reach, tilts, parts, positions, count, frames, band, probe, forward, inverse):
    vmem = pl.BlockSpec(memory_space=pltpu.VMEM)
    smem = pl.BlockSpec(memory_space=pltpu.SMEM)
    return pl.pallas_call(
        functools.partial(frames_kernel, reach, tilts),
        out_shape=[
            jax.ShapeDtypeStruct(band.shape, jnp.float32),
            jax.ShapeDtypeStruct(parts, jnp.float32),
        ],
        in_specs=[vmem, smem] + [vmem] * 5,
        out_specs=[vmem] * 2,
        scratch_shapes=[
            pltpu.VMEM((3,) + probe.shape[1:], jnp.float32),
            pltpu.SMEM(positions.shape, jnp.int32),
            pltpu.SemaphoreType.DMA,
        ],
        compiler_params=pltpu.CompilerParams(vmem_limit_bytes=24 * 1024 * 1024),
    )(positions, count, frames, band, probe, forward, inverse)


def greet(tilts, devices):
    t, p = lax.axis_index("tilt"), lax.axis_index("pos")
    barrier = pltpu.get_barrier_semaphore()
    for k in range(1, devices):
        pl.semaphore_signal(
            barrier,
            inc=1,
            device_id=(t, lax.rem(p + k, devices)),
            device_id_type=pl.DeviceIdType.MESH,
        )
    for k in range(1, tilts):
        pl.semaphore_signal(
            barrier,
            inc=1,
            device_id=(lax.rem(t + k, tilts), p),
            device_id_type=pl.DeviceIdType.MESH,
        )
    pl.semaphore_wait(barrier, devices - 1 + tilts - 1)


def send(src, dst, sem_out, sem_in, tilt, pos):
    return pltpu.make_async_remote_copy(
        src_ref=src,
        dst_ref=dst,
        send_sem=sem_out,
        recv_sem=sem_in,
        device_id=(tilt, pos),
        device_id_type=pl.DeviceIdType.MESH,
    )


def relayed(devices):
    return devices == 8


def gather_kernel(
    devices,
    field_any,
    frames_any,
    probe_any,
    fwd_any,
    inv_any,
    pos_any,
    band,
    frames_ref,
    probe_ref,
    fwd_ref,
    inv_ref,
    pos_ref,
    own,
    slots,
    stage,
    out_sem,
    in_sem,
    relay_out,
    relay_in,
    local_sem,
):
    t, p = lax.axis_index("tilt"), lax.axis_index("pos")
    chip, chips = p // 2, devices // 2
    rows = own.shape[1]
    groups = own.shape[2] // LANES

    own_copy = pltpu.make_async_copy(field_any.at[0], own, local_sem.at[0])
    own_copy.start()
    loads = [
        pltpu.make_async_copy(src, dst, local_sem.at[1 + n])
        for n, (src, dst) in enumerate(
            [
                (pos_any, pos_ref),
                (probe_any, probe_ref),
                (fwd_any, fwd_ref),
                (inv_any, inv_ref),
                (frames_any.at[0], frames_ref),
            ]
        )
    ]
    greet(1, devices)
    own_copy.wait()

    def place(src, b):
        for c in range(2):
            for g in range(groups):
                band[c, g, pl.ds(b * rows, rows), :] = src[
                    c, :, g * LANES : (g + 1) * LANES
                ].astype(jnp.float32)

    def role(odd):
        partner = p - 1 if odd else p + 1
        has_left, has_right = chip > 0, chip < chips - 1
        near, far = (3, 4) if odd else (1, 0)
        onward = 4 if odd else 0
        from_partner = 1 if odd else 3
        opposite = 0 if odd else 4
        outer, inner = (has_right, has_left) if odd else (has_left, has_right)
        slot_left, slot_right = (4, 1) if odd else (3, 0)
        pos_left, pos_right = 2 * chip - 1, 2 * chip + 2

        def copy(src, slot, c, out, pos):
            return send(
                src.at[c], slots.at[slot, c], out_sem.at[out, c], in_sem.at[slot, c], t, pos
            )

        to_left = [copy(own, slot_left, c, 1, pos_left) for c in range(2)]
        to_right = [copy(own, slot_right, c, 2, pos_right) for c in range(2)]
        to_partner = [copy(own, 3 if odd else 1, c, 0, partner) for c in range(2)]
        forward = [copy(slots.at[near], onward, c, 3, partner) for c in range(2)]

        def arrived(slot, c):
            copy(own, slot, c, 0, partner).wait_recv()

        if relayed(devices):
            across = lax.rem(p + 4, 8)
            to_stage = send(own.at[1], stage, relay_out.at[0], relay_in.at[0], t, across)
            staged_right = send(
                stage, slots.at[slot_right, 1], relay_out.at[1], in_sem.at[slot_right, 1], t, 4
            )
            staged_left = send(
                stage, slots.at[slot_left, 1], relay_out.at[2], in_sem.at[slot_left, 1], t, 3
            )
            middle = (chip == 1) | (chip == 2)
            pl.when(middle)(to_stage.start)
            pl.when(has_left)(to_left[0].start)
            pl.when(has_right)(to_right[0].start)
            pl.when(has_left & (chip != 2))(to_left[1].start)
            pl.when(has_right & (chip != 1))(to_right[1].start)
        else:
            for c in range(2):
                pl.when(has_left)(to_left[c].start)
                pl.when(has_right)(to_right[c].start)
        for c in range(2):
            to_partner[c].start()
        for load in loads:
            load.start()
        for c in range(2):
            band[c, groups] = jnp.zeros(band.shape[2:], jnp.float32)
        place(own, 2)
        for c in range(2):
            arrived(from_partner, c)
        place(slots.at[from_partner], from_partner)
        if relayed(devices):

            @pl.when(chip == 0)
            def _():
                to_stage.wait_recv()
                staged_left.start()

            @pl.when(chip == 3)
            def _():
                to_stage.wait_recv()
                staged_right.start()

        @pl.when(outer)
        def _():
            for c in range(2):
                arrived(near, c)
                forward[c].start()
            place(slots.at[near], near)
            for c in range(2):
                arrived(far, c)
            place(slots.at[far], far)

        @pl.when(inner)
        def _():
            for c in range(2):
                arrived(opposite, c)
            place(slots.at[opposite], opposite)

        for load in loads:
            load.wait()
        pl.when(has_left)(to_left[0].wait_send)
        pl.when(has_right)(to_right[0].wait_send)
        if relayed(devices):
            pl.when(middle)(to_stage.wait_send)
            pl.when(has_left & (chip != 2))(to_left[1].wait_send)
            pl.when(has_right & (chip != 1))(to_right[1].wait_send)
            pl.when(chip == 0)(staged_left.wait_send)
            pl.when(chip == 3)(staged_right.wait_send)
        else:
            pl.when(has_left)(to_left[1].wait_send)
            pl.when(has_right)(to_right[1].wait_send)
        for c in range(2):
            to_partner[c].wait_send()
            pl.when(outer)(forward[c].wait_send)

    pl.when(lax.rem(p, 2) == 0)(lambda: role(False))
    pl.when(lax.rem(p, 2) == 1)(lambda: role(True))


def gather(devices, field, frames, probe, forward, inverse, positions):
    hbm = pl.BlockSpec(memory_space=pltpu.HBM)
    vmem = pl.BlockSpec(memory_space=pltpu.VMEM)
    _, planes, rows, columns = field.shape
    block = (planes, rows, columns)
    groups = columns // LANES
    dma = pltpu.SemaphoreType.DMA
    held = 4 * planes * (groups + 1) * 5 * rows * LANES + sum(
        a.size * a.dtype.itemsize for a in (frames, probe, forward, inverse)
    )
    return pl.pallas_call(
        functools.partial(gather_kernel, devices),
        out_shape=[
            pltpu.VMEM((planes, groups + 1, 5 * rows, LANES), jnp.float32),
            pltpu.VMEM(frames.shape[1:], frames.dtype),
            pltpu.VMEM(probe.shape, probe.dtype),
            pltpu.VMEM(forward.shape, forward.dtype),
            pltpu.VMEM(inverse.shape, inverse.dtype),
            pltpu.VMEM(positions.shape, positions.dtype),
        ],
        in_specs=[hbm] * 6,
        out_specs=[vmem] * 6,
        scratch_shapes=[
            pltpu.VMEM(block, field.dtype),
            pltpu.VMEM((5,) + block, field.dtype),
            pltpu.VMEM((rows, columns), field.dtype),
            dma((4, 2)),
            dma((5, 2)),
            dma((3,)),
            dma((1,)),
            dma((6,)),
        ],
        compiler_params=pltpu.CompilerParams(
            collective_id=1, has_side_effects=True, vmem_limit_bytes=62 * 1024 * 1024 - held
        ),
    )(field, frames, probe, forward, inverse, positions)


def exchange_kernel(tilts, devices, *refs):
    grads, sums, object_ref, probe_ref = refs[:4]
    mine, extra, from_left, from_right, near, distant, stage = refs[4:11]
    half, got0, got1, plane, column, got2, result = refs[11:18]
    obj_out, obj_in, stage_out, stage_in = refs[18:22]
    out0, in0, out1, in1, out2, in2, out3, in3, out4, in4, out5, in5 = refs[22:]
    t, p = lax.axis_index("tilt"), lax.axis_index("pos")
    chip, chips = p // 2, devices // 2
    e = lax.rem(p, 2)
    partner = p + 1 - 2 * e
    groups, rows = mine.shape[1:3]
    chunk = column.shape[0] // 2
    relay = relayed(devices)
    greet(tilts, devices)

    def block(b):
        return grads.at[:, pl.ds(0, groups), pl.ds(b * rows, rows), :]

    swap = send(sums.at[1 - e], got0, out0.at[0], in0.at[0], t, partner)

    def objects(odd, step):
        has = chip < chips - 1 if odd else chip > 0
        way = 1 if odd else -1
        middle = (chip == 1) if odd else (chip == 2)
        corner = (chip == 3) if odd else (chip == 0)
        lands = from_left if odd else from_right
        side = 0 if odd else 1
        across = lax.rem(p + 4, 8)

        def out(src, n, c, pos):
            return send(src.at[c], lands.at[c], obj_out.at[n, c], obj_in.at[side, c], t, pos)

        far = [out(distant, 0, c, p + 2 * way) for c in range(2)]
        close = [out(near, 1, c, p + way) for c in range(2)]
        to_extra = send(
            block(0 if odd else 4), extra, obj_out.at[2, 0], obj_in.at[2, 0], t, partner
        )
        to_mine = send(block(1 if odd else 3), mine, obj_out.at[2, 1], obj_in.at[2, 1], t, partner)
        if relay:
            up = [
                send(src.at[1], stage.at[n], stage_out.at[n], stage_in.at[n], t, across)
                for n, src in enumerate([distant, near])
            ]
            onto = [(5, 4), (2, 3)][side]
            on = [
                send(stage.at[n], lands.at[1], stage_out.at[2 + n], obj_in.at[side, 1], t, onto[n])
                for n in range(2)
            ]
        if step == 0:
            to_extra.start()
            b = 4 if odd else 0
            for c in range(2):
                distant[c] = grads[c, 0:groups, pl.ds(b * rows, rows), :].astype(distant.dtype)
            pl.when(has)(far[0].start)
            if relay:
                pl.when(middle)(up[0].start)
        elif step == 1:
            if relay:
                pl.when(has & ~middle)(far[1].start)
            else:
                pl.when(has)(far[1].start)
            to_mine.start()
            to_extra.wait_recv()
            b = 3 if odd else 1
            for c in range(2):
                near[c] = (
                    grads[c, 0:groups, pl.ds(b * rows, rows), :] + extra[c]
                ).astype(near.dtype)
            pl.when(has)(close[0].start)
            if relay:
                pl.when(middle)(up[1].start)
                pl.when(has & ~middle)(close[1].start)

                @pl.when(corner)
                def _():
                    up[0].wait_recv()
                    on[0].start()
            else:
                pl.when(has)(close[1].start)
        elif step == 2:
            if relay:

                @pl.when(corner)
                def _():
                    up[1].wait_recv()
                    on[1].start()
        else:
            to_mine.wait_recv()
            to_extra.wait_send()
            to_mine.wait_send()
            pl.when(has)(far[0].wait_send)
            pl.when(has)(close[0].wait_send)
            if relay:
                for n, direct in enumerate([far[1], close[1]]):
                    pl.when(has & ~middle)(direct.wait_send)
                    pl.when(middle)(up[n].wait_send)
                    pl.when(corner)(on[n].wait_send)
            else:
                pl.when(has)(far[1].wait_send)
                pl.when(has)(close[1].wait_send)

    def both(step):
        pl.when(e == 0)(lambda: objects(False, step))
        pl.when(e == 1)(lambda: objects(True, step))

    swap.start()
    both(0)
    swap.wait_recv()
    half[...] = (sums[e] + got0[...]).astype(half.dtype)
    round1 = []
    for k in range(1, chips):
        other = lax.rem(chip + k, chips)
        round1.append(
            send(half.at[other], got1.at[k - 1], out1.at[k - 1], in1.at[k - 1], t, 2 * other + e)
        )
        round1[-1].start()
    both(1)
    total = sums[e, chip] + got0[chip]
    for k in range(1, chips):
        round1[k - 1].wait_recv()
        total = total + got1[k - 1].astype(jnp.float32)
    for s in range(tilts):
        plane[s] = total[s * 3 * chunk : (s + 1) * 3 * chunk]
    round2 = []
    for k in range(1, tilts):
        other = lax.rem(t + k, tilts)
        round2.append(
            send(plane.at[other], got2.at[k - 1], out2.at[k - 1], in2.at[k - 1], other, p)
        )
        round2[-1].start()
    both(2)
    total = plane[t]
    for k in range(1, tilts):
        round2[k - 1].wait_recv()
        total = total + got2[k - 1]
    below = total[2 * chunk :]
    column[...] = total[: 2 * chunk] / jnp.concatenate([below, below], 0)
    result[e, chip, t] = column[...]
    round3 = []
    for k in range(1, tilts):
        other = lax.rem(t + k, tilts)
        round3.append(
            send(column, result.at[e, chip, t], out3.at[k - 1], in3.at[k - 1], other, p)
        )
        round3[-1].start()
    for k in range(1, tilts):
        round3[k - 1].wait_recv()
    round4 = []
    for k in range(1, chips):
        other = lax.rem(chip + k, chips)
        round4.append(
            send(
                result.at[e, chip],
                result.at[e, chip],
                out4.at[k - 1],
                in4.at[k - 1],
                t,
                2 * other + e,
            )
        )
        round4[-1].start()
    for k in range(1, chips):
        round4[k - 1].wait_recv()
    back = send(result.at[e], result.at[e], out5.at[0], in5.at[0], t, partner)
    back.start()

    both(3)
    for c in range(2):
        for g in range(groups):
            object_ref[0, c, :, g * LANES : (g + 1) * LANES] = (
                grads[c, g, pl.ds(2 * rows, rows), :] + mine[c, g]
            )
    for side, has, landed in [(0, chip > 0, from_left), (1, chip < chips - 1, from_right)]:

        @pl.when(has)
        def _():
            for c in range(2):
                send(
                    near.at[c], landed.at[c], obj_out.at[1, c], obj_in.at[side, c], t, partner
                ).wait_recv()
                for g in range(groups):
                    object_ref[0, c, :, g * LANES : (g + 1) * LANES] += landed[c, g].astype(
                        jnp.float32
                    )

    back.wait_recv()
    for i in range(2):
        for c in range(chips):
            for s in range(tilts):
                start = ((i * chips + c) * tilts + s) * chunk
                for k in range(2):
                    probe_ref[k, start : start + chunk, :] = result[
                        i, c, s, k * chunk : (k + 1) * chunk, :
                    ]
    swap.wait_send()
    for copy in round1 + round2 + round3 + round4:
        copy.wait_send()
    back.wait_send()


def exchange(tilts, devices, width, rows, grads, sums):
    vmem = pl.BlockSpec(memory_space=pltpu.VMEM)
    planes, groups = grads.shape[0], grads.shape[1] - 1
    _, chips, part, _ = sums.shape
    third = part // tilts
    block = (planes, groups, rows, LANES)
    dma = pltpu.SemaphoreType.DMA
    f32, bf16 = jnp.float32, jnp.bfloat16
    return pl.pallas_call(
        functools.partial(exchange_kernel, tilts, devices),
        out_shape=[
            jax.ShapeDtypeStruct((1, planes, rows, groups * LANES), f32),
            jax.ShapeDtypeStruct((2, width, width), f32),
        ],
        in_specs=[vmem] * 2,
        out_specs=[vmem] * 2,
        scratch_shapes=[pltpu.VMEM(block, f32)] * 2
        + [pltpu.VMEM(block, bf16)] * 4
        + [
            pltpu.VMEM((2,) + block[1:], bf16),
            pltpu.VMEM((chips, part, width), bf16),
            pltpu.VMEM((chips, part, width), f32),
            pltpu.VMEM((chips - 1, part, width), bf16),
            pltpu.VMEM((tilts, third, width), f32),
            pltpu.VMEM((2 * third // 3, width), f32),
            pltpu.VMEM((tilts - 1, third, width), f32),
            pltpu.VMEM((2, chips, tilts, 2 * third // 3, width), f32),
        ]
        + [dma((3, 2)), dma((3, 2)), dma((4,)), dma((2,))]
        + [dma((1,))] * 2
        + [dma((chips - 1,))] * 2
        + [dma((tilts - 1,))] * 4
        + [dma((chips - 1,))] * 2
        + [dma((1,))] * 2,
        compiler_params=pltpu.CompilerParams(
            collective_id=2, has_side_effects=True, vmem_limit_bytes=20 * 1024 * 1024
        ),
    )(grads, sums)


def local(tilts, devices, intensity, positions, counts, object_field, probe):
    width = probe.shape[-1]
    rows = object_field.shape[2]
    reach = width // rows
    assert reach == 2 and devices % 2 == 0
    forward, inverse = dft_tables(width)
    band, frames, probe_v, forward, inverse, places = gather(
        devices, object_field, intensity, probe, forward, inverse, positions[0].T
    )
    parts = (2, devices // 2, 3 * width // devices, width)
    grads, sums = frame_sums(
        reach, tilts, parts, places, counts, frames, band, probe_v, forward, inverse
    )
    return tuple(exchange(tilts, devices, width, rows, grads, sums))


def solution(mesh):
    placed = (
        P("tilt", "pos", None, None),
        P("tilt", "pos", None),
        P("tilt", "pos"),
        P("tilt", None, "pos", None),
        P(),
    )
    return jax.shard_map(
        functools.partial(local, mesh.shape["tilt"], mesh.shape["pos"]),
        mesh=mesh,
        in_specs=placed,
        out_specs=(P("tilt", None, "pos", None), P()),
        check_vma=False,
    )
```

```python
import functools
import math

import jax
import jax.numpy as jnp
import ml_dtypes
import numpy as np
from jax import lax
from jax.experimental import pallas as pl
from jax.experimental.pallas import tpu as pltpu
from jax.sharding import PartitionSpec as P

LANES = 128
GROUP = 4
EXTRACT = 256
SPREAD = 64


def orders(length):
    quarter, halfway = length // 4, length // 2
    low = np.concatenate([2 * np.arange(quarter), 2 * np.arange(quarter) + 1])
    mirror = (length - low) % length
    mirror[0] = halfway
    split = np.concatenate([low, mirror])
    plain = np.arange(halfway)
    mirror = (length - plain) % length
    mirror[0] = halfway
    return split, np.concatenate([plain, mirror])


def dft_tables(length):
    index = np.arange(length, dtype=np.int64)
    phase = (index[:, None] * index[None, :] % length).astype(np.float64) * (
        2.0 * np.pi / length
    )
    cosine = np.cos(phase) / np.sqrt(length)
    sine = np.sin(phase) / np.sqrt(length)
    halfway = length // 2
    rows, columns = orders(length)

    def paired(order):
        table = np.concatenate([cosine[:, order[:halfway]], sine[:, order[:halfway]]], 1)
        table[:, halfway] = cosine[:, halfway]
        return table

    forward_columns = paired(columns)
    forward_rows = paired(rows).T
    quarter = length // 4
    even = np.concatenate([rows[:quarter], rows[halfway : halfway + quarter]])
    odd = np.concatenate([rows[quarter:halfway], rows[halfway + quarter :]])

    def side(ks):
        c, s = cosine[:halfway, ks], sine[:halfway, ks]
        return np.block([[c, -s], [s, c]])

    inverse_rows = np.concatenate([side(even), side(odd)], 0)
    c, s = cosine[columns], sine[columns]
    inverse_columns = np.block([[c, s], [-s, c]])
    stack = np.concatenate([forward_columns, forward_rows, inverse_rows], 0)

    def cast(table):
        return jnp.asarray(table.astype(np.float32)).astype(jnp.bfloat16)

    return cast(stack), cast(inverse_columns)


def frames_kernel(
    reach,
    tilts,
    pos_any,
    count_ref,
    frames_ref,
    band,
    probe_ref,
    fwd_ref,
    inv_ref,
    total,
    chunks_ref,
    sums_ref,
    patch_ref,
    pos_ref,
    pos_sem,
):
    fetch = pltpu.make_async_copy(pos_any, pos_ref, pos_sem)
    fetch.start()
    rows = band.shape[2] // (2 * reach + 1)
    width = probe_ref.shape[-1]
    wide = width // LANES

    total[...] = jnp.zeros_like(total)
    sums_ref[...] = jnp.zeros_like(sums_ref)
    first = (lax.axis_index("pos") - reach) * rows
    fetch.wait()

    lane = lax.broadcasted_iota(jnp.int32, (EXTRACT, LANES), 1)
    wide_lane = lax.broadcasted_iota(jnp.int32, (SPREAD, LANES), 1)
    edge = lane == 0
    top = lax.broadcasted_iota(jnp.int32, (8, width), 0) == 0
    mid = width // 2

    def dot(a, b):
        return jnp.dot(a, b, preferred_element_type=jnp.float32)

    def some_frames(at):
        spots = []
        for i in at:
            q = pos_ref[1, i]
            spots.append((pos_ref[0, i] - first, q // LANES, lax.rem(q, LANES)))
        pieces = [[] for _ in at]
        for start in range(0, width, EXTRACT):
            pr, pi = probe_ref[0, start : start + EXTRACT], probe_ref[1, start : start + EXTRACT]
            exits = []
            for n, (r, qb, qs) in enumerate(spots):
                near = lane < LANES - qs
                back_shift = lax.rem(LANES - qs, LANES)
                patch = []
                for c in range(2):
                    rolled = [
                        pltpu.roll(band[c, qb + j, pl.ds(r + start, EXTRACT), :], back_shift, 1)
                        for j in range(wide + 1)
                    ]
                    patch.append(
                        jnp.concatenate(
                            [jnp.where(near, rolled[j], rolled[j + 1]) for j in range(wide)], 1
                        )
                    )
                    patch_ref[n, c, start : start + EXTRACT] = patch[c]
                xr, xi = patch
                exits.append((pr * xr - pi * xi).astype(jnp.bfloat16))
                exits.append((pr * xi + pi * xr).astype(jnp.bfloat16))
            out = dot(jnp.concatenate(exits, 0), fwd_ref[0:width])
            for n in range(len(at)):
                re = out[2 * n * EXTRACT : (2 * n + 1) * EXTRACT]
                im = out[(2 * n + 1) * EXTRACT : (2 * n + 2) * EXTRACT]
                u, v, uu, vv = re[:, :LANES], re[:, LANES:], im[:, :LANES], im[:, LANES:]
                pieces[n].append(
                    jnp.concatenate(
                        [
                            u + jnp.where(edge, 0.0, vv),
                            jnp.where(edge, v, u - vv),
                            uu - jnp.where(edge, 0.0, v),
                            jnp.where(edge, vv, uu + v),
                        ],
                        1,
                    ).astype(jnp.bfloat16)
                )
        backs = []
        for n, i in enumerate(at):
            far = dot(fwd_ref[width : 2 * width], jnp.concatenate(pieces[n], 0))
            u, v = far[:mid, :width], far[mid:, :width]
            uu, vv = far[:mid, width:], far[mid:, width:]
            fr = jnp.concatenate(
                [
                    u[:8] + jnp.where(top, 0.0, vv[:8]),
                    u[8:] + vv[8:],
                    jnp.where(top, v[:8], u[:8] - vv[:8]),
                    u[8:] - vv[8:],
                ],
                0,
            )
            fi = jnp.concatenate(
                [
                    uu[:8] - jnp.where(top, 0.0, v[:8]),
                    uu[8:] - v[8:],
                    jnp.where(top, vv[:8], uu[:8] + v[:8]),
                    uu[8:] + v[8:],
                ],
                0,
            )
            misfit = fr * fr + fi * fi - frames_ref[i].astype(jnp.float32)
            br = (fr * misfit).astype(jnp.bfloat16)
            bi = (fi * misfit).astype(jnp.bfloat16)
            q = mid // 2
            backs.append(
                (
                    jnp.concatenate([br[:q], br[mid : mid + q], bi[:q], bi[mid : mid + q]], 0),
                    jnp.concatenate([br[q:mid], br[mid + q :], bi[q:mid], bi[mid + q :]], 0),
                )
            )
        mids = []
        for n, i in enumerate(at):
            ev = dot(fwd_ref[2 * width : 3 * width], backs[n][0])
            od = dot(fwd_ref[3 * width :], backs[n][1])
            add, sub = (ev + od).astype(jnp.bfloat16), (ev - od).astype(jnp.bfloat16)
            mids.append(
                jnp.concatenate(
                    [
                        jnp.concatenate([add[:mid], sub[:mid]], 0),
                        jnp.concatenate([add[mid:], sub[mid:]], 0),
                    ],
                    1,
                )
            )
        for start in range(0, width, SPREAD):
            waves = dot(
                jnp.concatenate([m[start : start + SPREAD] for m in mids], 0), inv_ref[...]
            )
            pr, pi = probe_ref[0, start : start + SPREAD], probe_ref[1, start : start + SPREAD]
            sums = [0.0, 0.0, 0.0]
            for n, (r, qb, qs) in enumerate(spots):
                xr = patch_ref[n, 0, start : start + SPREAD]
                xi = patch_ref[n, 1, start : start + SPREAD]
                wave = waves[n * SPREAD : (n + 1) * SPREAD]
                wr, wi = wave[:, :width], wave[:, width:]
                sums[0] += xr * wr + xi * wi
                sums[1] += xr * wi - xi * wr
                sums[2] += xr * xr + xi * xi
                far_side = wide_lane >= qs
                for c in range(2):
                    grad = pr * wr + pi * wi if c == 0 else pr * wi - pi * wr
                    grad = grad.astype(jnp.bfloat16).astype(jnp.float32)
                    rolled = [
                        pltpu.roll(grad[:, j * LANES : (j + 1) * LANES], qs, 1)
                        for j in range(wide)
                    ]
                    zero = jnp.zeros_like(rolled[0])
                    for j in range(wide + 1):
                        here = rolled[j] if j < wide else zero
                        before = rolled[j - 1] if j > 0 else zero
                        total[c, qb + j, pl.ds(r + start, SPREAD), :] += jnp.where(
                            far_side, here, before
                        )
            for k in range(3):
                sums_ref[k, start : start + SPREAD] += sums[k]

    count = count_ref[0, 0]
    group = GROUP

    @pl.loop(0, count // group)
    def _(i):
        some_frames([group * i + n for n in range(group)])

    done = count // group * group
    for size in (2, 1):
        left = (count - done) // size

        @pl.when(left > 0)
        def _(done=done, size=size):
            some_frames([done + n for n in range(size)])

        done = done + left * size

    pairs, chips, _, _ = chunks_ref.shape
    chunk = chunks_ref.shape[2] // (3 * tilts)
    for e in range(pairs):
        for c in range(chips):
            for t in range(tilts):
                start = ((e * chips + c) * tilts + t) * chunk
                for k in range(3):
                    chunks_ref[e, c, pl.ds((t * 3 + k) * chunk, chunk), :] = sums_ref[
                        k, start : start + chunk, :
                    ]


def frame_sums(reach, tilts, parts, positions, count, frames, band, probe, forward, inverse):
    vmem = pl.BlockSpec(memory_space=pltpu.VMEM)
    smem = pl.BlockSpec(memory_space=pltpu.SMEM)
    return pl.pallas_call(
        functools.partial(frames_kernel, reach, tilts),
        out_shape=[
            jax.ShapeDtypeStruct(band.shape, jnp.float32),
            jax.ShapeDtypeStruct(parts, jnp.float32),
        ],
        in_specs=[vmem, smem] + [vmem] * 5,
        out_specs=[vmem] * 2,
        scratch_shapes=[
            pltpu.VMEM((3,) + probe.shape[1:], jnp.float32),
            pltpu.VMEM((GROUP, 2) + probe.shape[1:], jnp.float32),
            pltpu.SMEM(positions.shape, jnp.int32),
            pltpu.SemaphoreType.DMA,
        ],
        compiler_params=pltpu.CompilerParams(vmem_limit_bytes=24 * 1024 * 1024),
    )(positions, count, frames, band, probe, forward, inverse)


def greet(tilts, devices):
    t, p = lax.axis_index("tilt"), lax.axis_index("pos")
    barrier = pltpu.get_barrier_semaphore()
    for k in range(1, devices):
        pl.semaphore_signal(
            barrier,
            inc=1,
            device_id=(t, lax.rem(p + k, devices)),
            device_id_type=pl.DeviceIdType.MESH,
        )
    for k in range(1, tilts):
        pl.semaphore_signal(
            barrier,
            inc=1,
            device_id=(lax.rem(t + k, tilts), p),
            device_id_type=pl.DeviceIdType.MESH,
        )
    pl.semaphore_wait(barrier, devices - 1 + tilts - 1)


def send(src, dst, sem_out, sem_in, tilt, pos):
    return pltpu.make_async_remote_copy(
        src_ref=src,
        dst_ref=dst,
        send_sem=sem_out,
        recv_sem=sem_in,
        device_id=(tilt, pos),
        device_id_type=pl.DeviceIdType.MESH,
    )


def relayed(devices):
    return devices == 8


def gather_kernel(
    devices,
    field_any,
    frames_any,
    probe_any,
    fwd_any,
    inv_any,
    pos_any,
    moves_any,
    band,
    frames_ref,
    probe_ref,
    fwd_ref,
    inv_ref,
    pos_ref,
    own,
    slots,
    stage,
    raw_ref,
    moves_ref,
    out_sem,
    in_sem,
    relay_out,
    relay_in,
    local_sem,
):
    t, p = lax.axis_index("tilt"), lax.axis_index("pos")
    chip, chips = p // 2, devices // 2
    rows = own.shape[1]
    groups = own.shape[2] // LANES

    own_copy = pltpu.make_async_copy(field_any.at[0], own, local_sem.at[0])
    own_copy.start()
    loads = [
        pltpu.make_async_copy(src, dst, local_sem.at[1 + n])
        for n, (src, dst) in enumerate(
            [
                (pos_any, pos_ref),
                (probe_any, probe_ref),
                (fwd_any, fwd_ref),
                (inv_any, inv_ref),
                (moves_any, moves_ref),
                (frames_any.at[0], raw_ref),
            ]
        )
    ]
    greet(1, devices)
    own_copy.wait()

    def place(src, b):
        for c in range(2):
            for g in range(groups):
                band[c, g, pl.ds(b * rows, rows), :] = src[
                    c, :, g * LANES : (g + 1) * LANES
                ].astype(jnp.float32)

    def reorder():
        slots_of, width = raw_ref.shape[0], raw_ref.shape[1]
        some = math.gcd(slots_of, 4)

        @pl.loop(0, slots_of // some)
        def _(i):
            moved = jnp.dot(
                jnp.concatenate([raw_ref[i * some + n] for n in range(some)], 0),
                moves_ref[1],
                preferred_element_type=jnp.float32,
            ).astype(jnp.bfloat16)
            for n in range(some):
                frames_ref[i * some + n] = jnp.dot(
                    moves_ref[0],
                    moved[n * width : (n + 1) * width],
                    preferred_element_type=jnp.float32,
                ).astype(frames_ref.dtype)

    def role(odd):
        partner = p - 1 if odd else p + 1
        has_left, has_right = chip > 0, chip < chips - 1
        near, far = (3, 4) if odd else (1, 0)
        onward = 4 if odd else 0
        from_partner = 1 if odd else 3
        opposite = 0 if odd else 4
        outer, inner = (has_right, has_left) if odd else (has_left, has_right)
        slot_left, slot_right = (4, 1) if odd else (3, 0)
        pos_left, pos_right = 2 * chip - 1, 2 * chip + 2

        def copy(src, slot, c, out, pos):
            return send(
                src.at[c], slots.at[slot, c], out_sem.at[out, c], in_sem.at[slot, c], t, pos
            )

        to_left = [copy(own, slot_left, c, 1, pos_left) for c in range(2)]
        to_right = [copy(own, slot_right, c, 2, pos_right) for c in range(2)]
        to_partner = [copy(own, 3 if odd else 1, c, 0, partner) for c in range(2)]
        forward = [copy(slots.at[near], onward, c, 3, partner) for c in range(2)]

        def arrived(slot, c):
            copy(own, slot, c, 0, partner).wait_recv()

        if relayed(devices):
            across = lax.rem(p + 4, 8)
            to_stage = send(own.at[1], stage, relay_out.at[0], relay_in.at[0], t, across)
            staged_right = send(
                stage, slots.at[slot_right, 1], relay_out.at[1], in_sem.at[slot_right, 1], t, 4
            )
            staged_left = send(
                stage, slots.at[slot_left, 1], relay_out.at[2], in_sem.at[slot_left, 1], t, 3
            )
            middle = (chip == 1) | (chip == 2)
            pl.when(middle)(to_stage.start)
            pl.when(has_left)(to_left[0].start)
            pl.when(has_right)(to_right[0].start)
            pl.when(has_left & (chip != 2))(to_left[1].start)
            pl.when(has_right & (chip != 1))(to_right[1].start)
        else:
            for c in range(2):
                pl.when(has_left)(to_left[c].start)
                pl.when(has_right)(to_right[c].start)
        for c in range(2):
            to_partner[c].start()
        for load in loads:
            load.start()
        for c in range(2):
            band[c, groups] = jnp.zeros(band.shape[2:], jnp.float32)
        place(own, 2)
        for c in range(2):
            arrived(from_partner, c)
        place(slots.at[from_partner], from_partner)
        if relayed(devices):

            @pl.when(chip == 0)
            def _():
                to_stage.wait_recv()
                staged_left.start()

            @pl.when(chip == 3)
            def _():
                to_stage.wait_recv()
                staged_right.start()

        for load in loads:
            load.wait()
        reorder()

        @pl.when(outer)
        def _():
            for c in range(2):
                arrived(near, c)
                forward[c].start()
            place(slots.at[near], near)
            for c in range(2):
                arrived(far, c)
            place(slots.at[far], far)

        @pl.when(inner)
        def _():
            for c in range(2):
                arrived(opposite, c)
            place(slots.at[opposite], opposite)

        pl.when(has_left)(to_left[0].wait_send)
        pl.when(has_right)(to_right[0].wait_send)
        if relayed(devices):
            pl.when(middle)(to_stage.wait_send)
            pl.when(has_left & (chip != 2))(to_left[1].wait_send)
            pl.when(has_right & (chip != 1))(to_right[1].wait_send)
            pl.when(chip == 0)(staged_left.wait_send)
            pl.when(chip == 3)(staged_right.wait_send)
        else:
            pl.when(has_left)(to_left[1].wait_send)
            pl.when(has_right)(to_right[1].wait_send)
        for c in range(2):
            to_partner[c].wait_send()
            pl.when(outer)(forward[c].wait_send)

    pl.when(lax.rem(p, 2) == 0)(lambda: role(False))
    pl.when(lax.rem(p, 2) == 1)(lambda: role(True))


def gather(devices, field, frames, probe, forward, inverse, positions, moves):
    hbm = pl.BlockSpec(memory_space=pltpu.HBM)
    vmem = pl.BlockSpec(memory_space=pltpu.VMEM)
    _, planes, rows, columns = field.shape
    block = (planes, rows, columns)
    groups = columns // LANES
    dma = pltpu.SemaphoreType.DMA
    held = 4 * planes * (groups + 1) * 5 * rows * LANES + sum(
        a.size * a.dtype.itemsize for a in (frames, probe, forward, inverse)
    )
    return pl.pallas_call(
        functools.partial(gather_kernel, devices),
        out_shape=[
            pltpu.VMEM((planes, groups + 1, 5 * rows, LANES), jnp.float32),
            pltpu.VMEM(frames.shape[1:], frames.dtype),
            pltpu.VMEM(probe.shape, probe.dtype),
            pltpu.VMEM(forward.shape, forward.dtype),
            pltpu.VMEM(inverse.shape, inverse.dtype),
            pltpu.VMEM(positions.shape, positions.dtype),
        ],
        in_specs=[hbm] * 7,
        out_specs=[vmem] * 6,
        scratch_shapes=[
            pltpu.VMEM(block, field.dtype),
            pltpu.VMEM((5,) + block, field.dtype),
            pltpu.VMEM((rows, columns), field.dtype),
            pltpu.VMEM(frames.shape[1:], frames.dtype),
            pltpu.VMEM(moves.shape, moves.dtype),
            dma((4, 2)),
            dma((5, 2)),
            dma((3,)),
            dma((1,)),
            dma((7,)),
        ],
        compiler_params=pltpu.CompilerParams(
            collective_id=1, has_side_effects=True, vmem_limit_bytes=62 * 1024 * 1024 - held
        ),
    )(field, frames, probe, forward, inverse, positions, moves)


def exchange_kernel(tilts, devices, *refs):
    grads, sums, object_ref, probe_ref = refs[:4]
    mine, extra, from_left, from_right, near, distant, stage = refs[4:11]
    half, got0, got1, plane, column, got2, result = refs[11:18]
    obj_out, obj_in, stage_out, stage_in = refs[18:22]
    out0, in0, out1, in1, out2, in2, out3, in3, out4, in4, out5, in5 = refs[22:]
    t, p = lax.axis_index("tilt"), lax.axis_index("pos")
    chip, chips = p // 2, devices // 2
    e = lax.rem(p, 2)
    partner = p + 1 - 2 * e
    groups, rows = mine.shape[1:3]
    chunk = column.shape[0] // 2
    relay = relayed(devices)
    greet(tilts, devices)

    def block(b):
        return grads.at[:, pl.ds(0, groups), pl.ds(b * rows, rows), :]

    swap = send(sums.at[1 - e], got0, out0.at[0], in0.at[0], t, partner)

    def objects(odd, step):
        has = chip < chips - 1 if odd else chip > 0
        way = 1 if odd else -1
        middle = (chip == 1) if odd else (chip == 2)
        corner = (chip == 3) if odd else (chip == 0)
        lands = from_left if odd else from_right
        side = 0 if odd else 1
        across = lax.rem(p + 4, 8)

        def out(src, n, c, pos):
            return send(src.at[c], lands.at[c], obj_out.at[n, c], obj_in.at[side, c], t, pos)

        far = [out(distant, 0, c, p + 2 * way) for c in range(2)]
        close = [out(near, 1, c, p + way) for c in range(2)]
        to_extra = send(
            block(0 if odd else 4), extra, obj_out.at[2, 0], obj_in.at[2, 0], t, partner
        )
        to_mine = send(block(1 if odd else 3), mine, obj_out.at[2, 1], obj_in.at[2, 1], t, partner)
        if relay:
            up = [
                send(src.at[1], stage.at[n], stage_out.at[n], stage_in.at[n], t, across)
                for n, src in enumerate([distant, near])
            ]
            onto = [(5, 4), (2, 3)][side]
            on = [
                send(stage.at[n], lands.at[1], stage_out.at[2 + n], obj_in.at[side, 1], t, onto[n])
                for n in range(2)
            ]
        if step == 0:
            to_extra.start()
            b = 4 if odd else 0
            for c in range(2):
                distant[c] = grads[c, 0:groups, pl.ds(b * rows, rows), :].astype(distant.dtype)
            pl.when(has)(far[0].start)
            if relay:
                pl.when(middle)(up[0].start)
        elif step == 1:
            if relay:
                pl.when(has & ~middle)(far[1].start)
            else:
                pl.when(has)(far[1].start)
            to_mine.start()
            to_extra.wait_recv()
            b = 3 if odd else 1
            for c in range(2):
                near[c] = (
                    grads[c, 0:groups, pl.ds(b * rows, rows), :] + extra[c]
                ).astype(near.dtype)
            pl.when(has)(close[0].start)
            if relay:
                pl.when(middle)(up[1].start)
                pl.when(has & ~middle)(close[1].start)

                @pl.when(corner)
                def _():
                    up[0].wait_recv()
                    on[0].start()
            else:
                pl.when(has)(close[1].start)
        elif step == 2:
            if relay:

                @pl.when(corner)
                def _():
                    up[1].wait_recv()
                    on[1].start()
        else:
            to_mine.wait_recv()
            to_extra.wait_send()
            to_mine.wait_send()
            pl.when(has)(far[0].wait_send)
            pl.when(has)(close[0].wait_send)
            if relay:
                for n, direct in enumerate([far[1], close[1]]):
                    pl.when(has & ~middle)(direct.wait_send)
                    pl.when(middle)(up[n].wait_send)
                    pl.when(corner)(on[n].wait_send)
            else:
                pl.when(has)(far[1].wait_send)
                pl.when(has)(close[1].wait_send)

    def both(step):
        pl.when(e == 0)(lambda: objects(False, step))
        pl.when(e == 1)(lambda: objects(True, step))

    swap.start()
    both(0)
    swap.wait_recv()
    half[...] = (sums[e] + got0[...]).astype(half.dtype)
    round1 = []
    for k in range(1, chips):
        other = lax.rem(chip + k, chips)
        round1.append(
            send(half.at[other], got1.at[k - 1], out1.at[k - 1], in1.at[k - 1], t, 2 * other + e)
        )
        round1[-1].start()
    both(1)
    total = sums[e, chip] + got0[chip]
    for k in range(1, chips):
        round1[k - 1].wait_recv()
        total = total + got1[k - 1].astype(jnp.float32)
    for s in range(tilts):
        plane[s] = total[s * 3 * chunk : (s + 1) * 3 * chunk]
    round2 = []
    for k in range(1, tilts):
        other = lax.rem(t + k, tilts)
        round2.append(
            send(plane.at[other], got2.at[k - 1], out2.at[k - 1], in2.at[k - 1], other, p)
        )
        round2[-1].start()
    both(2)
    total = plane[t]
    for k in range(1, tilts):
        round2[k - 1].wait_recv()
        total = total + got2[k - 1]
    below = total[2 * chunk :]
    column[...] = total[: 2 * chunk] / jnp.concatenate([below, below], 0)
    result[e, chip, t] = column[...]
    round3 = []
    for k in range(1, tilts):
        other = lax.rem(t + k, tilts)
        round3.append(
            send(column, result.at[e, chip, t], out3.at[k - 1], in3.at[k - 1], other, p)
        )
        round3[-1].start()
    for k in range(1, tilts):
        round3[k - 1].wait_recv()
    round4 = []
    for k in range(1, chips):
        other = lax.rem(chip + k, chips)
        round4.append(
            send(
                result.at[e, chip],
                result.at[e, chip],
                out4.at[k - 1],
                in4.at[k - 1],
                t,
                2 * other + e,
            )
        )
        round4[-1].start()
    for k in range(1, chips):
        round4[k - 1].wait_recv()
    back = send(result.at[e], result.at[e], out5.at[0], in5.at[0], t, partner)
    back.start()

    both(3)
    for c in range(2):
        for g in range(groups):
            object_ref[0, c, :, g * LANES : (g + 1) * LANES] = (
                grads[c, g, pl.ds(2 * rows, rows), :] + mine[c, g]
            )
    for side, has, landed in [(0, chip > 0, from_left), (1, chip < chips - 1, from_right)]:

        @pl.when(has)
        def _():
            for c in range(2):
                send(
                    near.at[c], landed.at[c], obj_out.at[1, c], obj_in.at[side, c], t, partner
                ).wait_recv()
                for g in range(groups):
                    object_ref[0, c, :, g * LANES : (g + 1) * LANES] += landed[c, g].astype(
                        jnp.float32
                    )

    back.wait_recv()
    for i in range(2):
        for c in range(chips):
            for s in range(tilts):
                start = ((i * chips + c) * tilts + s) * chunk
                for k in range(2):
                    probe_ref[k, start : start + chunk, :] = result[
                        i, c, s, k * chunk : (k + 1) * chunk, :
                    ]
    swap.wait_send()
    for copy in round1 + round2 + round3 + round4:
        copy.wait_send()
    back.wait_send()


def exchange(tilts, devices, width, rows, grads, sums):
    vmem = pl.BlockSpec(memory_space=pltpu.VMEM)
    planes, groups = grads.shape[0], grads.shape[1] - 1
    _, chips, part, _ = sums.shape
    third = part // tilts
    block = (planes, groups, rows, LANES)
    dma = pltpu.SemaphoreType.DMA
    f32, bf16 = jnp.float32, jnp.bfloat16
    return pl.pallas_call(
        functools.partial(exchange_kernel, tilts, devices),
        out_shape=[
            jax.ShapeDtypeStruct((1, planes, rows, groups * LANES), f32),
            jax.ShapeDtypeStruct((2, width, width), f32),
        ],
        in_specs=[vmem] * 2,
        out_specs=[vmem] * 2,
        scratch_shapes=[pltpu.VMEM(block, f32)] * 2
        + [pltpu.VMEM(block, bf16)] * 4
        + [
            pltpu.VMEM((2,) + block[1:], bf16),
            pltpu.VMEM((chips, part, width), bf16),
            pltpu.VMEM((chips, part, width), f32),
            pltpu.VMEM((chips - 1, part, width), bf16),
            pltpu.VMEM((tilts, third, width), f32),
            pltpu.VMEM((2 * third // 3, width), f32),
            pltpu.VMEM((tilts - 1, third, width), f32),
            pltpu.VMEM((2, chips, tilts, 2 * third // 3, width), f32),
        ]
        + [dma((3, 2)), dma((3, 2)), dma((4,)), dma((2,))]
        + [dma((1,))] * 2
        + [dma((chips - 1,))] * 2
        + [dma((tilts - 1,))] * 4
        + [dma((chips - 1,))] * 2
        + [dma((1,))] * 2,
        compiler_params=pltpu.CompilerParams(
            collective_id=2, has_side_effects=True, vmem_limit_bytes=20 * 1024 * 1024
        ),
    )(grads, sums)


def local(tilts, devices, intensity, positions, counts, object_field, probe):
    width = probe.shape[-1]
    rows = object_field.shape[2]
    reach = width // rows
    assert reach == 2 and devices % 2 == 0
    forward, inverse = dft_tables(width)
    row_order, column_order = orders(width)
    identity = np.eye(width, dtype=np.float32)
    moves = jnp.asarray(
        np.stack([identity[row_order], identity[column_order].T]).astype(ml_dtypes.bfloat16)
    )
    band, frames, probe_v, forward, inverse, places = gather(
        devices, object_field, intensity, probe, forward, inverse, positions[0].T, moves
    )
    parts = (2, devices // 2, 3 * width // devices, width)
    grads, sums = frame_sums(
        reach, tilts, parts, places, counts, frames, band, probe_v, forward, inverse
    )
    return tuple(exchange(tilts, devices, width, rows, grads, sums))


def solution(mesh):
    placed = (
        P("tilt", "pos", None, None),
        P("tilt", "pos", None),
        P("tilt", "pos"),
        P("tilt", None, "pos", None),
        P(),
    )
    return jax.shard_map(
        functools.partial(local, mesh.shape["tilt"], mesh.shape["pos"]),
        mesh=mesh,
        in_specs=placed,
        out_specs=(P("tilt", None, "pos", None), P()),
        check_vma=False,
    )
```

```python
import functools
import math

import jax
import jax.numpy as jnp
import ml_dtypes
import numpy as np
from jax import lax
from jax.experimental import pallas as pl
from jax.experimental.pallas import tpu as pltpu
from jax.sharding import PartitionSpec as P

LANES = 128
GROUP = 4
EXTRACT = 256
SPREAD = 64


def orders(length):
    quarter, halfway = length // 4, length // 2
    low = np.concatenate([2 * np.arange(quarter), 2 * np.arange(quarter) + 1])
    mirror = (length - low) % length
    mirror[0] = halfway
    split = np.concatenate([low, mirror])
    plain = np.arange(halfway)
    mirror = (length - plain) % length
    mirror[0] = halfway
    return split, np.concatenate([plain, mirror])


def dft_tables(length):
    index = np.arange(length, dtype=np.int64)
    phase = (index[:, None] * index[None, :] % length).astype(np.float64) * (
        2.0 * np.pi / length
    )
    cosine = np.cos(phase) / np.sqrt(length)
    sine = np.sin(phase) / np.sqrt(length)
    halfway = length // 2
    rows, columns = orders(length)

    def paired(order):
        table = np.concatenate([cosine[:, order[:halfway]], sine[:, order[:halfway]]], 1)
        table[:, halfway] = cosine[:, halfway]
        return table

    forward_columns = paired(columns)
    forward_rows = paired(rows).T
    quarter = length // 4
    even = np.concatenate([rows[:quarter], rows[halfway : halfway + quarter]])
    odd = np.concatenate([rows[quarter:halfway], rows[halfway + quarter :]])

    def side(ks):
        c, s = cosine[:halfway, ks], sine[:halfway, ks]
        return np.block([[c, -s], [s, c]])

    inverse_rows = np.concatenate([side(even), side(odd)], 0)
    c, s = cosine[columns], sine[columns]
    inverse_columns = np.block([[c, s], [-s, c]])
    stack = np.concatenate([forward_columns, forward_rows, inverse_rows], 0)

    def cast(table):
        return jnp.asarray(table.astype(np.float32)).astype(jnp.bfloat16)

    return cast(stack), cast(inverse_columns)


def frames_kernel(
    reach,
    tilts,
    pos_any,
    count_ref,
    frames_ref,
    band,
    probe_ref,
    fwd_ref,
    inv_ref,
    total,
    chunks_ref,
    sums_ref,
    patch_ref,
    pos_ref,
    pos_sem,
):
    fetch = pltpu.make_async_copy(pos_any, pos_ref, pos_sem)
    fetch.start()
    rows = band.shape[2] // (2 * reach + 1)
    width = probe_ref.shape[-1]
    wide = width // LANES

    total[...] = jnp.zeros_like(total)
    sums_ref[...] = jnp.zeros_like(sums_ref)
    first = (lax.axis_index("pos") - reach) * rows
    fetch.wait()

    lane = lax.broadcasted_iota(jnp.int32, (EXTRACT, LANES), 1)
    wide_lane = lax.broadcasted_iota(jnp.int32, (SPREAD, LANES), 1)
    edge = lane == 0
    top = lax.broadcasted_iota(jnp.int32, (8, width), 0) == 0
    mid = width // 2

    def dot(a, b):
        return jnp.dot(a, b, preferred_element_type=jnp.float32)

    def some_frames(at):
        spots = []
        for i in at:
            q = pos_ref[1, i]
            spots.append((pos_ref[0, i] - first, q // LANES, lax.rem(q, LANES)))
        pieces = [[] for _ in at]
        for start in range(0, width, EXTRACT):
            pr, pi = probe_ref[0, start : start + EXTRACT], probe_ref[1, start : start + EXTRACT]
            exits = []
            for n, (r, qb, qs) in enumerate(spots):
                near = lane < LANES - qs
                back_shift = lax.rem(LANES - qs, LANES)
                patch = []
                for c in range(2):
                    rolled = [
                        pltpu.roll(band[c, qb + j, pl.ds(r + start, EXTRACT), :], back_shift, 1)
                        for j in range(wide + 1)
                    ]
                    patch.append(
                        jnp.concatenate(
                            [jnp.where(near, rolled[j], rolled[j + 1]) for j in range(wide)], 1
                        )
                    )
                    patch_ref[n, c, start : start + EXTRACT] = patch[c]
                xr, xi = patch
                exits.append((pr * xr - pi * xi).astype(jnp.bfloat16))
                exits.append((pr * xi + pi * xr).astype(jnp.bfloat16))
            out = dot(jnp.concatenate(exits, 0), fwd_ref[0:width])
            for n in range(len(at)):
                re = out[2 * n * EXTRACT : (2 * n + 1) * EXTRACT]
                im = out[(2 * n + 1) * EXTRACT : (2 * n + 2) * EXTRACT]
                u, v, uu, vv = re[:, :LANES], re[:, LANES:], im[:, :LANES], im[:, LANES:]
                pieces[n].append(
                    jnp.concatenate(
                        [
                            u + jnp.where(edge, 0.0, vv),
                            jnp.where(edge, v, u - vv),
                            uu - jnp.where(edge, 0.0, v),
                            jnp.where(edge, vv, uu + v),
                        ],
                        1,
                    ).astype(jnp.bfloat16)
                )
        backs = []
        for n, i in enumerate(at):
            far = dot(fwd_ref[width : 2 * width], jnp.concatenate(pieces[n], 0))
            u, v = far[:mid, :width], far[mid:, :width]
            uu, vv = far[:mid, width:], far[mid:, width:]
            fr = jnp.concatenate(
                [
                    u[:8] + jnp.where(top, 0.0, vv[:8]),
                    u[8:] + vv[8:],
                    jnp.where(top, v[:8], u[:8] - vv[:8]),
                    u[8:] - vv[8:],
                ],
                0,
            )
            fi = jnp.concatenate(
                [
                    uu[:8] - jnp.where(top, 0.0, v[:8]),
                    uu[8:] - v[8:],
                    jnp.where(top, vv[:8], uu[:8] + v[:8]),
                    uu[8:] + v[8:],
                ],
                0,
            )
            misfit = fr * fr + fi * fi - frames_ref[i].astype(jnp.float32)
            br = (fr * misfit).astype(jnp.bfloat16)
            bi = (fi * misfit).astype(jnp.bfloat16)
            q = mid // 2
            backs.append(
                (
                    jnp.concatenate([br[:q], br[mid : mid + q], bi[:q], bi[mid : mid + q]], 0),
                    jnp.concatenate([br[q:mid], br[mid + q :], bi[q:mid], bi[mid + q :]], 0),
                )
            )
        mids = []
        for n, i in enumerate(at):
            ev = dot(fwd_ref[2 * width : 3 * width], backs[n][0])
            od = dot(fwd_ref[3 * width :], backs[n][1])
            add, sub = (ev + od).astype(jnp.bfloat16), (ev - od).astype(jnp.bfloat16)
            mids.append(
                jnp.concatenate(
                    [
                        jnp.concatenate([add[:mid], sub[:mid]], 0),
                        jnp.concatenate([add[mid:], sub[mid:]], 0),
                    ],
                    1,
                )
            )
        for start in range(0, width, SPREAD):
            waves = dot(
                jnp.concatenate([m[start : start + SPREAD] for m in mids], 0), inv_ref[...]
            )
            pr, pi = probe_ref[0, start : start + SPREAD], probe_ref[1, start : start + SPREAD]
            sums = [0.0, 0.0, 0.0]
            for n, (r, qb, qs) in enumerate(spots):
                xr = patch_ref[n, 0, start : start + SPREAD]
                xi = patch_ref[n, 1, start : start + SPREAD]
                wave = waves[n * SPREAD : (n + 1) * SPREAD]
                wr, wi = wave[:, :width], wave[:, width:]
                sums[0] += xr * wr + xi * wi
                sums[1] += xr * wi - xi * wr
                sums[2] += xr * xr + xi * xi
                far_side = wide_lane >= qs
                for c in range(2):
                    grad = pr * wr + pi * wi if c == 0 else pr * wi - pi * wr
                    grad = grad.astype(jnp.bfloat16).astype(jnp.float32)
                    rolled = [
                        pltpu.roll(grad[:, j * LANES : (j + 1) * LANES], qs, 1)
                        for j in range(wide)
                    ]
                    zero = jnp.zeros_like(rolled[0])
                    for j in range(wide + 1):
                        here = rolled[j] if j < wide else zero
                        before = rolled[j - 1] if j > 0 else zero
                        total[c, qb + j, pl.ds(r + start, SPREAD), :] += jnp.where(
                            far_side, here, before
                        )
            for k in range(3):
                sums_ref[k, start : start + SPREAD] += sums[k]

    count = count_ref[0, 0]
    group = GROUP

    @pl.loop(0, count // group)
    def _(i):
        some_frames([group * i + n for n in range(group)])

    done = count // group * group
    for size in (2, 1):
        left = (count - done) // size

        @pl.when(left > 0)
        def _(done=done, size=size):
            some_frames([done + n for n in range(size)])

        done = done + left * size

    pairs, chips, _, _ = chunks_ref.shape
    chunk = chunks_ref.shape[2] // (3 * tilts)
    for e in range(pairs):
        for c in range(chips):
            for t in range(tilts):
                start = ((e * chips + c) * tilts + t) * chunk
                for k in range(3):
                    chunks_ref[e, c, pl.ds((t * 3 + k) * chunk, chunk), :] = sums_ref[
                        k, start : start + chunk, :
                    ]


def frame_sums(reach, tilts, parts, positions, count, frames, band, probe, forward, inverse):
    vmem = pl.BlockSpec(memory_space=pltpu.VMEM)
    smem = pl.BlockSpec(memory_space=pltpu.SMEM)
    return pl.pallas_call(
        functools.partial(frames_kernel, reach, tilts),
        out_shape=[
            jax.ShapeDtypeStruct(band.shape, jnp.float32),
            jax.ShapeDtypeStruct(parts, jnp.float32),
        ],
        in_specs=[vmem, smem] + [vmem] * 5,
        out_specs=[vmem] * 2,
        scratch_shapes=[
            pltpu.VMEM((3,) + probe.shape[1:], jnp.float32),
            pltpu.VMEM((GROUP, 2) + probe.shape[1:], jnp.float32),
            pltpu.SMEM(positions.shape, jnp.int32),
            pltpu.SemaphoreType.DMA,
        ],
        compiler_params=pltpu.CompilerParams(vmem_limit_bytes=24 * 1024 * 1024),
    )(positions, count, frames, band, probe, forward, inverse)


def greet(tilts, devices):
    t, p = lax.axis_index("tilt"), lax.axis_index("pos")
    barrier = pltpu.get_barrier_semaphore()
    for k in range(1, devices):
        pl.semaphore_signal(
            barrier,
            inc=1,
            device_id=(t, lax.rem(p + k, devices)),
            device_id_type=pl.DeviceIdType.MESH,
        )
    for k in range(1, tilts):
        pl.semaphore_signal(
            barrier,
            inc=1,
            device_id=(lax.rem(t + k, tilts), p),
            device_id_type=pl.DeviceIdType.MESH,
        )
    pl.semaphore_wait(barrier, devices - 1 + tilts - 1)


def send(src, dst, sem_out, sem_in, tilt, pos):
    return pltpu.make_async_remote_copy(
        src_ref=src,
        dst_ref=dst,
        send_sem=sem_out,
        recv_sem=sem_in,
        device_id=(tilt, pos),
        device_id_type=pl.DeviceIdType.MESH,
    )


def relayed(devices):
    return devices == 8


def gather_kernel(
    devices,
    field_any,
    frames_any,
    probe_any,
    fwd_any,
    inv_any,
    pos_any,
    moves_any,
    band,
    frames_ref,
    probe_ref,
    fwd_ref,
    inv_ref,
    pos_ref,
    own,
    slots,
    stage,
    raw_ref,
    moves_ref,
    out_sem,
    in_sem,
    relay_out,
    relay_in,
    local_sem,
):
    t, p = lax.axis_index("tilt"), lax.axis_index("pos")
    chip, chips = p // 2, devices // 2
    rows = own.shape[1]
    groups = own.shape[2] // LANES

    own_copy = pltpu.make_async_copy(field_any.at[0], own, local_sem.at[0])
    own_copy.start()
    loads = [
        pltpu.make_async_copy(src, dst, local_sem.at[1 + n])
        for n, (src, dst) in enumerate(
            [
                (pos_any, pos_ref),
                (probe_any, probe_ref),
                (fwd_any, fwd_ref),
                (inv_any, inv_ref),
                (moves_any, moves_ref),
                (frames_any.at[0], raw_ref),
            ]
        )
    ]
    greet(1, devices)
    own_copy.wait()

    def place(src, b):
        for c in range(2):
            for g in range(groups):
                band[c, g, pl.ds(b * rows, rows), :] = src[
                    c, :, g * LANES : (g + 1) * LANES
                ].astype(jnp.float32)

    def reorder():
        slots_of, width = raw_ref.shape[0], raw_ref.shape[1]
        some = math.gcd(slots_of, 4)

        @pl.loop(0, slots_of // some)
        def _(i):
            moved = jnp.dot(
                jnp.concatenate([raw_ref[i * some + n] for n in range(some)], 0),
                moves_ref[1],
                preferred_element_type=jnp.float32,
            ).astype(jnp.bfloat16)
            for n in range(some):
                frames_ref[i * some + n] = jnp.dot(
                    moves_ref[0],
                    moved[n * width : (n + 1) * width],
                    preferred_element_type=jnp.float32,
                ).astype(frames_ref.dtype)

    def role(odd):
        partner = p - 1 if odd else p + 1
        has_left, has_right = chip > 0, chip < chips - 1
        near, far = (3, 4) if odd else (1, 0)
        onward = 4 if odd else 0
        from_partner = 1 if odd else 3
        opposite = 0 if odd else 4
        outer, inner = (has_right, has_left) if odd else (has_left, has_right)
        slot_left, slot_right = (4, 1) if odd else (3, 0)
        pos_left, pos_right = 2 * chip - 1, 2 * chip + 2

        def copy(src, slot, c, out, pos):
            return send(
                src.at[c], slots.at[slot, c], out_sem.at[out, c], in_sem.at[slot, c], t, pos
            )

        to_left = [copy(own, slot_left, c, 1, pos_left) for c in range(2)]
        to_right = [copy(own, slot_right, c, 2, pos_right) for c in range(2)]
        to_partner = [copy(own, 3 if odd else 1, c, 0, partner) for c in range(2)]
        forward = [copy(slots.at[near], onward, c, 3, partner) for c in range(2)]

        def arrived(slot, c):
            copy(own, slot, c, 0, partner).wait_recv()

        to_near, to_far = (to_right, to_left) if odd else (to_left, to_right)
        has_near, has_far = (has_right, has_left) if odd else (has_left, has_right)
        if relayed(devices):
            across = lax.rem(p + 4, 8)
            source, relay = (chip == 2, chip == 0) if odd else (chip == 1, chip == 3)
            slot_far, pos_far = (slot_left, 3) if odd else (slot_right, 4)
            direct = has_far & ~source
            to_stage = [
                send(own.at[c], stage.at[c], relay_out.at[0, c], relay_in.at[c], t, across)
                for c in range(2)
            ]
            staged = [
                send(
                    stage.at[c],
                    slots.at[slot_far, c],
                    relay_out.at[1, c],
                    in_sem.at[slot_far, c],
                    t,
                    pos_far,
                )
                for c in range(2)
            ]
        else:
            direct = has_far
        for c in range(2):
            if relayed(devices):
                pl.when(source)(to_stage[c].start)
            pl.when(has_near)(to_near[c].start)
        for c in range(2):
            pl.when(direct)(to_far[c].start)
        for c in range(2):
            to_partner[c].start()
        for load in loads:
            load.start()
        for c in range(2):
            band[c, groups] = jnp.zeros(band.shape[2:], jnp.float32)
        place(own, 2)
        for c in range(2):
            arrived(from_partner, c)
        place(slots.at[from_partner], from_partner)
        for load in loads:
            load.wait()
        reorder()
        if relayed(devices):

            @pl.when(relay)
            def _():
                for c in range(2):
                    to_stage[c].wait_recv()
                    staged[c].start()

        @pl.when(outer)
        def _():
            for c in range(2):
                arrived(near, c)
                forward[c].start()
            place(slots.at[near], near)
            for c in range(2):
                arrived(far, c)
            place(slots.at[far], far)

        @pl.when(inner)
        def _():
            for c in range(2):
                arrived(opposite, c)
            place(slots.at[opposite], opposite)

        for c in range(2):
            pl.when(has_near)(to_near[c].wait_send)
            pl.when(direct)(to_far[c].wait_send)
            if relayed(devices):
                pl.when(source)(to_stage[c].wait_send)
                pl.when(relay)(staged[c].wait_send)
        for c in range(2):
            to_partner[c].wait_send()
            pl.when(outer)(forward[c].wait_send)

    pl.when(lax.rem(p, 2) == 0)(lambda: role(False))
    pl.when(lax.rem(p, 2) == 1)(lambda: role(True))


def gather(devices, field, frames, probe, forward, inverse, positions, moves):
    hbm = pl.BlockSpec(memory_space=pltpu.HBM)
    vmem = pl.BlockSpec(memory_space=pltpu.VMEM)
    _, planes, rows, columns = field.shape
    block = (planes, rows, columns)
    groups = columns // LANES
    dma = pltpu.SemaphoreType.DMA
    held = 4 * planes * (groups + 1) * 5 * rows * LANES + sum(
        a.size * a.dtype.itemsize for a in (frames, probe, forward, inverse)
    )
    return pl.pallas_call(
        functools.partial(gather_kernel, devices),
        out_shape=[
            pltpu.VMEM((planes, groups + 1, 5 * rows, LANES), jnp.float32),
            pltpu.VMEM(frames.shape[1:], frames.dtype),
            pltpu.VMEM(probe.shape, probe.dtype),
            pltpu.VMEM(forward.shape, forward.dtype),
            pltpu.VMEM(inverse.shape, inverse.dtype),
            pltpu.VMEM(positions.shape, positions.dtype),
        ],
        in_specs=[hbm] * 7,
        out_specs=[vmem] * 6,
        scratch_shapes=[
            pltpu.VMEM(block, field.dtype),
            pltpu.VMEM((5,) + block, field.dtype),
            pltpu.VMEM(block, field.dtype),
            pltpu.VMEM(frames.shape[1:], frames.dtype),
            pltpu.VMEM(moves.shape, moves.dtype),
            dma((4, 2)),
            dma((5, 2)),
            dma((2, 2)),
            dma((2,)),
            dma((7,)),
        ],
        compiler_params=pltpu.CompilerParams(
            collective_id=1, has_side_effects=True, vmem_limit_bytes=62 * 1024 * 1024 - held
        ),
    )(field, frames, probe, forward, inverse, positions, moves)


def exchange_kernel(tilts, devices, *refs):
    grads, sums, mine, from_left, from_right, result = refs[:6]
    extra, near, distant, stage = refs[6:10]
    half, got0, got1, plane, column, got2 = refs[10:16]
    obj_out, obj_in, stage_out, stage_in = refs[16:20]
    out0, in0, out1, in1, out2, in2, out3, in3, out4, in4, out5, in5 = refs[20:]
    t, p = lax.axis_index("tilt"), lax.axis_index("pos")
    chip, chips = p // 2, devices // 2
    e = lax.rem(p, 2)
    partner = p + 1 - 2 * e
    groups, rows = mine.shape[1:3]
    chunk = column.shape[0] // 2
    relay = relayed(devices)
    greet(tilts, devices)

    def block(b):
        return grads.at[:, pl.ds(0, groups), pl.ds(b * rows, rows), :]

    chips_rows = half.shape[1]
    pieces = out0.shape[0]
    piece = chips_rows // pieces
    per = tilts // pieces

    def cut(n):
        return pl.ds(n * piece, piece)

    swap = [
        send(
            sums.at[1 - e, :, cut(n), :], got0.at[:, cut(n), :], out0.at[n], in0.at[n], t, partner
        )
        for n in range(pieces)
    ]

    def objects(odd, step):
        has = chip < chips - 1 if odd else chip > 0
        way = 1 if odd else -1
        middle = (chip == 1) if odd else (chip == 2)
        corner = (chip == 3) if odd else (chip == 0)
        lands = from_left if odd else from_right
        side = 0 if odd else 1
        across = lax.rem(p + 4, 8)

        def out(src, n, c, pos):
            return send(src.at[c], lands.at[c], obj_out.at[n, c], obj_in.at[side, c], t, pos)

        far = [out(distant, 0, c, p + 2 * way) for c in range(2)]
        close = [out(near, 1, c, p + way) for c in range(2)]
        to_extra = send(
            block(0 if odd else 4), extra, obj_out.at[2, 0], obj_in.at[2, 0], t, partner
        )
        to_mine = send(block(1 if odd else 3), mine, obj_out.at[2, 1], obj_in.at[2, 1], t, partner)
        if relay:
            up = [
                send(src.at[1], stage.at[n], stage_out.at[n], stage_in.at[n], t, across)
                for n, src in enumerate([distant, near])
            ]
            onto = [(5, 4), (2, 3)][side]
            on = [
                send(stage.at[n], lands.at[1], stage_out.at[2 + n], obj_in.at[side, 1], t, onto[n])
                for n in range(2)
            ]
        if step == 0:
            to_extra.start()
            b = 4 if odd else 0
            for c in range(2):
                distant[c] = grads[c, 0:groups, pl.ds(b * rows, rows), :].astype(distant.dtype)
            pl.when(has)(far[0].start)
            if relay:
                pl.when(middle)(up[0].start)
        elif step == 1:
            if relay:
                pl.when(has & ~middle)(far[1].start)
            else:
                pl.when(has)(far[1].start)
            to_mine.start()
            to_extra.wait_recv()
            b = 3 if odd else 1
            for c in range(2):
                near[c] = (
                    grads[c, 0:groups, pl.ds(b * rows, rows), :] + extra[c]
                ).astype(near.dtype)
            pl.when(has)(close[0].start)
            if relay:
                pl.when(middle)(up[1].start)
                pl.when(has & ~middle)(close[1].start)

                @pl.when(corner)
                def _():
                    up[0].wait_recv()
                    on[0].start()
            else:
                pl.when(has)(close[1].start)
        elif step == 2:
            if relay:

                @pl.when(corner)
                def _():
                    up[1].wait_recv()
                    on[1].start()
        else:
            to_mine.wait_recv()
            to_extra.wait_send()
            to_mine.wait_send()
            pl.when(has)(far[0].wait_send)
            pl.when(has)(close[0].wait_send)
            if relay:
                for n, direct in enumerate([far[1], close[1]]):
                    pl.when(has & ~middle)(direct.wait_send)
                    pl.when(middle)(up[n].wait_send)
                    pl.when(corner)(on[n].wait_send)
            else:
                pl.when(has)(far[1].wait_send)
                pl.when(has)(close[1].wait_send)

    def both(step):
        pl.when(e == 0)(lambda: objects(False, step))
        pl.when(e == 1)(lambda: objects(True, step))

    for copy in swap:
        copy.start()
    both(0)
    round1 = []
    for n in range(pieces):
        swap[n].wait_recv()
        half[:, cut(n), :] = (sums[e, :, cut(n), :] + got0[:, cut(n), :]).astype(half.dtype)
        for k in range(1, chips):
            other = lax.rem(chip + k, chips)
            round1.append(
                send(
                    half.at[other, cut(n)],
                    got1.at[k - 1, cut(n)],
                    out1.at[n, k - 1],
                    in1.at[n, k - 1],
                    t,
                    2 * other + e,
                )
            )
            round1[-1].start()
    both(1)
    for n in range(pieces):
        total = sums[e, chip, cut(n)] + got0[chip, cut(n)]
        for k in range(1, chips):
            round1[n * (chips - 1) + k - 1].wait_recv()
            total = total + got1[k - 1, cut(n)].astype(jnp.float32)
        for s in range(per):
            other = n * per + s
            plane[other] = total[s * 3 * chunk : (s + 1) * 3 * chunk]

            @pl.when(t != other)
            def _(other=other):
                k = lax.rem(other - t + tilts, tilts) - 1
                send(plane.at[other], got2.at[k], out2.at[k], in2.at[k], other, p).start()

    both(2)
    total = plane[t]
    for k in range(1, tilts):
        send(plane.at[0], got2.at[k - 1], out2.at[k - 1], in2.at[k - 1], t, partner).wait_recv()
        total = total + got2[k - 1]
    below = total[2 * chunk :]
    column[...] = total[: 2 * chunk] / jnp.concatenate([below, below], 0)
    result[e, chip, t] = column[...]
    round3 = []
    for k in range(1, tilts):
        other = lax.rem(t + k, tilts)
        round3.append(
            send(column, result.at[e, chip, t], out3.at[k - 1], in3.at[k - 1], other, p)
        )
        round3[-1].start()
    order = sorted(range(tilts), key=lambda m: min(m, tilts - m))
    round4 = []
    for m in order:
        whose = lax.rem(t - m + tilts, tilts)
        if m > 0:
            round3[m - 1].wait_recv()
        for k in range(1, chips):
            other = lax.rem(chip + k, chips)
            round4.append(
                send(
                    result.at[e, chip, whose],
                    result.at[e, chip, whose],
                    out4.at[m, k - 1],
                    in4.at[m, k - 1],
                    t,
                    2 * other + e,
                )
            )
            round4[-1].start()
    both(3)
    for side, has, landed in [(0, chip > 0, from_left), (1, chip < chips - 1, from_right)]:

        @pl.when(has)
        def _():
            for c in range(2):
                send(
                    near.at[c], landed.at[c], obj_out.at[1, c], obj_in.at[side, c], t, partner
                ).wait_recv()

    back = []
    for n, m in enumerate(order):
        whose = lax.rem(t - m + tilts, tilts)
        for k in range(1, chips):
            round4[n * (chips - 1) + k - 1].wait_recv()
        back.append(
            send(result.at[e, :, whose], result.at[e, :, whose], out5.at[m], in5.at[m], t, partner)
        )
        back[-1].start()
    for copy in back:
        copy.wait_recv()
    for copy in swap + round1 + round3 + round4 + back:
        copy.wait_send()
    for k in range(1, tilts):
        send(plane.at[0], got2.at[k - 1], out2.at[k - 1], in2.at[k - 1], t, partner).wait_send()


def exchange(tilts, devices, width, rows, grads, sums):
    vmem = pl.BlockSpec(memory_space=pltpu.VMEM)
    planes, groups = grads.shape[0], grads.shape[1] - 1
    _, chips, part, _ = sums.shape
    third = part // tilts
    pieces = 2 if tilts % 2 == 0 and part % 32 == 0 else 1
    block = (planes, groups, rows, LANES)
    dma = pltpu.SemaphoreType.DMA
    f32, bf16 = jnp.float32, jnp.bfloat16
    return pl.pallas_call(
        functools.partial(exchange_kernel, tilts, devices),
        out_shape=[
            pltpu.VMEM(block, f32),
            pltpu.VMEM(block, bf16),
            pltpu.VMEM(block, bf16),
            pltpu.VMEM((2, chips, tilts, 2 * third // 3, width), f32),
        ],
        in_specs=[vmem] * 2,
        out_specs=[vmem] * 4,
        scratch_shapes=[pltpu.VMEM(block, f32)]
        + [pltpu.VMEM(block, bf16)] * 2
        + [
            pltpu.VMEM((2,) + block[1:], bf16),
            pltpu.VMEM((chips, part, width), bf16),
            pltpu.VMEM((chips, part, width), f32),
            pltpu.VMEM((chips - 1, part, width), bf16),
            pltpu.VMEM((tilts, third, width), f32),
            pltpu.VMEM((2 * third // 3, width), f32),
            pltpu.VMEM((tilts - 1, third, width), f32),
        ]
        + [dma((3, 2)), dma((3, 2)), dma((4,)), dma((2,))]
        + [dma((pieces,))] * 2
        + [dma((pieces, chips - 1))] * 2
        + [dma((tilts - 1,))] * 4
        + [dma((tilts, chips - 1))] * 2
        + [dma((tilts,))] * 2,
        compiler_params=pltpu.CompilerParams(
            collective_id=2, has_side_effects=True, vmem_limit_bytes=20 * 1024 * 1024
        ),
    )(grads, sums)


def finish_kernel(
    devices, total, mine, left, right, result, object_any, probe_any, object_ref, probe_ref, sems
):
    p = lax.axis_index("pos")
    has_left, has_right = p >= 2, p < devices - 2
    groups, rows = mine.shape[1:3]
    pairs, chips, tilts, part, _ = result.shape
    chunk = part // 2
    copies = []

    def leave(src, dst):
        copies.append(pltpu.make_async_copy(src, dst, sems.at[len(copies)]))
        copies[-1].start()

    for k in range(2):
        for i in range(pairs):
            for c in range(chips):
                for s in range(tilts):
                    start = ((i * chips + c) * tilts + s) * chunk
                    probe_ref[k, start : start + chunk, :] = result[
                        i, c, s, k * chunk : (k + 1) * chunk, :
                    ]
        leave(probe_ref.at[k], probe_any.at[k])
    for c in range(2):
        for g in range(groups):
            object_ref[c, :, g * LANES : (g + 1) * LANES] = (
                total[c, g, pl.ds(2 * rows, rows), :]
                + mine[c, g]
                + jnp.where(has_left, left[c, g].astype(jnp.float32), 0.0)
                + jnp.where(has_right, right[c, g].astype(jnp.float32), 0.0)
            )
        leave(object_ref.at[c], object_any.at[0, c])
    for copy in copies:
        copy.wait()


def finish(devices, width, total, mine, left, right, result):
    planes, groups, rows, _ = mine.shape
    vmem = pl.BlockSpec(memory_space=pltpu.VMEM)
    hbm = pl.BlockSpec(memory_space=pltpu.HBM)
    f32 = jnp.float32
    shapes = [(planes, rows, groups * LANES), (2, width, width)]
    return pl.pallas_call(
        functools.partial(finish_kernel, devices),
        out_shape=[
            jax.ShapeDtypeStruct((1,) + shapes[0], f32),
            jax.ShapeDtypeStruct(shapes[1], f32),
        ],
        in_specs=[vmem] * 5,
        out_specs=[hbm] * 2,
        scratch_shapes=[pltpu.VMEM(shape, f32) for shape in shapes]
        + [pltpu.SemaphoreType.DMA((4,))],
        compiler_params=pltpu.CompilerParams(vmem_limit_bytes=16 * 1024 * 1024),
    )(total, mine, left, right, result)


def local(tilts, devices, intensity, positions, counts, object_field, probe):
    width = probe.shape[-1]
    rows = object_field.shape[2]
    reach = width // rows
    assert reach == 2 and devices % 2 == 0
    forward, inverse = dft_tables(width)
    row_order, column_order = orders(width)
    identity = np.eye(width, dtype=np.float32)
    moves = jnp.asarray(
        np.stack([identity[row_order], identity[column_order].T]).astype(ml_dtypes.bfloat16)
    )
    band, frames, probe_v, forward, inverse, places = gather(
        devices, object_field, intensity, probe, forward, inverse, positions[0].T, moves
    )
    parts = (2, devices // 2, 3 * width // devices, width)
    grads, sums = frame_sums(
        reach, tilts, parts, places, counts, frames, band, probe_v, forward, inverse
    )
    parts = exchange(tilts, devices, width, rows, grads, sums)
    return tuple(finish(devices, width, grads, *parts))


def solution(mesh):
    placed = (
        P("tilt", "pos", None, None),
        P("tilt", "pos", None),
        P("tilt", "pos"),
        P("tilt", None, "pos", None),
        P(),
    )
    return jax.shard_map(
        functools.partial(local, mesh.shape["tilt"], mesh.shape["pos"]),
        mesh=mesh,
        in_specs=placed,
        out_specs=(P("tilt", None, "pos", None), P()),
        check_vma=False,
    )
```

```python
import functools
import math

import jax
import jax.numpy as jnp
import ml_dtypes
import numpy as np
from jax import lax
from jax.experimental import pallas as pl
from jax.experimental.pallas import tpu as pltpu
from jax.sharding import PartitionSpec as P

LANES = 128
GROUP = 4
EXTRACT = 256
SPREAD = 64


def orders(length):
    quarter, halfway = length // 4, length // 2
    low = np.concatenate([2 * np.arange(quarter), 2 * np.arange(quarter) + 1])
    mirror = (length - low) % length
    mirror[0] = halfway
    split = np.concatenate([low, mirror])
    plain = np.arange(halfway)
    mirror = (length - plain) % length
    mirror[0] = halfway
    return split, np.concatenate([plain, mirror])


def dft_tables(length):
    index = np.arange(length, dtype=np.int64)
    phase = (index[:, None] * index[None, :] % length).astype(np.float64) * (
        2.0 * np.pi / length
    )
    cosine = np.cos(phase) / np.sqrt(length)
    sine = np.sin(phase) / np.sqrt(length)
    halfway = length // 2
    rows, columns = orders(length)

    def paired(order):
        table = np.concatenate([cosine[:, order[:halfway]], sine[:, order[:halfway]]], 1)
        table[:, halfway] = cosine[:, halfway]
        return table

    forward_columns = paired(columns)
    forward_rows = paired(rows).T
    quarter = length // 4
    even = np.concatenate([rows[:quarter], rows[halfway : halfway + quarter]])
    odd = np.concatenate([rows[quarter:halfway], rows[halfway + quarter :]])

    def side(ks):
        c, s = cosine[:halfway, ks], sine[:halfway, ks]
        return np.block([[c, -s], [s, c]])

    inverse_rows = np.concatenate([side(even), side(odd)], 0)
    c, s = cosine[columns], sine[columns]
    inverse_columns = np.block([[c, s], [-s, c]])
    stack = np.concatenate([forward_columns, forward_rows, inverse_rows], 0)

    def cast(table):
        return jnp.asarray(table.astype(np.float32)).astype(jnp.bfloat16)

    return cast(stack), cast(inverse_columns)


def frames_kernel(
    reach,
    tilts,
    pos_any,
    count_ref,
    frames_ref,
    band,
    probe_ref,
    fwd_ref,
    inv_ref,
    total,
    chunks_ref,
    sums_ref,
    patch_ref,
    pos_ref,
    pos_sem,
):
    fetch = pltpu.make_async_copy(pos_any, pos_ref, pos_sem)
    fetch.start()
    rows = band.shape[2] // (2 * reach + 1)
    width = probe_ref.shape[-1]
    wide = width // LANES

    total[...] = jnp.zeros_like(total)
    sums_ref[...] = jnp.zeros_like(sums_ref)
    first = (lax.axis_index("pos") - reach) * rows
    fetch.wait()

    lane = lax.broadcasted_iota(jnp.int32, (EXTRACT, LANES), 1)
    wide_lane = lax.broadcasted_iota(jnp.int32, (SPREAD, LANES), 1)
    edge = lane == 0
    top = lax.broadcasted_iota(jnp.int32, (8, width), 0) == 0
    mid = width // 2

    def dot(a, b):
        return jnp.dot(a, b, preferred_element_type=jnp.float32)

    def some_frames(at):
        spots = []
        for i in at:
            q = pos_ref[1, i]
            spots.append((pos_ref[0, i] - first, q // LANES, lax.rem(q, LANES)))
        pieces = [[] for _ in at]
        for start in range(0, width, EXTRACT):
            pr, pi = probe_ref[0, start : start + EXTRACT], probe_ref[1, start : start + EXTRACT]
            exits = []
            for n, (r, qb, qs) in enumerate(spots):
                near = lane < LANES - qs
                back_shift = lax.rem(LANES - qs, LANES)
                patch = []
                for c in range(2):
                    rolled = [
                        pltpu.roll(band[c, qb + j, pl.ds(r + start, EXTRACT), :], back_shift, 1)
                        for j in range(wide + 1)
                    ]
                    patch.append(
                        jnp.concatenate(
                            [jnp.where(near, rolled[j], rolled[j + 1]) for j in range(wide)], 1
                        )
                    )
                    patch_ref[n, c, start : start + EXTRACT] = patch[c]
                xr, xi = patch
                exits.append((pr * xr - pi * xi).astype(jnp.bfloat16))
                exits.append((pr * xi + pi * xr).astype(jnp.bfloat16))
            out = dot(jnp.concatenate(exits, 0), fwd_ref[0:width])
            for n in range(len(at)):
                re = out[2 * n * EXTRACT : (2 * n + 1) * EXTRACT]
                im = out[(2 * n + 1) * EXTRACT : (2 * n + 2) * EXTRACT]
                u, v, uu, vv = re[:, :LANES], re[:, LANES:], im[:, :LANES], im[:, LANES:]
                pieces[n].append(
                    jnp.concatenate(
                        [
                            u + jnp.where(edge, 0.0, vv),
                            jnp.where(edge, v, u - vv),
                            uu - jnp.where(edge, 0.0, v),
                            jnp.where(edge, vv, uu + v),
                        ],
                        1,
                    ).astype(jnp.bfloat16)
                )
        backs = []
        for n, i in enumerate(at):
            far = dot(fwd_ref[width : 2 * width], jnp.concatenate(pieces[n], 0))
            u, v = far[:mid, :width], far[mid:, :width]
            uu, vv = far[:mid, width:], far[mid:, width:]
            fr = jnp.concatenate(
                [
                    u[:8] + jnp.where(top, 0.0, vv[:8]),
                    u[8:] + vv[8:],
                    jnp.where(top, v[:8], u[:8] - vv[:8]),
                    u[8:] - vv[8:],
                ],
                0,
            )
            fi = jnp.concatenate(
                [
                    uu[:8] - jnp.where(top, 0.0, v[:8]),
                    uu[8:] - v[8:],
                    jnp.where(top, vv[:8], uu[:8] + v[:8]),
                    uu[8:] + v[8:],
                ],
                0,
            )
            misfit = fr * fr + fi * fi - frames_ref[i].astype(jnp.float32)
            br = (fr * misfit).astype(jnp.bfloat16)
            bi = (fi * misfit).astype(jnp.bfloat16)
            q = mid // 2
            backs.append(
                (
                    jnp.concatenate([br[:q], br[mid : mid + q], bi[:q], bi[mid : mid + q]], 0),
                    jnp.concatenate([br[q:mid], br[mid + q :], bi[q:mid], bi[mid + q :]], 0),
                )
            )
        mids = []
        for n, i in enumerate(at):
            ev = dot(fwd_ref[2 * width : 3 * width], backs[n][0])
            od = dot(fwd_ref[3 * width :], backs[n][1])
            add, sub = (ev + od).astype(jnp.bfloat16), (ev - od).astype(jnp.bfloat16)
            mids.append(
                jnp.concatenate(
                    [
                        jnp.concatenate([add[:mid], sub[:mid]], 0),
                        jnp.concatenate([add[mid:], sub[mid:]], 0),
                    ],
                    1,
                )
            )
        for start in range(0, width, SPREAD):
            waves = dot(
                jnp.concatenate([m[start : start + SPREAD] for m in mids], 0), inv_ref[...]
            )
            pr, pi = probe_ref[0, start : start + SPREAD], probe_ref[1, start : start + SPREAD]
            sums = [0.0, 0.0, 0.0]
            for n, (r, qb, qs) in enumerate(spots):
                xr = patch_ref[n, 0, start : start + SPREAD]
                xi = patch_ref[n, 1, start : start + SPREAD]
                wave = waves[n * SPREAD : (n + 1) * SPREAD]
                wr, wi = wave[:, :width], wave[:, width:]
                sums[0] += xr * wr + xi * wi
                sums[1] += xr * wi - xi * wr
                sums[2] += xr * xr + xi * xi
                far_side = wide_lane >= qs
                for c in range(2):
                    grad = pr * wr + pi * wi if c == 0 else pr * wi - pi * wr
                    grad = grad.astype(jnp.bfloat16).astype(jnp.float32)
                    rolled = [
                        pltpu.roll(grad[:, j * LANES : (j + 1) * LANES], qs, 1)
                        for j in range(wide)
                    ]
                    zero = jnp.zeros_like(rolled[0])
                    for j in range(wide + 1):
                        here = rolled[j] if j < wide else zero
                        before = rolled[j - 1] if j > 0 else zero
                        total[c, qb + j, pl.ds(r + start, SPREAD), :] += jnp.where(
                            far_side, here, before
                        )
            for k in range(3):
                sums_ref[k, start : start + SPREAD] += sums[k]

    count = count_ref[0, 0]
    group = GROUP

    @pl.loop(0, count // group)
    def _(i):
        some_frames([group * i + n for n in range(group)])

    done = count // group * group
    for size in (2, 1):
        left = (count - done) // size

        @pl.when(left > 0)
        def _(done=done, size=size):
            some_frames([done + n for n in range(size)])

        done = done + left * size

    pairs, chips, _, _ = chunks_ref.shape
    chunk = chunks_ref.shape[2] // (3 * tilts)
    for e in range(pairs):
        for c in range(chips):
            for t in range(tilts):
                start = ((e * chips + c) * tilts + t) * chunk
                for k in range(3):
                    chunks_ref[e, c, pl.ds((t * 3 + k) * chunk, chunk), :] = sums_ref[
                        k, start : start + chunk, :
                    ]


def frame_sums(reach, tilts, parts, positions, count, frames, band, probe, forward, inverse):
    vmem = pl.BlockSpec(memory_space=pltpu.VMEM)
    smem = pl.BlockSpec(memory_space=pltpu.SMEM)
    return pl.pallas_call(
        functools.partial(frames_kernel, reach, tilts),
        out_shape=[
            jax.ShapeDtypeStruct(band.shape, jnp.float32),
            jax.ShapeDtypeStruct(parts, jnp.float32),
        ],
        in_specs=[vmem, smem] + [vmem] * 5,
        out_specs=[vmem] * 2,
        scratch_shapes=[
            pltpu.VMEM((3,) + probe.shape[1:], jnp.float32),
            pltpu.VMEM((GROUP, 2) + probe.shape[1:], jnp.float32),
            pltpu.SMEM(positions.shape, jnp.int32),
            pltpu.SemaphoreType.DMA,
        ],
        compiler_params=pltpu.CompilerParams(vmem_limit_bytes=24 * 1024 * 1024),
    )(positions, count, frames, band, probe, forward, inverse)


def greet(tilts, devices):
    t, p = lax.axis_index("tilt"), lax.axis_index("pos")
    barrier = pltpu.get_barrier_semaphore()
    for k in range(1, devices):
        pl.semaphore_signal(
            barrier,
            inc=1,
            device_id=(t, lax.rem(p + k, devices)),
            device_id_type=pl.DeviceIdType.MESH,
        )
    for k in range(1, tilts):
        pl.semaphore_signal(
            barrier,
            inc=1,
            device_id=(lax.rem(t + k, tilts), p),
            device_id_type=pl.DeviceIdType.MESH,
        )
    pl.semaphore_wait(barrier, devices - 1 + tilts - 1)


def send(src, dst, sem_out, sem_in, tilt, pos):
    return pltpu.make_async_remote_copy(
        src_ref=src,
        dst_ref=dst,
        send_sem=sem_out,
        recv_sem=sem_in,
        device_id=(tilt, pos),
        device_id_type=pl.DeviceIdType.MESH,
    )


def relayed(devices):
    return devices == 8


def gather_kernel(
    devices,
    field_any,
    frames_any,
    probe_any,
    fwd_any,
    inv_any,
    pos_any,
    moves_any,
    band,
    frames_ref,
    probe_ref,
    fwd_ref,
    inv_ref,
    pos_ref,
    own,
    slots,
    stage,
    raw_ref,
    moves_ref,
    out_sem,
    in_sem,
    relay_out,
    relay_in,
    local_sem,
):
    t, p = lax.axis_index("tilt"), lax.axis_index("pos")
    chip, chips = p // 2, devices // 2
    rows = own.shape[1]
    groups = own.shape[2] // LANES

    own_copy = pltpu.make_async_copy(field_any.at[0], own, local_sem.at[0])
    own_copy.start()
    loads = [
        pltpu.make_async_copy(src, dst, local_sem.at[1 + n])
        for n, (src, dst) in enumerate(
            [
                (pos_any, pos_ref),
                (probe_any, probe_ref),
                (fwd_any, fwd_ref),
                (inv_any, inv_ref),
                (moves_any, moves_ref),
                (frames_any.at[0], raw_ref),
            ]
        )
    ]
    greet(1, devices)
    own_copy.wait()

    def place(src, b):
        for c in range(2):
            for g in range(groups):
                band[c, g, pl.ds(b * rows, rows), :] = src[
                    c, :, g * LANES : (g + 1) * LANES
                ].astype(jnp.float32)

    def reorder():
        slots_of, width = raw_ref.shape[0], raw_ref.shape[1]
        some = math.gcd(slots_of, 4)

        @pl.loop(0, slots_of // some)
        def _(i):
            moved = jnp.dot(
                jnp.concatenate([raw_ref[i * some + n] for n in range(some)], 0),
                moves_ref[1],
                preferred_element_type=jnp.float32,
            ).astype(jnp.bfloat16)
            for n in range(some):
                frames_ref[i * some + n] = jnp.dot(
                    moves_ref[0],
                    moved[n * width : (n + 1) * width],
                    preferred_element_type=jnp.float32,
                ).astype(frames_ref.dtype)

    def role(odd):
        partner = p - 1 if odd else p + 1
        has_left, has_right = chip > 0, chip < chips - 1
        near, far = (3, 4) if odd else (1, 0)
        onward = 4 if odd else 0
        from_partner = 1 if odd else 3
        opposite = 0 if odd else 4
        outer, inner = (has_right, has_left) if odd else (has_left, has_right)
        slot_left, slot_right = (4, 1) if odd else (3, 0)
        pos_left, pos_right = 2 * chip - 1, 2 * chip + 2

        def copy(src, slot, c, out, pos):
            return send(
                src.at[c], slots.at[slot, c], out_sem.at[out, c], in_sem.at[slot, c], t, pos
            )

        to_left = [copy(own, slot_left, c, 1, pos_left) for c in range(2)]
        to_right = [copy(own, slot_right, c, 2, pos_right) for c in range(2)]
        to_partner = [copy(own, 3 if odd else 1, c, 0, partner) for c in range(2)]
        forward = [copy(slots.at[near], onward, c, 3, partner) for c in range(2)]

        def arrived(slot, c):
            copy(own, slot, c, 0, partner).wait_recv()

        to_near, to_far = (to_right, to_left) if odd else (to_left, to_right)
        has_near, has_far = (has_right, has_left) if odd else (has_left, has_right)
        if relayed(devices):
            across = lax.rem(p + 4, 8)
            source, relay = (chip == 2, chip == 0) if odd else (chip == 1, chip == 3)
            slot_far, pos_far = (slot_left, 3) if odd else (slot_right, 4)
            direct = has_far & ~source
            to_stage = [
                send(own.at[c], stage.at[c], relay_out.at[0, c], relay_in.at[c], t, across)
                for c in range(2)
            ]
            staged = [
                send(
                    stage.at[c],
                    slots.at[slot_far, c],
                    relay_out.at[1, c],
                    in_sem.at[slot_far, c],
                    t,
                    pos_far,
                )
                for c in range(2)
            ]
        else:
            direct = has_far
        for c in range(2):
            if relayed(devices):
                pl.when(source)(to_stage[c].start)
            pl.when(has_near)(to_near[c].start)
        for c in range(2):
            pl.when(direct)(to_far[c].start)
        for c in range(2):
            to_partner[c].start()
        for load in loads:
            load.start()
        for c in range(2):
            band[c, groups] = jnp.zeros(band.shape[2:], jnp.float32)
        place(own, 2)
        for c in range(2):
            arrived(from_partner, c)
        place(slots.at[from_partner], from_partner)
        for load in loads:
            load.wait()
        reorder()
        if relayed(devices):

            @pl.when(relay)
            def _():
                for c in range(2):
                    to_stage[c].wait_recv()
                    staged[c].start()

        @pl.when(outer)
        def _():
            for c in range(2):
                arrived(near, c)
                forward[c].start()
            place(slots.at[near], near)
            for c in range(2):
                arrived(far, c)
            place(slots.at[far], far)

        @pl.when(inner)
        def _():
            for c in range(2):
                arrived(opposite, c)
            place(slots.at[opposite], opposite)

        for c in range(2):
            pl.when(has_near)(to_near[c].wait_send)
            pl.when(direct)(to_far[c].wait_send)
            if relayed(devices):
                pl.when(source)(to_stage[c].wait_send)
                pl.when(relay)(staged[c].wait_send)
        for c in range(2):
            to_partner[c].wait_send()
            pl.when(outer)(forward[c].wait_send)

    pl.when(lax.rem(p, 2) == 0)(lambda: role(False))
    pl.when(lax.rem(p, 2) == 1)(lambda: role(True))


def gather(devices, field, frames, probe, forward, inverse, positions, moves):
    hbm = pl.BlockSpec(memory_space=pltpu.HBM)
    vmem = pl.BlockSpec(memory_space=pltpu.VMEM)
    _, planes, rows, columns = field.shape
    block = (planes, rows, columns)
    groups = columns // LANES
    dma = pltpu.SemaphoreType.DMA
    held = 4 * planes * (groups + 1) * 5 * rows * LANES + sum(
        a.size * a.dtype.itemsize for a in (frames, probe, forward, inverse)
    )
    return pl.pallas_call(
        functools.partial(gather_kernel, devices),
        out_shape=[
            pltpu.VMEM((planes, groups + 1, 5 * rows, LANES), jnp.float32),
            pltpu.VMEM(frames.shape[1:], frames.dtype),
            pltpu.VMEM(probe.shape, probe.dtype),
            pltpu.VMEM(forward.shape, forward.dtype),
            pltpu.VMEM(inverse.shape, inverse.dtype),
            pltpu.VMEM(positions.shape, positions.dtype),
        ],
        in_specs=[hbm] * 7,
        out_specs=[vmem] * 6,
        scratch_shapes=[
            pltpu.VMEM(block, field.dtype),
            pltpu.VMEM((5,) + block, field.dtype),
            pltpu.VMEM(block, field.dtype),
            pltpu.VMEM(frames.shape[1:], frames.dtype),
            pltpu.VMEM(moves.shape, moves.dtype),
            dma((4, 2)),
            dma((5, 2)),
            dma((2, 2)),
            dma((2,)),
            dma((7,)),
        ],
        compiler_params=pltpu.CompilerParams(
            collective_id=1, has_side_effects=True, vmem_limit_bytes=62 * 1024 * 1024 - held
        ),
    )(field, frames, probe, forward, inverse, positions, moves)


def exchange_kernel(tilts, devices, *refs):
    grads, sums, mine, from_left, from_right, result = refs[:6]
    extra, near, distant, stage = refs[6:10]
    half, got0, got1, plane, column, got2 = refs[10:16]
    obj_out, obj_in, stage_out, stage_in = refs[16:20]
    out0, in0, out1, in1, out2, in2, out3, in3, out4, in4, out5, in5 = refs[20:]
    t, p = lax.axis_index("tilt"), lax.axis_index("pos")
    chip, chips = p // 2, devices // 2
    e = lax.rem(p, 2)
    partner = p + 1 - 2 * e
    groups, rows = mine.shape[1:3]
    chunk = column.shape[0] // 2
    relay = relayed(devices)
    greet(tilts, devices)

    def block(b):
        return grads.at[:, pl.ds(0, groups), pl.ds(b * rows, rows), :]

    chips_rows = half.shape[1]
    pieces = out0.shape[0]
    piece = chips_rows // pieces
    per = tilts // pieces

    def cut(n):
        return pl.ds(n * piece, piece)

    swap = [
        send(
            sums.at[1 - e, :, cut(n), :], got0.at[:, cut(n), :], out0.at[n], in0.at[n], t, partner
        )
        for n in range(pieces)
    ]

    def objects(odd, step):
        has = chip < chips - 1 if odd else chip > 0
        way = 1 if odd else -1
        middle = (chip == 1) if odd else (chip == 2)
        corner = (chip == 3) if odd else (chip == 0)
        lands = from_left if odd else from_right
        side = 0 if odd else 1
        across = lax.rem(p + 4, 8)

        def out(src, n, c, pos):
            return send(src.at[c], lands.at[c], obj_out.at[n, c], obj_in.at[side, c], t, pos)

        far = [out(distant, 0, c, p + 2 * way) for c in range(2)]
        close = [out(near, 1, c, p + way) for c in range(2)]
        to_extra = send(
            block(0 if odd else 4), extra, obj_out.at[2, 0], obj_in.at[2, 0], t, partner
        )
        to_mine = send(block(1 if odd else 3), mine, obj_out.at[2, 1], obj_in.at[2, 1], t, partner)
        if relay:
            up = [
                send(src.at[1], stage.at[n], stage_out.at[n], stage_in.at[n], t, across)
                for n, src in enumerate([distant, near])
            ]
            onto = [(5, 4), (2, 3)][side]
            on = [
                send(stage.at[n], lands.at[1], stage_out.at[2 + n], obj_in.at[side, 1], t, onto[n])
                for n in range(2)
            ]
        if step == 0:
            to_extra.start()
            b = 4 if odd else 0
            for c in range(2):
                distant[c] = grads[c, 0:groups, pl.ds(b * rows, rows), :].astype(distant.dtype)
            if relay:
                pl.when(middle)(up[0].start)
        elif step == 1:
            if relay:
                pl.when(has)(far[0].start)
                pl.when(has & ~middle)(far[1].start)
            else:
                pl.when(has)(far[0].start)
                pl.when(has)(far[1].start)
            to_mine.start()
            to_extra.wait_recv()
            b = 3 if odd else 1
            for c in range(2):
                near[c] = (
                    grads[c, 0:groups, pl.ds(b * rows, rows), :] + extra[c]
                ).astype(near.dtype)
            pl.when(has)(close[0].start)
            if relay:
                pl.when(middle)(up[1].start)
                pl.when(has & ~middle)(close[1].start)

                @pl.when(corner)
                def _():
                    up[0].wait_recv()
                    on[0].start()
            else:
                pl.when(has)(close[1].start)
        elif step == 2:
            if relay:

                @pl.when(corner)
                def _():
                    up[1].wait_recv()
                    on[1].start()
        else:
            to_mine.wait_recv()
            to_extra.wait_send()
            to_mine.wait_send()
            pl.when(has)(far[0].wait_send)
            pl.when(has)(close[0].wait_send)
            if relay:
                for n, direct in enumerate([far[1], close[1]]):
                    pl.when(has & ~middle)(direct.wait_send)
                    pl.when(middle)(up[n].wait_send)
                    pl.when(corner)(on[n].wait_send)
            else:
                pl.when(has)(far[1].wait_send)
                pl.when(has)(close[1].wait_send)

    def both(step):
        pl.when(e == 0)(lambda: objects(False, step))
        pl.when(e == 1)(lambda: objects(True, step))

    for copy in swap:
        copy.start()
    both(0)
    round1 = []
    for n in range(pieces):
        swap[n].wait_recv()
        half[:, cut(n), :] = (sums[e, :, cut(n), :] + got0[:, cut(n), :]).astype(half.dtype)
        for k in range(1, chips):
            other = lax.rem(chip + k, chips)
            round1.append(
                send(
                    half.at[other, cut(n)],
                    got1.at[k - 1, cut(n)],
                    out1.at[n, k - 1],
                    in1.at[n, k - 1],
                    t,
                    2 * other + e,
                )
            )
            round1[-1].start()
    both(1)
    for n in range(pieces):
        total = sums[e, chip, cut(n)] + got0[chip, cut(n)]
        for k in range(1, chips):
            round1[n * (chips - 1) + k - 1].wait_recv()
            total = total + got1[k - 1, cut(n)].astype(jnp.float32)
        for s in range(per):
            other = n * per + s
            plane[other] = total[s * 3 * chunk : (s + 1) * 3 * chunk]

            @pl.when(t != other)
            def _(other=other):
                k = lax.rem(other - t + tilts, tilts) - 1
                send(plane.at[other], got2.at[k], out2.at[k], in2.at[k], other, p).start()

    both(2)
    total = plane[t]
    for k in range(1, tilts):
        send(plane.at[0], got2.at[k - 1], out2.at[k - 1], in2.at[k - 1], t, partner).wait_recv()
        total = total + got2[k - 1]
    below = total[2 * chunk :]
    column[...] = total[: 2 * chunk] / jnp.concatenate([below, below], 0)
    result[e, chip, t] = column[...]
    round3 = []
    for k in range(1, tilts):
        other = lax.rem(t + k, tilts)
        round3.append(
            send(column, result.at[e, chip, t], out3.at[k - 1], in3.at[k - 1], other, p)
        )
        round3[-1].start()
    order = sorted(range(tilts), key=lambda m: min(m, tilts - m))
    round4 = []
    for m in order:
        whose = lax.rem(t - m + tilts, tilts)
        if m > 0:
            round3[m - 1].wait_recv()
        for k in range(1, chips):
            other = lax.rem(chip + k, chips)
            round4.append(
                send(
                    result.at[e, chip, whose],
                    result.at[e, chip, whose],
                    out4.at[m, k - 1],
                    in4.at[m, k - 1],
                    t,
                    2 * other + e,
                )
            )
            round4[-1].start()
    both(3)
    for side, has, landed in [(0, chip > 0, from_left), (1, chip < chips - 1, from_right)]:

        @pl.when(has)
        def _():
            for c in range(2):
                send(
                    near.at[c], landed.at[c], obj_out.at[1, c], obj_in.at[side, c], t, partner
                ).wait_recv()

    back = []
    for n, m in enumerate(order):
        whose = lax.rem(t - m + tilts, tilts)
        for k in range(1, chips):
            round4[n * (chips - 1) + k - 1].wait_recv()
        back.append(
            send(result.at[e, :, whose], result.at[e, :, whose], out5.at[m], in5.at[m], t, partner)
        )
        back[-1].start()
    for copy in back:
        copy.wait_recv()
    for copy in swap + round1 + round3 + round4 + back:
        copy.wait_send()
    for k in range(1, tilts):
        send(plane.at[0], got2.at[k - 1], out2.at[k - 1], in2.at[k - 1], t, partner).wait_send()


def exchange(tilts, devices, width, rows, grads, sums):
    vmem = pl.BlockSpec(memory_space=pltpu.VMEM)
    planes, groups = grads.shape[0], grads.shape[1] - 1
    _, chips, part, _ = sums.shape
    third = part // tilts
    pieces = 2 if tilts % 2 == 0 and part % 32 == 0 else 1
    block = (planes, groups, rows, LANES)
    dma = pltpu.SemaphoreType.DMA
    f32, bf16 = jnp.float32, jnp.bfloat16
    return pl.pallas_call(
        functools.partial(exchange_kernel, tilts, devices),
        out_shape=[
            pltpu.VMEM(block, f32),
            pltpu.VMEM(block, bf16),
            pltpu.VMEM(block, bf16),
            pltpu.VMEM((2, chips, tilts, 2 * third // 3, width), f32),
        ],
        in_specs=[vmem] * 2,
        out_specs=[vmem] * 4,
        scratch_shapes=[pltpu.VMEM(block, f32)]
        + [pltpu.VMEM(block, bf16)] * 2
        + [
            pltpu.VMEM((2,) + block[1:], bf16),
            pltpu.VMEM((chips, part, width), bf16),
            pltpu.VMEM((chips, part, width), f32),
            pltpu.VMEM((chips - 1, part, width), bf16),
            pltpu.VMEM((tilts, third, width), f32),
            pltpu.VMEM((2 * third // 3, width), f32),
            pltpu.VMEM((tilts - 1, third, width), f32),
        ]
        + [dma((3, 2)), dma((3, 2)), dma((4,)), dma((2,))]
        + [dma((pieces,))] * 2
        + [dma((pieces, chips - 1))] * 2
        + [dma((tilts - 1,))] * 4
        + [dma((tilts, chips - 1))] * 2
        + [dma((tilts,))] * 2,
        compiler_params=pltpu.CompilerParams(
            collective_id=2, has_side_effects=True, vmem_limit_bytes=20 * 1024 * 1024
        ),
    )(grads, sums)


def finish_kernel(
    devices, total, mine, left, right, result, object_any, probe_any, object_ref, probe_ref, sems
):
    p = lax.axis_index("pos")
    has_left, has_right = p >= 2, p < devices - 2
    groups, rows = mine.shape[1:3]
    pairs, chips, tilts, part, _ = result.shape
    chunk = part // 2
    copies = []

    def leave(src, dst):
        copies.append(pltpu.make_async_copy(src, dst, sems.at[len(copies)]))
        copies[-1].start()

    for k in range(2):
        for i in range(pairs):
            for c in range(chips):
                for s in range(tilts):
                    start = ((i * chips + c) * tilts + s) * chunk
                    probe_ref[k, start : start + chunk, :] = result[
                        i, c, s, k * chunk : (k + 1) * chunk, :
                    ]
        leave(probe_ref.at[k], probe_any.at[k])
    for c in range(2):
        for g in range(groups):
            object_ref[c, :, g * LANES : (g + 1) * LANES] = (
                total[c, g, pl.ds(2 * rows, rows), :]
                + mine[c, g]
                + jnp.where(has_left, left[c, g].astype(jnp.float32), 0.0)
                + jnp.where(has_right, right[c, g].astype(jnp.float32), 0.0)
            )
        leave(object_ref.at[c], object_any.at[0, c])
    for copy in copies:
        copy.wait()


def finish(devices, width, total, mine, left, right, result):
    planes, groups, rows, _ = mine.shape
    vmem = pl.BlockSpec(memory_space=pltpu.VMEM)
    hbm = pl.BlockSpec(memory_space=pltpu.HBM)
    f32 = jnp.float32
    shapes = [(planes, rows, groups * LANES), (2, width, width)]
    return pl.pallas_call(
        functools.partial(finish_kernel, devices),
        out_shape=[
            jax.ShapeDtypeStruct((1,) + shapes[0], f32),
            jax.ShapeDtypeStruct(shapes[1], f32),
        ],
        in_specs=[vmem] * 5,
        out_specs=[hbm] * 2,
        scratch_shapes=[pltpu.VMEM(shape, f32) for shape in shapes]
        + [pltpu.SemaphoreType.DMA((4,))],
        compiler_params=pltpu.CompilerParams(vmem_limit_bytes=16 * 1024 * 1024),
    )(total, mine, left, right, result)


def local(tilts, devices, intensity, positions, counts, object_field, probe):
    width = probe.shape[-1]
    rows = object_field.shape[2]
    reach = width // rows
    assert reach == 2 and devices % 2 == 0
    forward, inverse = dft_tables(width)
    row_order, column_order = orders(width)
    identity = np.eye(width, dtype=np.float32)
    moves = jnp.asarray(
        np.stack([identity[row_order], identity[column_order].T]).astype(ml_dtypes.bfloat16)
    )
    band, frames, probe_v, forward, inverse, places = gather(
        devices, object_field, intensity, probe, forward, inverse, positions[0].T, moves
    )
    parts = (2, devices // 2, 3 * width // devices, width)
    grads, sums = frame_sums(
        reach, tilts, parts, places, counts, frames, band, probe_v, forward, inverse
    )
    parts = exchange(tilts, devices, width, rows, grads, sums)
    return tuple(finish(devices, width, grads, *parts))


def solution(mesh):
    placed = (
        P("tilt", "pos", None, None),
        P("tilt", "pos", None),
        P("tilt", "pos"),
        P("tilt", None, "pos", None),
        P(),
    )
    return jax.shard_map(
        functools.partial(local, mesh.shape["tilt"], mesh.shape["pos"]),
        mesh=mesh,
        in_specs=placed,
        out_specs=(P("tilt", None, "pos", None), P()),
        check_vma=False,
    )
```

```python
import functools
import math

import jax
import jax.numpy as jnp
import ml_dtypes
import numpy as np
from jax import lax
from jax.experimental import pallas as pl
from jax.experimental.pallas import tpu as pltpu
from jax.sharding import PartitionSpec as P

LANES = 128
GROUP = 4
EXTRACT = 256
SPREAD = 64


def orders(length):
    quarter, halfway = length // 4, length // 2
    low = np.concatenate([2 * np.arange(quarter), 2 * np.arange(quarter) + 1])
    mirror = (length - low) % length
    mirror[0] = halfway
    split = np.concatenate([low, mirror])
    plain = np.arange(halfway)
    mirror = (length - plain) % length
    mirror[0] = halfway
    return split, np.concatenate([plain, mirror])


def dft_tables(length):
    index = np.arange(length, dtype=np.int64)
    phase = (index[:, None] * index[None, :] % length).astype(np.float64) * (
        2.0 * np.pi / length
    )
    cosine = np.cos(phase) / np.sqrt(length)
    sine = np.sin(phase) / np.sqrt(length)
    halfway = length // 2
    rows, columns = orders(length)

    def paired(order):
        table = np.concatenate([cosine[:, order[:halfway]], sine[:, order[:halfway]]], 1)
        table[:, halfway] = cosine[:, halfway]
        return table

    forward_columns = paired(columns)
    forward_rows = paired(rows).T
    quarter = length // 4
    even = np.concatenate([rows[:quarter], rows[halfway : halfway + quarter]])
    odd = np.concatenate([rows[quarter:halfway], rows[halfway + quarter :]])

    def side(ks):
        c, s = cosine[:halfway, ks], sine[:halfway, ks]
        return np.block([[c, -s], [s, c]])

    inverse_rows = np.concatenate([side(even), side(odd)], 0)
    c, s = cosine[columns], sine[columns]
    inverse_columns = np.block([[c, s], [-s, c]])
    stack = np.concatenate([forward_columns, forward_rows, inverse_rows], 0)

    def cast(table):
        return jnp.asarray(table.astype(np.float32)).astype(jnp.bfloat16)

    return cast(stack), cast(inverse_columns)


def frames_kernel(
    reach,
    tilts,
    pos_any,
    count_ref,
    frames_ref,
    band,
    probe_ref,
    fwd_ref,
    inv_ref,
    clear_total,
    clear_sums,
    total,
    chunks_ref,
    sums_ref,
    patch_ref,
    pos_ref,
    pos_sem,
):
    fetch = pltpu.make_async_copy(pos_any, pos_ref, pos_sem)
    fetch.start()
    rows = band.shape[2] // (2 * reach + 1)
    width = probe_ref.shape[-1]
    wide = width // LANES

    first = (lax.axis_index("pos") - reach) * rows
    fetch.wait()

    lane = lax.broadcasted_iota(jnp.int32, (EXTRACT, LANES), 1)
    wide_lane = lax.broadcasted_iota(jnp.int32, (SPREAD, LANES), 1)
    edge = lane == 0
    top = lax.broadcasted_iota(jnp.int32, (8, width), 0) == 0
    mid = width // 2

    def dot(a, b):
        return jnp.dot(a, b, preferred_element_type=jnp.float32)

    def some_frames(at):
        spots = []
        for i in at:
            q = pos_ref[1, i]
            spots.append((pos_ref[0, i] - first, q // LANES, lax.rem(q, LANES)))
        pieces = [[] for _ in at]
        for start in range(0, width, EXTRACT):
            pr, pi = probe_ref[0, start : start + EXTRACT], probe_ref[1, start : start + EXTRACT]
            exits = []
            for n, (r, qb, qs) in enumerate(spots):
                near = lane < LANES - qs
                back_shift = lax.rem(LANES - qs, LANES)
                patch = []
                for c in range(2):
                    rolled = [
                        pltpu.roll(band[c, qb + j, pl.ds(r + start, EXTRACT), :], back_shift, 1)
                        for j in range(wide + 1)
                    ]
                    patch.append(
                        jnp.concatenate(
                            [jnp.where(near, rolled[j], rolled[j + 1]) for j in range(wide)], 1
                        )
                    )
                    patch_ref[n, c, start : start + EXTRACT] = patch[c]
                xr, xi = patch
                exits.append((pr * xr - pi * xi).astype(jnp.bfloat16))
                exits.append((pr * xi + pi * xr).astype(jnp.bfloat16))
            out = dot(jnp.concatenate(exits, 0), fwd_ref[0:width])
            for n in range(len(at)):
                re = out[2 * n * EXTRACT : (2 * n + 1) * EXTRACT]
                im = out[(2 * n + 1) * EXTRACT : (2 * n + 2) * EXTRACT]
                u, v, uu, vv = re[:, :LANES], re[:, LANES:], im[:, :LANES], im[:, LANES:]
                pieces[n].append(
                    jnp.concatenate(
                        [
                            u + jnp.where(edge, 0.0, vv),
                            jnp.where(edge, v, u - vv),
                            uu - jnp.where(edge, 0.0, v),
                            jnp.where(edge, vv, uu + v),
                        ],
                        1,
                    ).astype(jnp.bfloat16)
                )
        backs = []
        for n, i in enumerate(at):
            far = dot(fwd_ref[width : 2 * width], jnp.concatenate(pieces[n], 0))
            u, v = far[:mid, :width], far[mid:, :width]
            uu, vv = far[:mid, width:], far[mid:, width:]
            fr = jnp.concatenate(
                [
                    u[:8] + jnp.where(top, 0.0, vv[:8]),
                    u[8:] + vv[8:],
                    jnp.where(top, v[:8], u[:8] - vv[:8]),
                    u[8:] - vv[8:],
                ],
                0,
            )
            fi = jnp.concatenate(
                [
                    uu[:8] - jnp.where(top, 0.0, v[:8]),
                    uu[8:] - v[8:],
                    jnp.where(top, vv[:8], uu[:8] + v[:8]),
                    uu[8:] + v[8:],
                ],
                0,
            )
            misfit = fr * fr + fi * fi - frames_ref[i].astype(jnp.float32)
            br = (fr * misfit).astype(jnp.bfloat16)
            bi = (fi * misfit).astype(jnp.bfloat16)
            q = mid // 2
            backs.append(
                (
                    jnp.concatenate([br[:q], br[mid : mid + q], bi[:q], bi[mid : mid + q]], 0),
                    jnp.concatenate([br[q:mid], br[mid + q :], bi[q:mid], bi[mid + q :]], 0),
                )
            )
        mids = []
        for n, i in enumerate(at):
            ev = dot(fwd_ref[2 * width : 3 * width], backs[n][0])
            od = dot(fwd_ref[3 * width :], backs[n][1])
            add, sub = (ev + od).astype(jnp.bfloat16), (ev - od).astype(jnp.bfloat16)
            mids.append(
                jnp.concatenate(
                    [
                        jnp.concatenate([add[:mid], sub[:mid]], 0),
                        jnp.concatenate([add[mid:], sub[mid:]], 0),
                    ],
                    1,
                )
            )
        for start in range(0, width, SPREAD):
            waves = dot(
                jnp.concatenate([m[start : start + SPREAD] for m in mids], 0), inv_ref[...]
            )
            pr, pi = probe_ref[0, start : start + SPREAD], probe_ref[1, start : start + SPREAD]
            sums = [0.0, 0.0, 0.0]
            for n, (r, qb, qs) in enumerate(spots):
                xr = patch_ref[n, 0, start : start + SPREAD]
                xi = patch_ref[n, 1, start : start + SPREAD]
                wave = waves[n * SPREAD : (n + 1) * SPREAD]
                wr, wi = wave[:, :width], wave[:, width:]
                sums[0] += xr * wr + xi * wi
                sums[1] += xr * wi - xi * wr
                sums[2] += xr * xr + xi * xi
                far_side = wide_lane >= qs
                for c in range(2):
                    grad = pr * wr + pi * wi if c == 0 else pr * wi - pi * wr
                    grad = grad.astype(jnp.bfloat16).astype(jnp.float32)
                    rolled = [
                        pltpu.roll(grad[:, j * LANES : (j + 1) * LANES], qs, 1)
                        for j in range(wide)
                    ]
                    zero = jnp.zeros_like(rolled[0])
                    for j in range(wide + 1):
                        here = rolled[j] if j < wide else zero
                        before = rolled[j - 1] if j > 0 else zero
                        total[c, qb + j, pl.ds(r + start, SPREAD), :] += jnp.where(
                            far_side, here, before
                        )
            for k in range(3):
                sums_ref[k, start : start + SPREAD] += sums[k]

    count = count_ref[0, 0]
    group = GROUP

    @pl.loop(0, count // group)
    def _(i):
        some_frames([group * i + n for n in range(group)])

    done = count // group * group
    for size in (2, 1):
        left = (count - done) // size

        @pl.when(left > 0)
        def _(done=done, size=size):
            some_frames([done + n for n in range(size)])

        done = done + left * size

    pairs, chips, _, _ = chunks_ref.shape
    chunk = chunks_ref.shape[2] // (3 * tilts)
    for e in range(pairs):
        for c in range(chips):
            for t in range(tilts):
                start = ((e * chips + c) * tilts + t) * chunk
                for k in range(3):
                    chunks_ref[e, c, pl.ds((t * 3 + k) * chunk, chunk), :] = sums_ref[
                        k, start : start + chunk, :
                    ]


def frame_sums(
    reach, tilts, parts, positions, count, frames, band, probe, forward, inverse, total, sums
):
    vmem = pl.BlockSpec(memory_space=pltpu.VMEM)
    smem = pl.BlockSpec(memory_space=pltpu.SMEM)
    return pl.pallas_call(
        functools.partial(frames_kernel, reach, tilts),
        out_shape=[
            jax.ShapeDtypeStruct(band.shape, jnp.float32),
            jax.ShapeDtypeStruct(parts, jnp.float32),
            jax.ShapeDtypeStruct(sums.shape, jnp.float32),
        ],
        in_specs=[vmem, smem] + [vmem] * 7,
        out_specs=[vmem] * 3,
        input_output_aliases={7: 0, 8: 2},
        scratch_shapes=[
            pltpu.VMEM((GROUP, 2) + probe.shape[1:], jnp.float32),
            pltpu.SMEM(positions.shape, jnp.int32),
            pltpu.SemaphoreType.DMA,
        ],
        compiler_params=pltpu.CompilerParams(vmem_limit_bytes=24 * 1024 * 1024),
    )(positions, count, frames, band, probe, forward, inverse, total, sums)[:2]


def greet(tilts, devices):
    t, p = lax.axis_index("tilt"), lax.axis_index("pos")
    barrier = pltpu.get_barrier_semaphore()
    for k in range(1, devices):
        pl.semaphore_signal(
            barrier,
            inc=1,
            device_id=(t, lax.rem(p + k, devices)),
            device_id_type=pl.DeviceIdType.MESH,
        )
    for k in range(1, tilts):
        pl.semaphore_signal(
            barrier,
            inc=1,
            device_id=(lax.rem(t + k, tilts), p),
            device_id_type=pl.DeviceIdType.MESH,
        )
    pl.semaphore_wait(barrier, devices - 1 + tilts - 1)


def send(src, dst, sem_out, sem_in, tilt, pos):
    return pltpu.make_async_remote_copy(
        src_ref=src,
        dst_ref=dst,
        send_sem=sem_out,
        recv_sem=sem_in,
        device_id=(tilt, pos),
        device_id_type=pl.DeviceIdType.MESH,
    )


def relayed(devices):
    return devices == 8


def gather_kernel(
    devices,
    field_any,
    frames_any,
    probe_any,
    fwd_any,
    inv_any,
    pos_any,
    moves_any,
    band,
    frames_ref,
    probe_ref,
    fwd_ref,
    inv_ref,
    pos_ref,
    total,
    sums_ref,
    own,
    slots,
    stage,
    raw_ref,
    moves_ref,
    out_sem,
    in_sem,
    relay_out,
    relay_in,
    local_sem,
):
    t, p = lax.axis_index("tilt"), lax.axis_index("pos")
    chip, chips = p // 2, devices // 2
    rows = own.shape[1]
    groups = own.shape[2] // LANES

    own_copy = pltpu.make_async_copy(field_any.at[0], own, local_sem.at[0])
    own_copy.start()
    loads = [
        pltpu.make_async_copy(src, dst, local_sem.at[1 + n])
        for n, (src, dst) in enumerate(
            [
                (pos_any, pos_ref),
                (probe_any, probe_ref),
                (fwd_any, fwd_ref),
                (inv_any, inv_ref),
                (moves_any, moves_ref),
                (frames_any.at[0], raw_ref),
            ]
        )
    ]
    greet(1, devices)
    own_copy.wait()

    def place(src, b):
        for c in range(2):
            for g in range(groups):
                band[c, g, pl.ds(b * rows, rows), :] = src[
                    c, :, g * LANES : (g + 1) * LANES
                ].astype(jnp.float32)

    def reorder():
        slots_of, width = raw_ref.shape[0], raw_ref.shape[1]
        some = math.gcd(slots_of, 4)

        @pl.loop(0, slots_of // some)
        def _(i):
            moved = jnp.dot(
                jnp.concatenate([raw_ref[i * some + n] for n in range(some)], 0),
                moves_ref[1],
                preferred_element_type=jnp.float32,
            ).astype(jnp.bfloat16)
            for n in range(some):
                frames_ref[i * some + n] = jnp.dot(
                    moves_ref[0],
                    moved[n * width : (n + 1) * width],
                    preferred_element_type=jnp.float32,
                ).astype(frames_ref.dtype)

    def role(odd):
        partner = p - 1 if odd else p + 1
        has_left, has_right = chip > 0, chip < chips - 1
        near, far = (3, 4) if odd else (1, 0)
        onward = 4 if odd else 0
        from_partner = 1 if odd else 3
        opposite = 0 if odd else 4
        outer, inner = (has_right, has_left) if odd else (has_left, has_right)
        slot_left, slot_right = (4, 1) if odd else (3, 0)
        pos_left, pos_right = 2 * chip - 1, 2 * chip + 2

        def copy(src, slot, c, out, pos):
            return send(
                src.at[c], slots.at[slot, c], out_sem.at[out, c], in_sem.at[slot, c], t, pos
            )

        to_left = [copy(own, slot_left, c, 1, pos_left) for c in range(2)]
        to_right = [copy(own, slot_right, c, 2, pos_right) for c in range(2)]
        to_partner = [copy(own, 3 if odd else 1, c, 0, partner) for c in range(2)]
        forward = [copy(slots.at[near], onward, c, 3, partner) for c in range(2)]

        def arrived(slot, c):
            copy(own, slot, c, 0, partner).wait_recv()

        to_near, to_far = (to_right, to_left) if odd else (to_left, to_right)
        has_near, has_far = (has_right, has_left) if odd else (has_left, has_right)
        if relayed(devices):
            across = lax.rem(p + 4, 8)
            source, relay = (chip == 2, chip == 0) if odd else (chip == 1, chip == 3)
            slot_far, pos_far = (slot_left, 3) if odd else (slot_right, 4)
            direct = has_far & ~source
            to_stage = [
                send(own.at[c], stage.at[c], relay_out.at[0, c], relay_in.at[c], t, across)
                for c in range(2)
            ]
            staged = [
                send(
                    stage.at[c],
                    slots.at[slot_far, c],
                    relay_out.at[1, c],
                    in_sem.at[slot_far, c],
                    t,
                    pos_far,
                )
                for c in range(2)
            ]
        else:
            direct = has_far
        for c in range(2):
            if relayed(devices):
                pl.when(source)(to_stage[c].start)
            pl.when(has_near)(to_near[c].start)
        for c in range(2):
            pl.when(direct)(to_far[c].start)
        for c in range(2):
            to_partner[c].start()
        for load in loads:
            load.start()
        for c in range(2):
            band[c, groups] = jnp.zeros(band.shape[2:], jnp.float32)
        place(own, 2)
        total[...] = jnp.zeros_like(total)
        sums_ref[...] = jnp.zeros_like(sums_ref)
        for c in range(2):
            arrived(from_partner, c)
        place(slots.at[from_partner], from_partner)
        for load in loads:
            load.wait()
        reorder()
        if relayed(devices):

            @pl.when(relay)
            def _():
                for c in range(2):
                    to_stage[c].wait_recv()
                    staged[c].start()

        @pl.when(outer)
        def _():
            for c in range(2):
                arrived(near, c)
                forward[c].start()
            place(slots.at[near], near)
            for c in range(2):
                arrived(far, c)
            place(slots.at[far], far)

        @pl.when(inner)
        def _():
            for c in range(2):
                arrived(opposite, c)
            place(slots.at[opposite], opposite)

        for c in range(2):
            pl.when(has_near)(to_near[c].wait_send)
            pl.when(direct)(to_far[c].wait_send)
            if relayed(devices):
                pl.when(source)(to_stage[c].wait_send)
                pl.when(relay)(staged[c].wait_send)
        for c in range(2):
            to_partner[c].wait_send()
            pl.when(outer)(forward[c].wait_send)

    pl.when(lax.rem(p, 2) == 0)(lambda: role(False))
    pl.when(lax.rem(p, 2) == 1)(lambda: role(True))


def gather(devices, field, frames, probe, forward, inverse, positions, moves):
    hbm = pl.BlockSpec(memory_space=pltpu.HBM)
    vmem = pl.BlockSpec(memory_space=pltpu.VMEM)
    _, planes, rows, columns = field.shape
    block = (planes, rows, columns)
    groups = columns // LANES
    dma = pltpu.SemaphoreType.DMA
    held = 8 * planes * (groups + 1) * 5 * rows * LANES + 6 * probe.size + sum(
        a.size * a.dtype.itemsize for a in (frames, probe, forward, inverse)
    )
    return pl.pallas_call(
        functools.partial(gather_kernel, devices),
        out_shape=[
            pltpu.VMEM((planes, groups + 1, 5 * rows, LANES), jnp.float32),
            pltpu.VMEM(frames.shape[1:], frames.dtype),
            pltpu.VMEM(probe.shape, probe.dtype),
            pltpu.VMEM(forward.shape, forward.dtype),
            pltpu.VMEM(inverse.shape, inverse.dtype),
            pltpu.VMEM(positions.shape, positions.dtype),
            pltpu.VMEM((planes, groups + 1, 5 * rows, LANES), jnp.float32),
            pltpu.VMEM((3,) + probe.shape[1:], jnp.float32),
        ],
        in_specs=[hbm] * 7,
        out_specs=[vmem] * 8,
        scratch_shapes=[
            pltpu.VMEM(block, field.dtype),
            pltpu.VMEM((5,) + block, field.dtype),
            pltpu.VMEM(block, field.dtype),
            pltpu.VMEM(frames.shape[1:], frames.dtype),
            pltpu.VMEM(moves.shape, moves.dtype),
            dma((4, 2)),
            dma((5, 2)),
            dma((2, 2)),
            dma((2,)),
            dma((7,)),
        ],
        compiler_params=pltpu.CompilerParams(
            collective_id=1, has_side_effects=True, vmem_limit_bytes=62 * 1024 * 1024 - held
        ),
    )(field, frames, probe, forward, inverse, positions, moves)


def exchange_kernel(tilts, devices, *refs):
    grads, sums, mine, from_left, from_right, result = refs[:6]
    extra, near, distant, stage = refs[6:10]
    half, got0, got1, plane, column, got2 = refs[10:16]
    obj_out, obj_in, stage_out, stage_in = refs[16:20]
    out0, in0, out1, in1, out2, in2, out3, in3, out4, in4, out5, in5 = refs[20:]
    t, p = lax.axis_index("tilt"), lax.axis_index("pos")
    chip, chips = p // 2, devices // 2
    e = lax.rem(p, 2)
    partner = p + 1 - 2 * e
    groups, rows = mine.shape[1:3]
    chunk = column.shape[0] // 2
    relay = relayed(devices)
    greet(tilts, devices)

    def block(b):
        return grads.at[:, pl.ds(0, groups), pl.ds(b * rows, rows), :]

    chips_rows = half.shape[1]
    pieces = out0.shape[0]
    piece = chips_rows // pieces
    per = tilts // pieces

    def cut(n):
        return pl.ds(n * piece, piece)

    swap = [
        send(
            sums.at[1 - e, :, cut(n), :], got0.at[:, cut(n), :], out0.at[n], in0.at[n], t, partner
        )
        for n in range(pieces)
    ]

    def objects(odd, step):
        has = chip < chips - 1 if odd else chip > 0
        way = 1 if odd else -1
        middle = (chip == 1) if odd else (chip == 2)
        corner = (chip == 3) if odd else (chip == 0)
        lands = from_left if odd else from_right
        side = 0 if odd else 1
        across = lax.rem(p + 4, 8)

        def out(src, n, c, pos):
            return send(src.at[c], lands.at[c], obj_out.at[n, c], obj_in.at[side, c], t, pos)

        far = [out(distant, 0, c, p + 2 * way) for c in range(2)]
        close = [out(near, 1, c, p + way) for c in range(2)]
        to_extra = send(
            block(0 if odd else 4), extra, obj_out.at[2, 0], obj_in.at[2, 0], t, partner
        )
        to_mine = send(block(1 if odd else 3), mine, obj_out.at[2, 1], obj_in.at[2, 1], t, partner)
        if relay:
            up = [
                send(src.at[1], stage.at[n], stage_out.at[n], stage_in.at[n], t, across)
                for n, src in enumerate([distant, near])
            ]
            onto = [(5, 4), (2, 3)][side]
            on = [
                send(stage.at[n], lands.at[1], stage_out.at[2 + n], obj_in.at[side, 1], t, onto[n])
                for n in range(2)
            ]
        if step == 0:
            to_extra.start()
            b = 4 if odd else 0
            for c in range(2):
                distant[c] = grads[c, 0:groups, pl.ds(b * rows, rows), :].astype(distant.dtype)
            if relay:
                pl.when(middle)(up[0].start)
        elif step == 1:
            if relay:
                pl.when(has)(far[0].start)
                pl.when(has & ~middle)(far[1].start)
            else:
                pl.when(has)(far[0].start)
                pl.when(has)(far[1].start)
            to_mine.start()
            to_extra.wait_recv()
            b = 3 if odd else 1
            for c in range(2):
                near[c] = (
                    grads[c, 0:groups, pl.ds(b * rows, rows), :] + extra[c]
                ).astype(near.dtype)
            pl.when(has)(close[0].start)
            if relay:
                pl.when(middle)(up[1].start)
                pl.when(has & ~middle)(close[1].start)

                @pl.when(corner)
                def _():
                    up[0].wait_recv()
                    on[0].start()
            else:
                pl.when(has)(close[1].start)
        elif step == 2:
            if relay:

                @pl.when(corner)
                def _():
                    up[1].wait_recv()
                    on[1].start()
        else:
            to_mine.wait_recv()
            to_extra.wait_send()
            to_mine.wait_send()
            pl.when(has)(far[0].wait_send)
            pl.when(has)(close[0].wait_send)
            if relay:
                for n, direct in enumerate([far[1], close[1]]):
                    pl.when(has & ~middle)(direct.wait_send)
                    pl.when(middle)(up[n].wait_send)
                    pl.when(corner)(on[n].wait_send)
            else:
                pl.when(has)(far[1].wait_send)
                pl.when(has)(close[1].wait_send)

    def both(step):
        pl.when(e == 0)(lambda: objects(False, step))
        pl.when(e == 1)(lambda: objects(True, step))

    for copy in swap:
        copy.start()
    both(0)
    round1 = []
    for n in range(pieces):
        swap[n].wait_recv()
        half[:, cut(n), :] = (sums[e, :, cut(n), :] + got0[:, cut(n), :]).astype(half.dtype)
        for k in range(1, chips):
            other = lax.rem(chip + k, chips)
            round1.append(
                send(
                    half.at[other, cut(n)],
                    got1.at[k - 1, cut(n)],
                    out1.at[n, k - 1],
                    in1.at[n, k - 1],
                    t,
                    2 * other + e,
                )
            )
            round1[-1].start()
    both(1)
    for n in range(pieces):
        total = sums[e, chip, cut(n)] + got0[chip, cut(n)]
        for k in range(1, chips):
            round1[n * (chips - 1) + k - 1].wait_recv()
            total = total + got1[k - 1, cut(n)].astype(jnp.float32)
        for s in range(per):
            other = n * per + s
            plane[other] = total[s * 3 * chunk : (s + 1) * 3 * chunk]

            @pl.when(t != other)
            def _(other=other):
                k = lax.rem(other - t + tilts, tilts) - 1
                send(plane.at[other], got2.at[k], out2.at[k], in2.at[k], other, p).start()

    both(2)
    total = plane[t]
    for k in range(1, tilts):
        send(plane.at[0], got2.at[k - 1], out2.at[k - 1], in2.at[k - 1], t, partner).wait_recv()
        total = total + got2[k - 1]
    below = total[2 * chunk :]
    column[...] = total[: 2 * chunk] / jnp.concatenate([below, below], 0)
    result[e, chip, t] = column[...]
    round3 = []
    for k in range(1, tilts):
        other = lax.rem(t + k, tilts)
        round3.append(
            send(column, result.at[e, chip, t], out3.at[k - 1], in3.at[k - 1], other, p)
        )
        round3[-1].start()
    order = sorted(range(tilts), key=lambda m: min(m, tilts - m))
    round4 = []
    for m in order:
        whose = lax.rem(t - m + tilts, tilts)
        if m > 0:
            round3[m - 1].wait_recv()
        for k in range(1, chips):
            other = lax.rem(chip + k, chips)
            round4.append(
                send(
                    result.at[e, chip, whose],
                    result.at[e, chip, whose],
                    out4.at[m, k - 1],
                    in4.at[m, k - 1],
                    t,
                    2 * other + e,
                )
            )
            round4[-1].start()
    both(3)
    for side, has, landed in [(0, chip > 0, from_left), (1, chip < chips - 1, from_right)]:

        @pl.when(has)
        def _():
            for c in range(2):
                send(
                    near.at[c], landed.at[c], obj_out.at[1, c], obj_in.at[side, c], t, partner
                ).wait_recv()

    back = []
    for n, m in enumerate(order):
        whose = lax.rem(t - m + tilts, tilts)
        for k in range(1, chips):
            round4[n * (chips - 1) + k - 1].wait_recv()
        back.append(
            send(result.at[e, :, whose], result.at[e, :, whose], out5.at[m], in5.at[m], t, partner)
        )
        back[-1].start()
    for copy in back:
        copy.wait_recv()
    for copy in swap + round1 + round3 + round4 + back:
        copy.wait_send()
    for k in range(1, tilts):
        send(plane.at[0], got2.at[k - 1], out2.at[k - 1], in2.at[k - 1], t, partner).wait_send()


def exchange(tilts, devices, width, rows, grads, sums):
    vmem = pl.BlockSpec(memory_space=pltpu.VMEM)
    planes, groups = grads.shape[0], grads.shape[1] - 1
    _, chips, part, _ = sums.shape
    third = part // tilts
    pieces = 2 if tilts % 2 == 0 and part % 32 == 0 else 1
    block = (planes, groups, rows, LANES)
    dma = pltpu.SemaphoreType.DMA
    f32, bf16 = jnp.float32, jnp.bfloat16
    return pl.pallas_call(
        functools.partial(exchange_kernel, tilts, devices),
        out_shape=[
            pltpu.VMEM(block, f32),
            pltpu.VMEM(block, bf16),
            pltpu.VMEM(block, bf16),
            pltpu.VMEM((2, chips, tilts, 2 * third // 3, width), f32),
        ],
        in_specs=[vmem] * 2,
        out_specs=[vmem] * 4,
        scratch_shapes=[pltpu.VMEM(block, f32)]
        + [pltpu.VMEM(block, bf16)] * 2
        + [
            pltpu.VMEM((2,) + block[1:], bf16),
            pltpu.VMEM((chips, part, width), bf16),
            pltpu.VMEM((chips, part, width), f32),
            pltpu.VMEM((chips - 1, part, width), bf16),
            pltpu.VMEM((tilts, third, width), f32),
            pltpu.VMEM((2 * third // 3, width), f32),
            pltpu.VMEM((tilts - 1, third, width), f32),
        ]
        + [dma((3, 2)), dma((3, 2)), dma((4,)), dma((2,))]
        + [dma((pieces,))] * 2
        + [dma((pieces, chips - 1))] * 2
        + [dma((tilts - 1,))] * 4
        + [dma((tilts, chips - 1))] * 2
        + [dma((tilts,))] * 2,
        compiler_params=pltpu.CompilerParams(
            collective_id=2, has_side_effects=True, vmem_limit_bytes=20 * 1024 * 1024
        ),
    )(grads, sums)


def finish_kernel(
    devices, total, mine, left, right, result, object_any, probe_any, object_ref, probe_ref, sems
):
    p = lax.axis_index("pos")
    has_left, has_right = p >= 2, p < devices - 2
    groups, rows = mine.shape[1:3]
    pairs, chips, tilts, part, _ = result.shape
    chunk = part // 2
    copies = []

    def leave(src, dst):
        copies.append(pltpu.make_async_copy(src, dst, sems.at[len(copies)]))
        copies[-1].start()

    for k in range(2):
        for i in range(pairs):
            for c in range(chips):
                for s in range(tilts):
                    start = ((i * chips + c) * tilts + s) * chunk
                    probe_ref[k, start : start + chunk, :] = result[
                        i, c, s, k * chunk : (k + 1) * chunk, :
                    ]
        leave(probe_ref.at[k], probe_any.at[k])
    for c in range(2):
        for g in range(groups):
            object_ref[c, :, g * LANES : (g + 1) * LANES] = (
                total[c, g, pl.ds(2 * rows, rows), :]
                + mine[c, g]
                + jnp.where(has_left, left[c, g].astype(jnp.float32), 0.0)
                + jnp.where(has_right, right[c, g].astype(jnp.float32), 0.0)
            )
        leave(object_ref.at[c], object_any.at[0, c])
    for copy in copies:
        copy.wait()


def finish(devices, width, total, mine, left, right, result):
    planes, groups, rows, _ = mine.shape
    vmem = pl.BlockSpec(memory_space=pltpu.VMEM)
    hbm = pl.BlockSpec(memory_space=pltpu.HBM)
    f32 = jnp.float32
    shapes = [(planes, rows, groups * LANES), (2, width, width)]
    return pl.pallas_call(
        functools.partial(finish_kernel, devices),
        out_shape=[
            jax.ShapeDtypeStruct((1,) + shapes[0], f32),
            jax.ShapeDtypeStruct(shapes[1], f32),
        ],
        in_specs=[vmem] * 5,
        out_specs=[hbm] * 2,
        scratch_shapes=[pltpu.VMEM(shape, f32) for shape in shapes]
        + [pltpu.SemaphoreType.DMA((4,))],
        compiler_params=pltpu.CompilerParams(vmem_limit_bytes=16 * 1024 * 1024),
    )(total, mine, left, right, result)


def local(tilts, devices, intensity, positions, counts, object_field, probe):
    width = probe.shape[-1]
    rows = object_field.shape[2]
    reach = width // rows
    assert reach == 2 and devices % 2 == 0
    forward, inverse = dft_tables(width)
    row_order, column_order = orders(width)
    identity = np.eye(width, dtype=np.float32)
    moves = jnp.asarray(
        np.stack([identity[row_order], identity[column_order].T]).astype(ml_dtypes.bfloat16)
    )
    band, frames, probe_v, forward, inverse, places, total, sums = gather(
        devices, object_field, intensity, probe, forward, inverse, positions[0].T, moves
    )
    parts = (2, devices // 2, 3 * width // devices, width)
    grads, sums = frame_sums(
        reach,
        tilts,
        parts,
        places,
        counts,
        frames,
        band,
        probe_v,
        forward,
        inverse,
        total,
        sums,
    )
    parts = exchange(tilts, devices, width, rows, grads, sums)
    return tuple(finish(devices, width, grads, *parts))


def solution(mesh):
    placed = (
        P("tilt", "pos", None, None),
        P("tilt", "pos", None),
        P("tilt", "pos"),
        P("tilt", None, "pos", None),
        P(),
    )
    return jax.shard_map(
        functools.partial(local, mesh.shape["tilt"], mesh.shape["pos"]),
        mesh=mesh,
        in_specs=placed,
        out_specs=(P("tilt", None, "pos", None), P()),
        check_vma=False,
    )
```

```python
import functools
import math

import jax
import jax.numpy as jnp
import ml_dtypes
import numpy as np
from jax import lax
from jax.experimental import pallas as pl
from jax.experimental.pallas import tpu as pltpu
from jax.sharding import PartitionSpec as P

LANES = 128
GROUP = 4
EXTRACT = 256
SPREAD = 64


def orders(length):
    quarter, halfway = length // 4, length // 2
    low = np.concatenate([2 * np.arange(quarter), 2 * np.arange(quarter) + 1])
    mirror = (length - low) % length
    mirror[0] = halfway
    split = np.concatenate([low, mirror])
    plain = np.arange(halfway)
    mirror = (length - plain) % length
    mirror[0] = halfway
    return split, np.concatenate([plain, mirror])


def dft_tables(length):
    index = np.arange(length, dtype=np.int64)
    phase = (index[:, None] * index[None, :] % length).astype(np.float64) * (
        2.0 * np.pi / length
    )
    cosine = np.cos(phase) / np.sqrt(length)
    sine = np.sin(phase) / np.sqrt(length)
    halfway = length // 2
    rows, columns = orders(length)

    def paired(order):
        table = np.concatenate([cosine[:, order[:halfway]], sine[:, order[:halfway]]], 1)
        table[:, halfway] = cosine[:, halfway]
        return table

    forward_columns = paired(columns)
    forward_rows = paired(rows).T
    quarter = length // 4
    even = np.concatenate([rows[:quarter], rows[halfway : halfway + quarter]])
    odd = np.concatenate([rows[quarter:halfway], rows[halfway + quarter :]])

    def side(ks):
        c, s = cosine[:halfway, ks], sine[:halfway, ks]
        return np.block([[c, -s], [s, c]])

    inverse_rows = np.concatenate([side(even), side(odd)], 0)
    c, s = cosine[columns], sine[columns]
    inverse_columns = np.block([[c, s], [-s, c]])
    stack = np.concatenate([forward_columns, forward_rows, inverse_rows], 0)

    def cast(table):
        return jnp.asarray(table.astype(np.float32)).astype(jnp.bfloat16)

    return cast(stack), cast(inverse_columns)


def frames_kernel(
    reach,
    tilts,
    pos_any,
    count_ref,
    frames_ref,
    band,
    probe_ref,
    fwd_ref,
    inv_ref,
    total,
    chunks_ref,
    sums_ref,
    patch_ref,
    pos_ref,
    pos_sem,
):
    fetch = pltpu.make_async_copy(pos_any, pos_ref, pos_sem)
    fetch.start()
    rows = band.shape[2] // (2 * reach + 1)
    width = probe_ref.shape[-1]
    wide = width // LANES

    total[...] = jnp.zeros_like(total)
    sums_ref[...] = jnp.zeros_like(sums_ref)
    first = (lax.axis_index("pos") - reach) * rows
    fetch.wait()

    lane = lax.broadcasted_iota(jnp.int32, (EXTRACT, LANES), 1)
    wide_lane = lax.broadcasted_iota(jnp.int32, (SPREAD, LANES), 1)
    edge = lane == 0
    top = lax.broadcasted_iota(jnp.int32, (8, width), 0) == 0
    mid = width // 2

    def dot(a, b):
        return jnp.dot(a, b, preferred_element_type=jnp.float32)

    def some_frames(at):
        spots = []
        for i in at:
            q = pos_ref[1, i]
            spots.append((pos_ref[0, i] - first, q // LANES, lax.rem(q, LANES)))
        pieces = [[] for _ in at]
        for start in range(0, width, EXTRACT):
            pr, pi = probe_ref[0, start : start + EXTRACT], probe_ref[1, start : start + EXTRACT]
            exits = []
            for n, (r, qb, qs) in enumerate(spots):
                near = lane < LANES - qs
                back_shift = lax.rem(LANES - qs, LANES)
                patch = []
                for c in range(2):
                    rolled = [
                        pltpu.roll(band[c, qb + j, pl.ds(r + start, EXTRACT), :], back_shift, 1)
                        for j in range(wide + 1)
                    ]
                    patch.append(
                        jnp.concatenate(
                            [jnp.where(near, rolled[j], rolled[j + 1]) for j in range(wide)], 1
                        )
                    )
                    patch_ref[n, c, start : start + EXTRACT] = patch[c]
                xr, xi = patch
                exits.append((pr * xr - pi * xi).astype(jnp.bfloat16))
                exits.append((pr * xi + pi * xr).astype(jnp.bfloat16))
            out = dot(jnp.concatenate(exits, 0), fwd_ref[0:width])
            for n in range(len(at)):
                re = out[2 * n * EXTRACT : (2 * n + 1) * EXTRACT]
                im = out[(2 * n + 1) * EXTRACT : (2 * n + 2) * EXTRACT]
                u, v, uu, vv = re[:, :LANES], re[:, LANES:], im[:, :LANES], im[:, LANES:]
                pieces[n].append(
                    jnp.concatenate(
                        [
                            u + jnp.where(edge, 0.0, vv),
                            jnp.where(edge, v, u - vv),
                            uu - jnp.where(edge, 0.0, v),
                            jnp.where(edge, vv, uu + v),
                        ],
                        1,
                    ).astype(jnp.bfloat16)
                )
        backs = []
        for n, i in enumerate(at):
            far = dot(fwd_ref[width : 2 * width], jnp.concatenate(pieces[n], 0))
            u, v = far[:mid, :width], far[mid:, :width]
            uu, vv = far[:mid, width:], far[mid:, width:]
            fr = jnp.concatenate(
                [
                    u[:8] + jnp.where(top, 0.0, vv[:8]),
                    u[8:] + vv[8:],
                    jnp.where(top, v[:8], u[:8] - vv[:8]),
                    u[8:] - vv[8:],
                ],
                0,
            )
            fi = jnp.concatenate(
                [
                    uu[:8] - jnp.where(top, 0.0, v[:8]),
                    uu[8:] - v[8:],
                    jnp.where(top, vv[:8], uu[:8] + v[:8]),
                    uu[8:] + v[8:],
                ],
                0,
            )
            misfit = fr * fr + fi * fi - frames_ref[i].astype(jnp.float32)
            br = (fr * misfit).astype(jnp.bfloat16)
            bi = (fi * misfit).astype(jnp.bfloat16)
            q = mid // 2
            backs.append(
                (
                    jnp.concatenate([br[:q], br[mid : mid + q], bi[:q], bi[mid : mid + q]], 0),
                    jnp.concatenate([br[q:mid], br[mid + q :], bi[q:mid], bi[mid + q :]], 0),
                )
            )
        mids = []
        for n, i in enumerate(at):
            ev = dot(fwd_ref[2 * width : 3 * width], backs[n][0])
            od = dot(fwd_ref[3 * width :], backs[n][1])
            add, sub = (ev + od).astype(jnp.bfloat16), (ev - od).astype(jnp.bfloat16)
            mids.append(
                jnp.concatenate(
                    [
                        jnp.concatenate([add[:mid], sub[:mid]], 0),
                        jnp.concatenate([add[mid:], sub[mid:]], 0),
                    ],
                    1,
                )
            )
        for start in range(0, width, SPREAD):
            waves = dot(
                jnp.concatenate([m[start : start + SPREAD] for m in mids], 0), inv_ref[...]
            )
            pr, pi = probe_ref[0, start : start + SPREAD], probe_ref[1, start : start + SPREAD]
            sums = [0.0, 0.0, 0.0]
            for n, (r, qb, qs) in enumerate(spots):
                xr = patch_ref[n, 0, start : start + SPREAD]
                xi = patch_ref[n, 1, start : start + SPREAD]
                wave = waves[n * SPREAD : (n + 1) * SPREAD]
                wr, wi = wave[:, :width], wave[:, width:]
                sums[0] += xr * wr + xi * wi
                sums[1] += xr * wi - xi * wr
                sums[2] += xr * xr + xi * xi
                far_side = wide_lane >= qs
                for c in range(2):
                    grad = pr * wr + pi * wi if c == 0 else pr * wi - pi * wr
                    grad = grad.astype(jnp.bfloat16).astype(jnp.float32)
                    rolled = [
                        pltpu.roll(grad[:, j * LANES : (j + 1) * LANES], qs, 1)
                        for j in range(wide)
                    ]
                    zero = jnp.zeros_like(rolled[0])
                    for j in range(wide + 1):
                        here = rolled[j] if j < wide else zero
                        before = rolled[j - 1] if j > 0 else zero
                        total[c, qb + j, pl.ds(r + start, SPREAD), :] += jnp.where(
                            far_side, here, before
                        )
            for k in range(3):
                sums_ref[k, start : start + SPREAD] += sums[k]

    count = count_ref[0, 0]
    group = GROUP

    @pl.loop(0, count // group)
    def _(i):
        some_frames([group * i + n for n in range(group)])

    done = count // group * group
    for size in (2, 1):
        left = (count - done) // size

        @pl.when(left > 0)
        def _(done=done, size=size):
            some_frames([done + n for n in range(size)])

        done = done + left * size

    pairs, chips, _, _ = chunks_ref.shape
    chunk = chunks_ref.shape[2] // (3 * tilts)
    for e in range(pairs):
        for c in range(chips):
            for t in range(tilts):
                start = ((e * chips + c) * tilts + t) * chunk
                for k in range(3):
                    chunks_ref[e, c, pl.ds((t * 3 + k) * chunk, chunk), :] = sums_ref[
                        k, start : start + chunk, :
                    ]


def frame_sums(reach, tilts, parts, positions, count, frames, band, probe, forward, inverse):
    vmem = pl.BlockSpec(memory_space=pltpu.VMEM)
    smem = pl.BlockSpec(memory_space=pltpu.SMEM)
    return pl.pallas_call(
        functools.partial(frames_kernel, reach, tilts),
        out_shape=[
            jax.ShapeDtypeStruct(band.shape, jnp.float32),
            jax.ShapeDtypeStruct(parts, jnp.float32),
        ],
        in_specs=[vmem, smem] + [vmem] * 5,
        out_specs=[vmem] * 2,
        scratch_shapes=[
            pltpu.VMEM((3,) + probe.shape[1:], jnp.float32),
            pltpu.VMEM((GROUP, 2) + probe.shape[1:], jnp.float32),
            pltpu.SMEM(positions.shape, jnp.int32),
            pltpu.SemaphoreType.DMA,
        ],
        compiler_params=pltpu.CompilerParams(vmem_limit_bytes=24 * 1024 * 1024),
    )(positions, count, frames, band, probe, forward, inverse)


def greet(tilts, devices):
    t, p = lax.axis_index("tilt"), lax.axis_index("pos")
    barrier = pltpu.get_barrier_semaphore()
    for k in range(1, devices):
        pl.semaphore_signal(
            barrier,
            inc=1,
            device_id=(t, lax.rem(p + k, devices)),
            device_id_type=pl.DeviceIdType.MESH,
        )
    for k in range(1, tilts):
        pl.semaphore_signal(
            barrier,
            inc=1,
            device_id=(lax.rem(t + k, tilts), p),
            device_id_type=pl.DeviceIdType.MESH,
        )
    pl.semaphore_wait(barrier, devices - 1 + tilts - 1)


def send(src, dst, sem_out, sem_in, tilt, pos):
    return pltpu.make_async_remote_copy(
        src_ref=src,
        dst_ref=dst,
        send_sem=sem_out,
        recv_sem=sem_in,
        device_id=(tilt, pos),
        device_id_type=pl.DeviceIdType.MESH,
    )


def relayed(devices):
    return devices == 8


def gather_kernel(
    devices,
    field_any,
    frames_any,
    probe_any,
    fwd_any,
    inv_any,
    pos_any,
    moves_any,
    band,
    frames_ref,
    probe_ref,
    fwd_ref,
    inv_ref,
    pos_ref,
    own,
    slots,
    stage,
    raw_ref,
    moves_ref,
    out_sem,
    in_sem,
    relay_out,
    relay_in,
    local_sem,
):
    t, p = lax.axis_index("tilt"), lax.axis_index("pos")
    chip, chips = p // 2, devices // 2
    rows = own.shape[1]
    groups = own.shape[2] // LANES

    own_copy = pltpu.make_async_copy(field_any.at[0], own, local_sem.at[0])
    own_copy.start()
    loads = [
        pltpu.make_async_copy(src, dst, local_sem.at[1 + n])
        for n, (src, dst) in enumerate(
            [
                (pos_any, pos_ref),
                (probe_any, probe_ref),
                (fwd_any, fwd_ref),
                (inv_any, inv_ref),
                (moves_any, moves_ref),
                (frames_any.at[0], raw_ref),
            ]
        )
    ]
    greet(1, devices)
    own_copy.wait()

    def place(src, b):
        for c in range(2):
            for g in range(groups):
                band[c, g, pl.ds(b * rows, rows), :] = src[
                    c, :, g * LANES : (g + 1) * LANES
                ].astype(jnp.float32)

    def reorder():
        slots_of, width = raw_ref.shape[0], raw_ref.shape[1]
        some = math.gcd(slots_of, 4)

        @pl.loop(0, slots_of // some)
        def _(i):
            moved = jnp.dot(
                jnp.concatenate([raw_ref[i * some + n] for n in range(some)], 0),
                moves_ref[1],
                preferred_element_type=jnp.float32,
            ).astype(jnp.bfloat16)
            for n in range(some):
                frames_ref[i * some + n] = jnp.dot(
                    moves_ref[0],
                    moved[n * width : (n + 1) * width],
                    preferred_element_type=jnp.float32,
                ).astype(frames_ref.dtype)

    def role(odd):
        partner = p - 1 if odd else p + 1
        has_left, has_right = chip > 0, chip < chips - 1
        near, far = (3, 4) if odd else (1, 0)
        onward = 4 if odd else 0
        from_partner = 1 if odd else 3
        opposite = 0 if odd else 4
        outer, inner = (has_right, has_left) if odd else (has_left, has_right)
        slot_left, slot_right = (4, 1) if odd else (3, 0)
        pos_left, pos_right = 2 * chip - 1, 2 * chip + 2

        def copy(src, slot, c, out, pos):
            return send(
                src.at[c], slots.at[slot, c], out_sem.at[out, c], in_sem.at[slot, c], t, pos
            )

        to_left = [copy(own, slot_left, c, 1, pos_left) for c in range(2)]
        to_right = [copy(own, slot_right, c, 2, pos_right) for c in range(2)]
        to_partner = [copy(own, 3 if odd else 1, c, 0, partner) for c in range(2)]
        forward = [copy(slots.at[near], onward, c, 3, partner) for c in range(2)]

        def arrived(slot, c):
            copy(own, slot, c, 0, partner).wait_recv()

        to_near, to_far = (to_right, to_left) if odd else (to_left, to_right)
        has_near, has_far = (has_right, has_left) if odd else (has_left, has_right)
        if relayed(devices):
            across = lax.rem(p + 4, 8)
            source, relay = (chip == 2, chip == 0) if odd else (chip == 1, chip == 3)
            slot_far, pos_far = (slot_left, 3) if odd else (slot_right, 4)
            direct = has_far & ~source
            to_stage = [
                send(own.at[c], stage.at[c], relay_out.at[0, c], relay_in.at[c], t, across)
                for c in range(2)
            ]
            staged = [
                send(
                    stage.at[c],
                    slots.at[slot_far, c],
                    relay_out.at[1, c],
                    in_sem.at[slot_far, c],
                    t,
                    pos_far,
                )
                for c in range(2)
            ]
        else:
            direct = has_far
        for c in range(2):
            if relayed(devices):
                pl.when(source)(to_stage[c].start)
            pl.when(has_near)(to_near[c].start)
        for c in range(2):
            pl.when(direct)(to_far[c].start)
        for c in range(2):
            to_partner[c].start()
        for load in loads:
            load.start()
        for c in range(2):
            band[c, groups] = jnp.zeros(band.shape[2:], jnp.float32)
        place(own, 2)
        for c in range(2):
            arrived(from_partner, c)
        place(slots.at[from_partner], from_partner)
        for load in loads:
            load.wait()
        reorder()
        if relayed(devices):

            @pl.when(relay)
            def _():
                for c in range(2):
                    to_stage[c].wait_recv()
                    staged[c].start()

        @pl.when(outer)
        def _():
            for c in range(2):
                arrived(near, c)
                forward[c].start()
            place(slots.at[near], near)
            for c in range(2):
                arrived(far, c)
            place(slots.at[far], far)

        @pl.when(inner)
        def _():
            for c in range(2):
                arrived(opposite, c)
            place(slots.at[opposite], opposite)

        for c in range(2):
            pl.when(has_near)(to_near[c].wait_send)
            pl.when(direct)(to_far[c].wait_send)
            if relayed(devices):
                pl.when(source)(to_stage[c].wait_send)
                pl.when(relay)(staged[c].wait_send)
        for c in range(2):
            to_partner[c].wait_send()
            pl.when(outer)(forward[c].wait_send)

    pl.when(lax.rem(p, 2) == 0)(lambda: role(False))
    pl.when(lax.rem(p, 2) == 1)(lambda: role(True))


def gather(devices, field, frames, probe, forward, inverse, positions, moves):
    hbm = pl.BlockSpec(memory_space=pltpu.HBM)
    vmem = pl.BlockSpec(memory_space=pltpu.VMEM)
    _, planes, rows, columns = field.shape
    block = (planes, rows, columns)
    groups = columns // LANES
    dma = pltpu.SemaphoreType.DMA
    held = 4 * planes * (groups + 1) * 5 * rows * LANES + sum(
        a.size * a.dtype.itemsize for a in (frames, probe, forward, inverse)
    )
    return pl.pallas_call(
        functools.partial(gather_kernel, devices),
        out_shape=[
            pltpu.VMEM((planes, groups + 1, 5 * rows, LANES), jnp.float32),
            pltpu.VMEM(frames.shape[1:], frames.dtype),
            pltpu.VMEM(probe.shape, probe.dtype),
            pltpu.VMEM(forward.shape, forward.dtype),
            pltpu.VMEM(inverse.shape, inverse.dtype),
            pltpu.VMEM(positions.shape, positions.dtype),
        ],
        in_specs=[hbm] * 7,
        out_specs=[vmem] * 6,
        scratch_shapes=[
            pltpu.VMEM(block, field.dtype),
            pltpu.VMEM((5,) + block, field.dtype),
            pltpu.VMEM(block, field.dtype),
            pltpu.VMEM(frames.shape[1:], frames.dtype),
            pltpu.VMEM(moves.shape, moves.dtype),
            dma((4, 2)),
            dma((5, 2)),
            dma((2, 2)),
            dma((2,)),
            dma((7,)),
        ],
        compiler_params=pltpu.CompilerParams(
            collective_id=1, has_side_effects=True, vmem_limit_bytes=62 * 1024 * 1024 - held
        ),
    )(field, frames, probe, forward, inverse, positions, moves)


def exchange_kernel(tilts, devices, *refs):
    grads, sums, mine, from_left, from_right, result = refs[:6]
    extra, near, distant, stage = refs[6:10]
    half, got0, got1, plane, column, got2 = refs[10:16]
    obj_out, obj_in, stage_out, stage_in = refs[16:20]
    out0, in0, out1, in1, out2, in2, out3, in3, out4, in4, out5, in5 = refs[20:]
    t, p = lax.axis_index("tilt"), lax.axis_index("pos")
    chip, chips = p // 2, devices // 2
    e = lax.rem(p, 2)
    partner = p + 1 - 2 * e
    groups, rows = mine.shape[1:3]
    chunk = column.shape[0] // 2
    relay = relayed(devices)
    greet(tilts, devices)

    def block(b):
        return grads.at[:, pl.ds(0, groups), pl.ds(b * rows, rows), :]

    chips_rows = half.shape[1]
    pieces = out0.shape[0]
    piece = chips_rows // pieces
    per = tilts // pieces

    def cut(n):
        return pl.ds(n * piece, piece)

    swap = [
        send(
            sums.at[1 - e, :, cut(n), :], got0.at[:, cut(n), :], out0.at[n], in0.at[n], t, partner
        )
        for n in range(pieces)
    ]

    def objects(odd, step):
        has = chip < chips - 1 if odd else chip > 0
        way = 1 if odd else -1
        middle = (chip == 1) if odd else (chip == 2)
        corner = (chip == 3) if odd else (chip == 0)
        lands = from_left if odd else from_right
        side = 0 if odd else 1
        across = lax.rem(p + 4, 8)

        def out(src, n, c, pos):
            return send(src.at[c], lands.at[c], obj_out.at[n, c], obj_in.at[side, c], t, pos)

        far = [out(distant, 0, c, p + 2 * way) for c in range(2)]
        close = [out(near, 1, c, p + way) for c in range(2)]
        to_extra = send(
            block(0 if odd else 4), extra, obj_out.at[2, 0], obj_in.at[2, 0], t, partner
        )
        to_mine = send(block(1 if odd else 3), mine, obj_out.at[2, 1], obj_in.at[2, 1], t, partner)
        if relay:
            up = [
                send(src.at[1], stage.at[n], stage_out.at[n], stage_in.at[n], t, across)
                for n, src in enumerate([distant, near])
            ]
            onto = [(5, 4), (2, 3)][side]
            on = [
                send(stage.at[n], lands.at[1], stage_out.at[2 + n], obj_in.at[side, 1], t, onto[n])
                for n in range(2)
            ]
        if step == 0:
            to_extra.start()
            b = 4 if odd else 0
            for c in range(2):
                distant[c] = grads[c, 0:groups, pl.ds(b * rows, rows), :].astype(distant.dtype)
            if relay:
                pl.when(middle)(up[0].start)
        elif step == 1:
            if relay:
                pl.when(has)(far[0].start)
                pl.when(has & ~middle)(far[1].start)
            else:
                pl.when(has)(far[0].start)
                pl.when(has)(far[1].start)
            to_mine.start()
            to_extra.wait_recv()
            b = 3 if odd else 1
            for c in range(2):
                near[c] = (
                    grads[c, 0:groups, pl.ds(b * rows, rows), :] + extra[c]
                ).astype(near.dtype)
            pl.when(has)(close[0].start)
            if relay:
                pl.when(middle)(up[1].start)

                @pl.when(corner)
                def _():
                    up[0].wait_recv()
                    on[0].start()
        elif step == 2:
            if relay:
                pl.when(has & ~middle)(close[1].start)

                @pl.when(corner)
                def _():
                    up[1].wait_recv()
                    on[1].start()
            else:
                pl.when(has)(close[1].start)
        else:
            to_mine.wait_recv()
            to_extra.wait_send()
            to_mine.wait_send()
            pl.when(has)(far[0].wait_send)
            pl.when(has)(close[0].wait_send)
            if relay:
                for n, direct in enumerate([far[1], close[1]]):
                    pl.when(has & ~middle)(direct.wait_send)
                    pl.when(middle)(up[n].wait_send)
                    pl.when(corner)(on[n].wait_send)
            else:
                pl.when(has)(far[1].wait_send)
                pl.when(has)(close[1].wait_send)

    def both(step):
        pl.when(e == 0)(lambda: objects(False, step))
        pl.when(e == 1)(lambda: objects(True, step))

    for copy in swap:
        copy.start()
    both(0)
    round1 = []
    for n in range(pieces):
        swap[n].wait_recv()
        half[:, cut(n), :] = (sums[e, :, cut(n), :] + got0[:, cut(n), :]).astype(half.dtype)
        for k in range(1, chips):
            other = lax.rem(chip + k, chips)
            round1.append(
                send(
                    half.at[other, cut(n)],
                    got1.at[k - 1, cut(n)],
                    out1.at[n, k - 1],
                    in1.at[n, k - 1],
                    t,
                    2 * other + e,
                )
            )
            round1[-1].start()
    both(1)
    for n in range(pieces):
        total = sums[e, chip, cut(n)] + got0[chip, cut(n)]
        for k in range(1, chips):
            round1[n * (chips - 1) + k - 1].wait_recv()
            total = total + got1[k - 1, cut(n)].astype(jnp.float32)
        for s in range(per):
            other = n * per + s
            plane[other] = total[s * 3 * chunk : (s + 1) * 3 * chunk]

            @pl.when(t != other)
            def _(other=other):
                k = lax.rem(other - t + tilts, tilts) - 1
                send(plane.at[other], got2.at[k], out2.at[k], in2.at[k], other, p).start()

    total = plane[t]
    for k in range(1, tilts):
        send(plane.at[0], got2.at[k - 1], out2.at[k - 1], in2.at[k - 1], t, partner).wait_recv()
        total = total + got2[k - 1]
    below = total[2 * chunk :]
    column[...] = total[: 2 * chunk] / jnp.concatenate([below, below], 0)
    result[e, chip, t] = column[...]
    round3 = []
    for k in range(1, tilts):
        other = lax.rem(t + k, tilts)
        round3.append(
            send(column, result.at[e, chip, t], out3.at[k - 1], in3.at[k - 1], other, p)
        )
        round3[-1].start()
    order = sorted(range(tilts), key=lambda m: min(m, tilts - m))
    round4 = []
    for m in order:
        whose = lax.rem(t - m + tilts, tilts)
        if m > 0:
            round3[m - 1].wait_recv()
        for k in range(1, chips):
            other = lax.rem(chip + k, chips)
            round4.append(
                send(
                    result.at[e, chip, whose],
                    result.at[e, chip, whose],
                    out4.at[m, k - 1],
                    in4.at[m, k - 1],
                    t,
                    2 * other + e,
                )
            )
            round4[-1].start()
    both(2)
    back = []
    for n, m in enumerate(order):
        whose = lax.rem(t - m + tilts, tilts)
        for k in range(1, chips):
            round4[n * (chips - 1) + k - 1].wait_recv()
        back.append(
            send(result.at[e, :, whose], result.at[e, :, whose], out5.at[m], in5.at[m], t, partner)
        )
        back[-1].start()
    both(3)
    for side, has, landed in [(0, chip > 0, from_left), (1, chip < chips - 1, from_right)]:

        @pl.when(has)
        def _():
            for c in range(2):
                send(
                    near.at[c], landed.at[c], obj_out.at[1, c], obj_in.at[side, c], t, partner
                ).wait_recv()

    for copy in back:
        copy.wait_recv()
    for copy in swap + round1 + round3 + round4 + back:
        copy.wait_send()
    for k in range(1, tilts):
        send(plane.at[0], got2.at[k - 1], out2.at[k - 1], in2.at[k - 1], t, partner).wait_send()


def exchange(tilts, devices, width, rows, grads, sums):
    vmem = pl.BlockSpec(memory_space=pltpu.VMEM)
    planes, groups = grads.shape[0], grads.shape[1] - 1
    _, chips, part, _ = sums.shape
    third = part // tilts
    pieces = 2 if tilts % 2 == 0 and part % 32 == 0 else 1
    block = (planes, groups, rows, LANES)
    dma = pltpu.SemaphoreType.DMA
    f32, bf16 = jnp.float32, jnp.bfloat16
    return pl.pallas_call(
        functools.partial(exchange_kernel, tilts, devices),
        out_shape=[
            pltpu.VMEM(block, f32),
            pltpu.VMEM(block, bf16),
            pltpu.VMEM(block, bf16),
            pltpu.VMEM((2, chips, tilts, 2 * third // 3, width), f32),
        ],
        in_specs=[vmem] * 2,
        out_specs=[vmem] * 4,
        scratch_shapes=[pltpu.VMEM(block, f32)]
        + [pltpu.VMEM(block, bf16)] * 2
        + [
            pltpu.VMEM((2,) + block[1:], bf16),
            pltpu.VMEM((chips, part, width), bf16),
            pltpu.VMEM((chips, part, width), f32),
            pltpu.VMEM((chips - 1, part, width), bf16),
            pltpu.VMEM((tilts, third, width), f32),
            pltpu.VMEM((2 * third // 3, width), f32),
            pltpu.VMEM((tilts - 1, third, width), f32),
        ]
        + [dma((3, 2)), dma((3, 2)), dma((4,)), dma((2,))]
        + [dma((pieces,))] * 2
        + [dma((pieces, chips - 1))] * 2
        + [dma((tilts - 1,))] * 4
        + [dma((tilts, chips - 1))] * 2
        + [dma((tilts,))] * 2,
        compiler_params=pltpu.CompilerParams(
            collective_id=2, has_side_effects=True, vmem_limit_bytes=20 * 1024 * 1024
        ),
    )(grads, sums)


def finish_kernel(
    devices, total, mine, left, right, result, object_any, probe_any, object_ref, probe_ref, sems
):
    p = lax.axis_index("pos")
    has_left, has_right = p >= 2, p < devices - 2
    groups, rows = mine.shape[1:3]
    pairs, chips, tilts, part, _ = result.shape
    chunk = part // 2
    copies = []

    def leave(src, dst):
        copies.append(pltpu.make_async_copy(src, dst, sems.at[len(copies)]))
        copies[-1].start()

    for k in range(2):
        for i in range(pairs):
            for c in range(chips):
                for s in range(tilts):
                    start = ((i * chips + c) * tilts + s) * chunk
                    probe_ref[k, start : start + chunk, :] = result[
                        i, c, s, k * chunk : (k + 1) * chunk, :
                    ]
        leave(probe_ref.at[k], probe_any.at[k])
    for c in range(2):
        for g in range(groups):
            object_ref[c, :, g * LANES : (g + 1) * LANES] = (
                total[c, g, pl.ds(2 * rows, rows), :]
                + mine[c, g]
                + jnp.where(has_left, left[c, g].astype(jnp.float32), 0.0)
                + jnp.where(has_right, right[c, g].astype(jnp.float32), 0.0)
            )
        leave(object_ref.at[c], object_any.at[0, c])
    for copy in copies:
        copy.wait()


def finish(devices, width, total, mine, left, right, result):
    planes, groups, rows, _ = mine.shape
    vmem = pl.BlockSpec(memory_space=pltpu.VMEM)
    hbm = pl.BlockSpec(memory_space=pltpu.HBM)
    f32 = jnp.float32
    shapes = [(planes, rows, groups * LANES), (2, width, width)]
    return pl.pallas_call(
        functools.partial(finish_kernel, devices),
        out_shape=[
            jax.ShapeDtypeStruct((1,) + shapes[0], f32),
            jax.ShapeDtypeStruct(shapes[1], f32),
        ],
        in_specs=[vmem] * 5,
        out_specs=[hbm] * 2,
        scratch_shapes=[pltpu.VMEM(shape, f32) for shape in shapes]
        + [pltpu.SemaphoreType.DMA((4,))],
        compiler_params=pltpu.CompilerParams(vmem_limit_bytes=16 * 1024 * 1024),
    )(total, mine, left, right, result)


def local(tilts, devices, intensity, positions, counts, object_field, probe):
    width = probe.shape[-1]
    rows = object_field.shape[2]
    reach = width // rows
    assert reach == 2 and devices % 2 == 0
    forward, inverse = dft_tables(width)
    row_order, column_order = orders(width)
    identity = np.eye(width, dtype=np.float32)
    moves = jnp.asarray(
        np.stack([identity[row_order], identity[column_order].T]).astype(ml_dtypes.bfloat16)
    )
    band, frames, probe_v, forward, inverse, places = gather(
        devices, object_field, intensity, probe, forward, inverse, positions[0].T, moves
    )
    parts = (2, devices // 2, 3 * width // devices, width)
    grads, sums = frame_sums(
        reach, tilts, parts, places, counts, frames, band, probe_v, forward, inverse
    )
    parts = exchange(tilts, devices, width, rows, grads, sums)
    return tuple(finish(devices, width, grads, *parts))


def solution(mesh):
    placed = (
        P("tilt", "pos", None, None),
        P("tilt", "pos", None),
        P("tilt", "pos"),
        P("tilt", None, "pos", None),
        P(),
    )
    return jax.shard_map(
        functools.partial(local, mesh.shape["tilt"], mesh.shape["pos"]),
        mesh=mesh,
        in_specs=placed,
        out_specs=(P("tilt", None, "pos", None), P()),
        check_vma=False,
    )
```

```python
import functools
import math

import jax
import jax.numpy as jnp
import ml_dtypes
import numpy as np
from jax import lax
from jax.experimental import pallas as pl
from jax.experimental.pallas import tpu as pltpu
from jax.sharding import PartitionSpec as P

LANES = 128
GROUP = 4
EXTRACT = 256
SPREAD = 64


def orders(length):
    quarter, halfway = length // 4, length // 2
    low = np.concatenate([2 * np.arange(quarter), 2 * np.arange(quarter) + 1])
    mirror = (length - low) % length
    mirror[0] = halfway
    split = np.concatenate([low, mirror])
    plain = np.arange(halfway)
    mirror = (length - plain) % length
    mirror[0] = halfway
    return split, np.concatenate([plain, mirror])


def dft_tables(length):
    index = np.arange(length, dtype=np.int64)
    phase = (index[:, None] * index[None, :] % length).astype(np.float64) * (
        2.0 * np.pi / length
    )
    cosine = np.cos(phase) / np.sqrt(length)
    sine = np.sin(phase) / np.sqrt(length)
    halfway = length // 2
    rows, columns = orders(length)

    def paired(order):
        table = np.concatenate([cosine[:, order[:halfway]], sine[:, order[:halfway]]], 1)
        table[:, halfway] = cosine[:, halfway]
        return table

    forward_columns = paired(columns)
    forward_rows = paired(rows).T
    quarter = length // 4
    even = np.concatenate([rows[:quarter], rows[halfway : halfway + quarter]])
    odd = np.concatenate([rows[quarter:halfway], rows[halfway + quarter :]])

    def side(ks):
        c, s = cosine[:halfway, ks], sine[:halfway, ks]
        return np.block([[c, -s], [s, c]])

    inverse_rows = np.concatenate([side(even), side(odd)], 0)
    c, s = cosine[columns], sine[columns]
    inverse_columns = np.block([[c, s], [-s, c]])
    stack = np.concatenate([forward_columns, forward_rows, inverse_rows], 0)

    def cast(table):
        return jnp.asarray(table.astype(np.float32)).astype(jnp.bfloat16)

    return cast(stack), cast(inverse_columns)


def frames_kernel(
    reach,
    tilts,
    pos_any,
    count_ref,
    frames_ref,
    band,
    probe_ref,
    fwd_ref,
    inv_ref,
    total,
    chunks_ref,
    sums_ref,
    patch_ref,
    pos_ref,
    pos_sem,
):
    fetch = pltpu.make_async_copy(pos_any, pos_ref, pos_sem)
    fetch.start()
    rows = band.shape[2] // (2 * reach + 1)
    width = probe_ref.shape[-1]
    wide = width // LANES

    total[...] = jnp.zeros_like(total)
    sums_ref[...] = jnp.zeros_like(sums_ref)
    first = (lax.axis_index("pos") - reach) * rows
    fetch.wait()

    lane = lax.broadcasted_iota(jnp.int32, (EXTRACT, LANES), 1)
    wide_lane = lax.broadcasted_iota(jnp.int32, (SPREAD, LANES), 1)
    edge = lane == 0
    top = lax.broadcasted_iota(jnp.int32, (8, width), 0) == 0
    mid = width // 2

    def dot(a, b):
        return jnp.dot(a, b, preferred_element_type=jnp.float32)

    def some_frames(at):
        spots = []
        for i in at:
            q = pos_ref[1, i]
            spots.append((pos_ref[0, i] - first, q // LANES, lax.rem(q, LANES)))
        pieces = [[] for _ in at]
        for start in range(0, width, EXTRACT):
            pr, pi = probe_ref[0, start : start + EXTRACT], probe_ref[1, start : start + EXTRACT]
            exits = []
            for n, (r, qb, qs) in enumerate(spots):
                near = lane < LANES - qs
                back_shift = lax.rem(LANES - qs, LANES)
                patch = []
                for c in range(2):
                    rolled = [
                        pltpu.roll(band[c, qb + j, pl.ds(r + start, EXTRACT), :], back_shift, 1)
                        for j in range(wide + 1)
                    ]
                    patch.append(
                        jnp.concatenate(
                            [jnp.where(near, rolled[j], rolled[j + 1]) for j in range(wide)], 1
                        )
                    )
                    patch_ref[n, c, start : start + EXTRACT] = patch[c]
                xr, xi = patch
                exits.append((pr * xr - pi * xi).astype(jnp.bfloat16))
                exits.append((pr * xi + pi * xr).astype(jnp.bfloat16))
            out = dot(jnp.concatenate(exits, 0), fwd_ref[0:width])
            for n in range(len(at)):
                re = out[2 * n * EXTRACT : (2 * n + 1) * EXTRACT]
                im = out[(2 * n + 1) * EXTRACT : (2 * n + 2) * EXTRACT]
                u, v, uu, vv = re[:, :LANES], re[:, LANES:], im[:, :LANES], im[:, LANES:]
                pieces[n].append(
                    jnp.concatenate(
                        [
                            u + jnp.where(edge, 0.0, vv),
                            jnp.where(edge, v, u - vv),
                            uu - jnp.where(edge, 0.0, v),
                            jnp.where(edge, vv, uu + v),
                        ],
                        1,
                    ).astype(jnp.bfloat16)
                )
        backs = []
        for n, i in enumerate(at):
            far = dot(fwd_ref[width : 2 * width], jnp.concatenate(pieces[n], 0))
            u, v = far[:mid, :width], far[mid:, :width]
            uu, vv = far[:mid, width:], far[mid:, width:]
            fr = jnp.concatenate(
                [
                    u[:8] + jnp.where(top, 0.0, vv[:8]),
                    u[8:] + vv[8:],
                    jnp.where(top, v[:8], u[:8] - vv[:8]),
                    u[8:] - vv[8:],
                ],
                0,
            )
            fi = jnp.concatenate(
                [
                    uu[:8] - jnp.where(top, 0.0, v[:8]),
                    uu[8:] - v[8:],
                    jnp.where(top, vv[:8], uu[:8] + v[:8]),
                    uu[8:] + v[8:],
                ],
                0,
            )
            misfit = fr * fr + fi * fi - frames_ref[i].astype(jnp.float32)
            br = (fr * misfit).astype(jnp.bfloat16)
            bi = (fi * misfit).astype(jnp.bfloat16)
            q = mid // 2
            backs.append(
                (
                    jnp.concatenate([br[:q], br[mid : mid + q], bi[:q], bi[mid : mid + q]], 0),
                    jnp.concatenate([br[q:mid], br[mid + q :], bi[q:mid], bi[mid + q :]], 0),
                )
            )
        mids = []
        for n, i in enumerate(at):
            ev = dot(fwd_ref[2 * width : 3 * width], backs[n][0])
            od = dot(fwd_ref[3 * width :], backs[n][1])
            add, sub = (ev + od).astype(jnp.bfloat16), (ev - od).astype(jnp.bfloat16)
            mids.append(
                jnp.concatenate(
                    [
                        jnp.concatenate([add[:mid], sub[:mid]], 0),
                        jnp.concatenate([add[mid:], sub[mid:]], 0),
                    ],
                    1,
                )
            )
        for start in range(0, width, SPREAD):
            waves = dot(
                jnp.concatenate([m[start : start + SPREAD] for m in mids], 0), inv_ref[...]
            )
            pr, pi = probe_ref[0, start : start + SPREAD], probe_ref[1, start : start + SPREAD]
            sums = [0.0, 0.0, 0.0]
            for n, (r, qb, qs) in enumerate(spots):
                xr = patch_ref[n, 0, start : start + SPREAD]
                xi = patch_ref[n, 1, start : start + SPREAD]
                wave = waves[n * SPREAD : (n + 1) * SPREAD]
                wr, wi = wave[:, :width], wave[:, width:]
                sums[0] += xr * wr + xi * wi
                sums[1] += xr * wi - xi * wr
                sums[2] += xr * xr + xi * xi
                far_side = wide_lane >= qs
                for c in range(2):
                    grad = pr * wr + pi * wi if c == 0 else pr * wi - pi * wr
                    grad = grad.astype(jnp.bfloat16).astype(jnp.float32)
                    rolled = [
                        pltpu.roll(grad[:, j * LANES : (j + 1) * LANES], qs, 1)
                        for j in range(wide)
                    ]
                    zero = jnp.zeros_like(rolled[0])
                    for j in range(wide + 1):
                        here = rolled[j] if j < wide else zero
                        before = rolled[j - 1] if j > 0 else zero
                        total[c, qb + j, pl.ds(r + start, SPREAD), :] += jnp.where(
                            far_side, here, before
                        )
            for k in range(3):
                sums_ref[k, start : start + SPREAD] += sums[k]

    count = count_ref[0, 0]
    group = GROUP

    @pl.loop(0, count // group)
    def _(i):
        some_frames([group * i + n for n in range(group)])

    done = count // group * group
    for size in (2, 1):
        left = (count - done) // size

        @pl.when(left > 0)
        def _(done=done, size=size):
            some_frames([done + n for n in range(size)])

        done = done + left * size

    pairs, chips, _, _ = chunks_ref.shape
    chunk = chunks_ref.shape[2] // (3 * tilts)
    for e in range(pairs):
        for c in range(chips):
            for t in range(tilts):
                start = ((e * chips + c) * tilts + t) * chunk
                for k in range(3):
                    chunks_ref[e, c, pl.ds((t * 3 + k) * chunk, chunk), :] = sums_ref[
                        k, start : start + chunk, :
                    ]


def frame_sums(reach, tilts, parts, positions, count, frames, band, probe, forward, inverse):
    vmem = pl.BlockSpec(memory_space=pltpu.VMEM)
    smem = pl.BlockSpec(memory_space=pltpu.SMEM)
    return pl.pallas_call(
        functools.partial(frames_kernel, reach, tilts),
        out_shape=[
            jax.ShapeDtypeStruct(band.shape, jnp.float32),
            jax.ShapeDtypeStruct(parts, jnp.float32),
        ],
        in_specs=[vmem, smem] + [vmem] * 5,
        out_specs=[vmem] * 2,
        scratch_shapes=[
            pltpu.VMEM((3,) + probe.shape[1:], jnp.float32),
            pltpu.VMEM((GROUP, 2) + probe.shape[1:], jnp.float32),
            pltpu.SMEM(positions.shape, jnp.int32),
            pltpu.SemaphoreType.DMA,
        ],
        compiler_params=pltpu.CompilerParams(vmem_limit_bytes=24 * 1024 * 1024),
    )(positions, count, frames, band, probe, forward, inverse)


def greet(tilts, devices, meanwhile=lambda: None):
    t, p = lax.axis_index("tilt"), lax.axis_index("pos")
    barrier = pltpu.get_barrier_semaphore()
    for k in range(1, devices):
        pl.semaphore_signal(
            barrier,
            inc=1,
            device_id=(t, lax.rem(p + k, devices)),
            device_id_type=pl.DeviceIdType.MESH,
        )
    for k in range(1, tilts):
        pl.semaphore_signal(
            barrier,
            inc=1,
            device_id=(lax.rem(t + k, tilts), p),
            device_id_type=pl.DeviceIdType.MESH,
        )
    meanwhile()
    pl.semaphore_wait(barrier, devices - 1 + tilts - 1)


def send(src, dst, sem_out, sem_in, tilt, pos):
    return pltpu.make_async_remote_copy(
        src_ref=src,
        dst_ref=dst,
        send_sem=sem_out,
        recv_sem=sem_in,
        device_id=(tilt, pos),
        device_id_type=pl.DeviceIdType.MESH,
    )


def relayed(devices):
    return devices == 8


def gather_kernel(
    devices,
    field_any,
    frames_any,
    probe_any,
    fwd_any,
    inv_any,
    pos_any,
    moves_any,
    band,
    frames_ref,
    probe_ref,
    fwd_ref,
    inv_ref,
    pos_ref,
    own,
    slots,
    stage,
    raw_ref,
    moves_ref,
    out_sem,
    in_sem,
    relay_out,
    relay_in,
    local_sem,
):
    t, p = lax.axis_index("tilt"), lax.axis_index("pos")
    chip, chips = p // 2, devices // 2
    rows = own.shape[1]
    groups = own.shape[2] // LANES

    own_copy = pltpu.make_async_copy(field_any.at[0], own, local_sem.at[0])
    own_copy.start()
    loads = [
        pltpu.make_async_copy(src, dst, local_sem.at[1 + n])
        for n, (src, dst) in enumerate(
            [
                (pos_any, pos_ref),
                (probe_any, probe_ref),
                (fwd_any, fwd_ref),
                (inv_any, inv_ref),
                (moves_any, moves_ref),
                (frames_any.at[0], raw_ref),
            ]
        )
    ]
    greet(1, devices)
    own_copy.wait()

    def place(src, b):
        for c in range(2):
            for g in range(groups):
                band[c, g, pl.ds(b * rows, rows), :] = src[
                    c, :, g * LANES : (g + 1) * LANES
                ].astype(jnp.float32)

    def reorder():
        slots_of, width = raw_ref.shape[0], raw_ref.shape[1]
        some = math.gcd(slots_of, 4)

        @pl.loop(0, slots_of // some)
        def _(i):
            moved = jnp.dot(
                jnp.concatenate([raw_ref[i * some + n] for n in range(some)], 0),
                moves_ref[1],
                preferred_element_type=jnp.float32,
            ).astype(jnp.bfloat16)
            for n in range(some):
                frames_ref[i * some + n] = jnp.dot(
                    moves_ref[0],
                    moved[n * width : (n + 1) * width],
                    preferred_element_type=jnp.float32,
                ).astype(frames_ref.dtype)

    def role(odd):
        partner = p - 1 if odd else p + 1
        has_left, has_right = chip > 0, chip < chips - 1
        near, far = (3, 4) if odd else (1, 0)
        onward = 4 if odd else 0
        from_partner = 1 if odd else 3
        opposite = 0 if odd else 4
        outer, inner = (has_right, has_left) if odd else (has_left, has_right)
        slot_left, slot_right = (4, 1) if odd else (3, 0)
        pos_left, pos_right = 2 * chip - 1, 2 * chip + 2

        def copy(src, slot, c, out, pos):
            return send(
                src.at[c], slots.at[slot, c], out_sem.at[out, c], in_sem.at[slot, c], t, pos
            )

        to_left = [copy(own, slot_left, c, 1, pos_left) for c in range(2)]
        to_right = [copy(own, slot_right, c, 2, pos_right) for c in range(2)]
        to_partner = [copy(own, 3 if odd else 1, c, 0, partner) for c in range(2)]
        forward = [copy(slots.at[near], onward, c, 3, partner) for c in range(2)]

        def arrived(slot, c):
            copy(own, slot, c, 0, partner).wait_recv()

        to_near, to_far = (to_right, to_left) if odd else (to_left, to_right)
        has_near, has_far = (has_right, has_left) if odd else (has_left, has_right)
        if relayed(devices):
            across = lax.rem(p + 4, 8)
            source, relay = (chip == 2, chip == 0) if odd else (chip == 1, chip == 3)
            slot_far, pos_far = (slot_left, 3) if odd else (slot_right, 4)
            direct = has_far & ~source
            to_stage = [
                send(own.at[c], stage.at[c], relay_out.at[0, c], relay_in.at[c], t, across)
                for c in range(2)
            ]
            staged = [
                send(
                    stage.at[c],
                    slots.at[slot_far, c],
                    relay_out.at[1, c],
                    in_sem.at[slot_far, c],
                    t,
                    pos_far,
                )
                for c in range(2)
            ]
        else:
            direct = has_far
        for c in range(2):
            if relayed(devices):
                pl.when(source)(to_stage[c].start)
            pl.when(has_near)(to_near[c].start)
        for c in range(2):
            pl.when(direct)(to_far[c].start)
        for c in range(2):
            to_partner[c].start()
        for load in loads:
            load.start()
        for c in range(2):
            band[c, groups] = jnp.zeros(band.shape[2:], jnp.float32)
        place(own, 2)
        for c in range(2):
            arrived(from_partner, c)
        place(slots.at[from_partner], from_partner)
        for load in loads:
            load.wait()
        reorder()
        if relayed(devices):

            @pl.when(relay)
            def _():
                for c in range(2):
                    to_stage[c].wait_recv()
                    staged[c].start()

        @pl.when(outer)
        def _():
            for c in range(2):
                arrived(near, c)
                forward[c].start()
            place(slots.at[near], near)
            for c in range(2):
                arrived(far, c)
            place(slots.at[far], far)

        @pl.when(inner)
        def _():
            for c in range(2):
                arrived(opposite, c)
            place(slots.at[opposite], opposite)

        for c in range(2):
            pl.when(has_near)(to_near[c].wait_send)
            pl.when(direct)(to_far[c].wait_send)
            if relayed(devices):
                pl.when(source)(to_stage[c].wait_send)
                pl.when(relay)(staged[c].wait_send)
        for c in range(2):
            to_partner[c].wait_send()
            pl.when(outer)(forward[c].wait_send)

    pl.when(lax.rem(p, 2) == 0)(lambda: role(False))
    pl.when(lax.rem(p, 2) == 1)(lambda: role(True))


def gather(devices, field, frames, probe, forward, inverse, positions, moves):
    hbm = pl.BlockSpec(memory_space=pltpu.HBM)
    vmem = pl.BlockSpec(memory_space=pltpu.VMEM)
    _, planes, rows, columns = field.shape
    block = (planes, rows, columns)
    groups = columns // LANES
    dma = pltpu.SemaphoreType.DMA
    held = 4 * planes * (groups + 1) * 5 * rows * LANES + sum(
        a.size * a.dtype.itemsize for a in (frames, probe, forward, inverse)
    )
    return pl.pallas_call(
        functools.partial(gather_kernel, devices),
        out_shape=[
            pltpu.VMEM((planes, groups + 1, 5 * rows, LANES), jnp.float32),
            pltpu.VMEM(frames.shape[1:], frames.dtype),
            pltpu.VMEM(probe.shape, probe.dtype),
            pltpu.VMEM(forward.shape, forward.dtype),
            pltpu.VMEM(inverse.shape, inverse.dtype),
            pltpu.VMEM(positions.shape, positions.dtype),
        ],
        in_specs=[hbm] * 7,
        out_specs=[vmem] * 6,
        scratch_shapes=[
            pltpu.VMEM(block, field.dtype),
            pltpu.VMEM((5,) + block, field.dtype),
            pltpu.VMEM(block, field.dtype),
            pltpu.VMEM(frames.shape[1:], frames.dtype),
            pltpu.VMEM(moves.shape, moves.dtype),
            dma((4, 2)),
            dma((5, 2)),
            dma((2, 2)),
            dma((2,)),
            dma((7,)),
        ],
        compiler_params=pltpu.CompilerParams(
            collective_id=1, has_side_effects=True, vmem_limit_bytes=62 * 1024 * 1024 - held
        ),
    )(field, frames, probe, forward, inverse, positions, moves)


def exchange_kernel(tilts, devices, *refs):
    grads, sums, mine, from_left, from_right, result = refs[:6]
    extra, near, distant, stage = refs[6:10]
    half, got0, got1, plane, column, got2, given = refs[10:17]
    obj_out, obj_in, stage_out, stage_in = refs[17:21]
    out0, in0, out1, in1, out2, in2, out3, in3, out4, in4, out5, in5 = refs[21:]
    t, p = lax.axis_index("tilt"), lax.axis_index("pos")
    chip, chips = p // 2, devices // 2
    e = lax.rem(p, 2)
    partner = p + 1 - 2 * e
    groups, rows = mine.shape[1:3]
    chunk = column.shape[0] // 2
    relay = relayed(devices)

    def meanwhile():
        given[...] = sums[1 - e].astype(given.dtype)

    greet(tilts, devices, meanwhile)

    def block(b):
        return grads.at[:, pl.ds(0, groups), pl.ds(b * rows, rows), :]

    chips_rows = half.shape[1]
    pieces = out0.shape[0]
    piece = chips_rows // pieces
    per = tilts // pieces

    def cut(n):
        return pl.ds(n * piece, piece)

    swap = [
        send(
            given.at[:, cut(n), :], got0.at[:, cut(n), :], out0.at[n], in0.at[n], t, partner
        )
        for n in range(pieces)
    ]

    def objects(odd, step):
        has = chip < chips - 1 if odd else chip > 0
        way = 1 if odd else -1
        middle = (chip == 1) if odd else (chip == 2)
        corner = (chip == 3) if odd else (chip == 0)
        lands = from_left if odd else from_right
        side = 0 if odd else 1
        across = lax.rem(p + 4, 8)

        def out(src, n, c, pos):
            return send(src.at[c], lands.at[c], obj_out.at[n, c], obj_in.at[side, c], t, pos)

        far = [out(distant, 0, c, p + 2 * way) for c in range(2)]
        close = [out(near, 1, c, p + way) for c in range(2)]
        to_extra = send(
            block(0 if odd else 4), extra, obj_out.at[2, 0], obj_in.at[2, 0], t, partner
        )
        to_mine = send(block(1 if odd else 3), mine, obj_out.at[2, 1], obj_in.at[2, 1], t, partner)
        if relay:
            up = [
                send(src.at[1], stage.at[n], stage_out.at[n], stage_in.at[n], t, across)
                for n, src in enumerate([distant, near])
            ]
            onto = [(5, 4), (2, 3)][side]
            on = [
                send(stage.at[n], lands.at[1], stage_out.at[2 + n], obj_in.at[side, 1], t, onto[n])
                for n in range(2)
            ]
        if step == 0:
            to_extra.start()
            b = 4 if odd else 0
            for c in range(2):
                distant[c] = grads[c, 0:groups, pl.ds(b * rows, rows), :].astype(distant.dtype)
            if relay:
                pl.when(middle)(up[0].start)
        elif step == 1:
            if relay:
                pl.when(has)(far[0].start)
                pl.when(has & ~middle)(far[1].start)
            else:
                pl.when(has)(far[0].start)
                pl.when(has)(far[1].start)
            to_mine.start()
            to_extra.wait_recv()
            b = 3 if odd else 1
            for c in range(2):
                near[c] = (
                    grads[c, 0:groups, pl.ds(b * rows, rows), :] + extra[c]
                ).astype(near.dtype)
            pl.when(has)(close[0].start)
            if relay:
                pl.when(middle)(up[1].start)

                @pl.when(corner)
                def _():
                    up[0].wait_recv()
                    on[0].start()
        elif step == 2:
            if relay:
                pl.when(has & ~middle)(close[1].start)

                @pl.when(corner)
                def _():
                    up[1].wait_recv()
                    on[1].start()
            else:
                pl.when(has)(close[1].start)
        else:
            to_mine.wait_recv()
            to_extra.wait_send()
            to_mine.wait_send()
            pl.when(has)(far[0].wait_send)
            pl.when(has)(close[0].wait_send)
            if relay:
                for n, direct in enumerate([far[1], close[1]]):
                    pl.when(has & ~middle)(direct.wait_send)
                    pl.when(middle)(up[n].wait_send)
                    pl.when(corner)(on[n].wait_send)
            else:
                pl.when(has)(far[1].wait_send)
                pl.when(has)(close[1].wait_send)

    def both(step):
        pl.when(e == 0)(lambda: objects(False, step))
        pl.when(e == 1)(lambda: objects(True, step))

    for copy in swap:
        copy.start()
    both(0)
    round1 = []
    for n in range(pieces):
        swap[n].wait_recv()
        half[:, cut(n), :] = (
            sums[e, :, cut(n), :] + got0[:, cut(n), :].astype(jnp.float32)
        ).astype(half.dtype)
        for k in range(1, chips):
            other = lax.rem(chip + k, chips)
            round1.append(
                send(
                    half.at[other, cut(n)],
                    got1.at[k - 1, cut(n)],
                    out1.at[n, k - 1],
                    in1.at[n, k - 1],
                    t,
                    2 * other + e,
                )
            )
            round1[-1].start()
    both(1)
    for n in range(pieces):
        total = sums[e, chip, cut(n)] + got0[chip, cut(n)].astype(jnp.float32)
        for k in range(1, chips):
            round1[n * (chips - 1) + k - 1].wait_recv()
            total = total + got1[k - 1, cut(n)].astype(jnp.float32)
        for s in range(per):
            other = n * per + s
            plane[other] = total[s * 3 * chunk : (s + 1) * 3 * chunk]

            @pl.when(t != other)
            def _(other=other):
                k = lax.rem(other - t + tilts, tilts) - 1
                send(plane.at[other], got2.at[k], out2.at[k], in2.at[k], other, p).start()

    total = plane[t]
    for k in range(1, tilts):
        send(plane.at[0], got2.at[k - 1], out2.at[k - 1], in2.at[k - 1], t, partner).wait_recv()
        total = total + got2[k - 1]
    below = total[2 * chunk :]
    column[...] = total[: 2 * chunk] / jnp.concatenate([below, below], 0)
    result[e, chip, t] = column[...]
    round3 = []
    for k in range(1, tilts):
        other = lax.rem(t + k, tilts)
        round3.append(
            send(column, result.at[e, chip, t], out3.at[k - 1], in3.at[k - 1], other, p)
        )
        round3[-1].start()
    order = sorted(range(tilts), key=lambda m: min(m, tilts - m))
    round4 = []
    for m in order:
        whose = lax.rem(t - m + tilts, tilts)
        if m > 0:
            round3[m - 1].wait_recv()
        for k in range(1, chips):
            other = lax.rem(chip + k, chips)
            round4.append(
                send(
                    result.at[e, chip, whose],
                    result.at[e, chip, whose],
                    out4.at[m, k - 1],
                    in4.at[m, k - 1],
                    t,
                    2 * other + e,
                )
            )
            round4[-1].start()
    both(2)
    back = []
    for n, m in enumerate(order):
        whose = lax.rem(t - m + tilts, tilts)
        for k in range(1, chips):
            round4[n * (chips - 1) + k - 1].wait_recv()
        back.append(
            send(result.at[e, :, whose], result.at[e, :, whose], out5.at[m], in5.at[m], t, partner)
        )
        back[-1].start()
    both(3)
    for side, has, landed in [(0, chip > 0, from_left), (1, chip < chips - 1, from_right)]:

        @pl.when(has)
        def _():
            for c in range(2):
                send(
                    near.at[c], landed.at[c], obj_out.at[1, c], obj_in.at[side, c], t, partner
                ).wait_recv()

    for copy in back:
        copy.wait_recv()
    for copy in swap + round1 + round3 + round4 + back:
        copy.wait_send()
    for k in range(1, tilts):
        send(plane.at[0], got2.at[k - 1], out2.at[k - 1], in2.at[k - 1], t, partner).wait_send()


def exchange(tilts, devices, width, rows, grads, sums):
    vmem = pl.BlockSpec(memory_space=pltpu.VMEM)
    planes, groups = grads.shape[0], grads.shape[1] - 1
    _, chips, part, _ = sums.shape
    third = part // tilts
    pieces = 2 if tilts % 2 == 0 and part % 32 == 0 else 1
    block = (planes, groups, rows, LANES)
    dma = pltpu.SemaphoreType.DMA
    f32, bf16 = jnp.float32, jnp.bfloat16
    return pl.pallas_call(
        functools.partial(exchange_kernel, tilts, devices),
        out_shape=[
            pltpu.VMEM(block, f32),
            pltpu.VMEM(block, bf16),
            pltpu.VMEM(block, bf16),
            pltpu.VMEM((2, chips, tilts, 2 * third // 3, width), f32),
        ],
        in_specs=[vmem] * 2,
        out_specs=[vmem] * 4,
        scratch_shapes=[pltpu.VMEM(block, f32)]
        + [pltpu.VMEM(block, bf16)] * 2
        + [
            pltpu.VMEM((2,) + block[1:], bf16),
            pltpu.VMEM((chips, part, width), bf16),
            pltpu.VMEM((chips, part, width), bf16),
            pltpu.VMEM((chips - 1, part, width), bf16),
            pltpu.VMEM((tilts, third, width), f32),
            pltpu.VMEM((2 * third // 3, width), f32),
            pltpu.VMEM((tilts - 1, third, width), f32),
            pltpu.VMEM((chips, part, width), bf16),
        ]
        + [dma((3, 2)), dma((3, 2)), dma((4,)), dma((2,))]
        + [dma((pieces,))] * 2
        + [dma((pieces, chips - 1))] * 2
        + [dma((tilts - 1,))] * 4
        + [dma((tilts, chips - 1))] * 2
        + [dma((tilts,))] * 2,
        compiler_params=pltpu.CompilerParams(
            collective_id=2, has_side_effects=True, vmem_limit_bytes=20 * 1024 * 1024
        ),
    )(grads, sums)


def finish_kernel(
    devices, total, mine, left, right, result, object_any, probe_any, object_ref, probe_ref, sems
):
    p = lax.axis_index("pos")
    has_left, has_right = p >= 2, p < devices - 2
    groups, rows = mine.shape[1:3]
    pairs, chips, tilts, part, _ = result.shape
    chunk = part // 2
    copies = []

    def leave(src, dst):
        copies.append(pltpu.make_async_copy(src, dst, sems.at[len(copies)]))
        copies[-1].start()

    for k in range(2):
        for i in range(pairs):
            for c in range(chips):
                for s in range(tilts):
                    start = ((i * chips + c) * tilts + s) * chunk
                    probe_ref[k, start : start + chunk, :] = result[
                        i, c, s, k * chunk : (k + 1) * chunk, :
                    ]
        leave(probe_ref.at[k], probe_any.at[k])
    for c in range(2):
        for g in range(groups):
            object_ref[c, :, g * LANES : (g + 1) * LANES] = (
                total[c, g, pl.ds(2 * rows, rows), :]
                + mine[c, g]
                + jnp.where(has_left, left[c, g].astype(jnp.float32), 0.0)
                + jnp.where(has_right, right[c, g].astype(jnp.float32), 0.0)
            )
        leave(object_ref.at[c], object_any.at[0, c])
    for copy in copies:
        copy.wait()


def finish(devices, width, total, mine, left, right, result):
    planes, groups, rows, _ = mine.shape
    vmem = pl.BlockSpec(memory_space=pltpu.VMEM)
    hbm = pl.BlockSpec(memory_space=pltpu.HBM)
    f32 = jnp.float32
    shapes = [(planes, rows, groups * LANES), (2, width, width)]
    return pl.pallas_call(
        functools.partial(finish_kernel, devices),
        out_shape=[
            jax.ShapeDtypeStruct((1,) + shapes[0], f32),
            jax.ShapeDtypeStruct(shapes[1], f32),
        ],
        in_specs=[vmem] * 5,
        out_specs=[hbm] * 2,
        scratch_shapes=[pltpu.VMEM(shape, f32) for shape in shapes]
        + [pltpu.SemaphoreType.DMA((4,))],
        compiler_params=pltpu.CompilerParams(vmem_limit_bytes=16 * 1024 * 1024),
    )(total, mine, left, right, result)


def local(tilts, devices, intensity, positions, counts, object_field, probe):
    width = probe.shape[-1]
    rows = object_field.shape[2]
    reach = width // rows
    assert reach == 2 and devices % 2 == 0
    forward, inverse = dft_tables(width)
    row_order, column_order = orders(width)
    identity = np.eye(width, dtype=np.float32)
    moves = jnp.asarray(
        np.stack([identity[row_order], identity[column_order].T]).astype(ml_dtypes.bfloat16)
    )
    band, frames, probe_v, forward, inverse, places = gather(
        devices, object_field, intensity, probe, forward, inverse, positions[0].T, moves
    )
    parts = (2, devices // 2, 3 * width // devices, width)
    grads, sums = frame_sums(
        reach, tilts, parts, places, counts, frames, band, probe_v, forward, inverse
    )
    parts = exchange(tilts, devices, width, rows, grads, sums)
    return tuple(finish(devices, width, grads, *parts))


def solution(mesh):
    placed = (
        P("tilt", "pos", None, None),
        P("tilt", "pos", None),
        P("tilt", "pos"),
        P("tilt", None, "pos", None),
        P(),
    )
    return jax.shard_map(
        functools.partial(local, mesh.shape["tilt"], mesh.shape["pos"]),
        mesh=mesh,
        in_specs=placed,
        out_specs=(P("tilt", None, "pos", None), P()),
        check_vma=False,
    )
```

```python
import functools
import math

import jax
import jax.numpy as jnp
import ml_dtypes
import numpy as np
from jax import lax
from jax.experimental import pallas as pl
from jax.experimental.pallas import tpu as pltpu
from jax.sharding import PartitionSpec as P

LANES = 128
GROUP = 4
EXTRACT = 256
SPREAD = 64


def orders(length):
    quarter, halfway = length // 4, length // 2
    low = np.concatenate([2 * np.arange(quarter), 2 * np.arange(quarter) + 1])
    mirror = (length - low) % length
    mirror[0] = halfway
    split = np.concatenate([low, mirror])
    plain = np.arange(halfway)
    mirror = (length - plain) % length
    mirror[0] = halfway
    return split, np.concatenate([plain, mirror])


def dft_tables(length):
    index = np.arange(length, dtype=np.int64)
    phase = (index[:, None] * index[None, :] % length).astype(np.float64) * (
        2.0 * np.pi / length
    )
    cosine = np.cos(phase) / np.sqrt(length)
    sine = np.sin(phase) / np.sqrt(length)
    halfway = length // 2
    rows, columns = orders(length)

    def paired(order):
        table = np.concatenate([cosine[:, order[:halfway]], sine[:, order[:halfway]]], 1)
        table[:, halfway] = cosine[:, halfway]
        return table

    forward_columns = paired(columns)
    forward_rows = paired(rows).T
    quarter = length // 4
    even = np.concatenate([rows[:quarter], rows[halfway : halfway + quarter]])
    odd = np.concatenate([rows[quarter:halfway], rows[halfway + quarter :]])

    def side(ks):
        c, s = cosine[:halfway, ks], sine[:halfway, ks]
        return np.block([[c, -s], [s, c]])

    inverse_rows = np.concatenate([side(even), side(odd)], 0)
    c, s = cosine[columns], sine[columns]
    inverse_columns = np.block([[c, s], [-s, c]])
    stack = np.concatenate([forward_columns, forward_rows, inverse_rows], 0)

    def cast(table):
        return jnp.asarray(table.astype(np.float32)).astype(jnp.bfloat16)

    return cast(stack), cast(inverse_columns)


def frames_kernel(
    reach,
    tilts,
    pos_any,
    count_ref,
    frames_ref,
    band,
    probe_ref,
    fwd_ref,
    inv_ref,
    total,
    chunks_ref,
    sums_ref,
    patch_ref,
    pos_ref,
    pos_sem,
):
    fetch = pltpu.make_async_copy(pos_any, pos_ref, pos_sem)
    fetch.start()
    rows = band.shape[2] // (2 * reach + 1)
    width = probe_ref.shape[-1]
    wide = width // LANES

    total[...] = jnp.zeros_like(total)
    sums_ref[...] = jnp.zeros_like(sums_ref)
    first = (lax.axis_index("pos") - reach) * rows
    fetch.wait()

    lane = lax.broadcasted_iota(jnp.int32, (EXTRACT, LANES), 1)
    wide_lane = lax.broadcasted_iota(jnp.int32, (SPREAD, LANES), 1)
    edge = lane == 0
    top = lax.broadcasted_iota(jnp.int32, (8, width), 0) == 0
    mid = width // 2

    def dot(a, b):
        return jnp.dot(a, b, preferred_element_type=jnp.float32)

    def some_frames(at):
        spots = []
        for i in at:
            q = pos_ref[1, i]
            spots.append((pos_ref[0, i] - first, q // LANES, lax.rem(q, LANES)))
        pieces = [[] for _ in at]
        for start in range(0, width, EXTRACT):
            pr, pi = probe_ref[0, start : start + EXTRACT], probe_ref[1, start : start + EXTRACT]
            exits = []
            for n, (r, qb, qs) in enumerate(spots):
                near = lane < LANES - qs
                back_shift = lax.rem(LANES - qs, LANES)
                patch = []
                for c in range(2):
                    rolled = [
                        pltpu.roll(band[c, qb + j, pl.ds(r + start, EXTRACT), :], back_shift, 1)
                        for j in range(wide + 1)
                    ]
                    patch.append(
                        jnp.concatenate(
                            [jnp.where(near, rolled[j], rolled[j + 1]) for j in range(wide)], 1
                        )
                    )
                    patch_ref[n, c, start : start + EXTRACT] = patch[c]
                xr, xi = patch
                exits.append((pr * xr - pi * xi).astype(jnp.bfloat16))
                exits.append((pr * xi + pi * xr).astype(jnp.bfloat16))
            out = dot(jnp.concatenate(exits, 0), fwd_ref[0:width])
            for n in range(len(at)):
                re = out[2 * n * EXTRACT : (2 * n + 1) * EXTRACT]
                im = out[(2 * n + 1) * EXTRACT : (2 * n + 2) * EXTRACT]
                u, v, uu, vv = re[:, :LANES], re[:, LANES:], im[:, :LANES], im[:, LANES:]
                pieces[n].append(
                    jnp.concatenate(
                        [
                            u + jnp.where(edge, 0.0, vv),
                            jnp.where(edge, v, u - vv),
                            uu - jnp.where(edge, 0.0, v),
                            jnp.where(edge, vv, uu + v),
                        ],
                        1,
                    ).astype(jnp.bfloat16)
                )
        backs = []
        for n, i in enumerate(at):
            far = dot(fwd_ref[width : 2 * width], jnp.concatenate(pieces[n], 0))
            u, v = far[:mid, :width], far[mid:, :width]
            uu, vv = far[:mid, width:], far[mid:, width:]
            fr = jnp.concatenate(
                [
                    u[:8] + jnp.where(top, 0.0, vv[:8]),
                    u[8:] + vv[8:],
                    jnp.where(top, v[:8], u[:8] - vv[:8]),
                    u[8:] - vv[8:],
                ],
                0,
            )
            fi = jnp.concatenate(
                [
                    uu[:8] - jnp.where(top, 0.0, v[:8]),
                    uu[8:] - v[8:],
                    jnp.where(top, vv[:8], uu[:8] + v[:8]),
                    uu[8:] + v[8:],
                ],
                0,
            )
            misfit = fr * fr + fi * fi - frames_ref[i].astype(jnp.float32)
            br = (fr * misfit).astype(jnp.bfloat16)
            bi = (fi * misfit).astype(jnp.bfloat16)
            q = mid // 2
            backs.append(
                (
                    jnp.concatenate([br[:q], br[mid : mid + q], bi[:q], bi[mid : mid + q]], 0),
                    jnp.concatenate([br[q:mid], br[mid + q :], bi[q:mid], bi[mid + q :]], 0),
                )
            )
        mids = []
        for n, i in enumerate(at):
            ev = dot(fwd_ref[2 * width : 3 * width], backs[n][0])
            od = dot(fwd_ref[3 * width :], backs[n][1])
            add, sub = (ev + od).astype(jnp.bfloat16), (ev - od).astype(jnp.bfloat16)
            mids.append(
                jnp.concatenate(
                    [
                        jnp.concatenate([add[:mid], sub[:mid]], 0),
                        jnp.concatenate([add[mid:], sub[mid:]], 0),
                    ],
                    1,
                )
            )
        for start in range(0, width, SPREAD):
            waves = dot(
                jnp.concatenate([m[start : start + SPREAD] for m in mids], 0), inv_ref[...]
            )
            pr, pi = probe_ref[0, start : start + SPREAD], probe_ref[1, start : start + SPREAD]
            sums = [0.0, 0.0, 0.0]
            for n, (r, qb, qs) in enumerate(spots):
                xr = patch_ref[n, 0, start : start + SPREAD]
                xi = patch_ref[n, 1, start : start + SPREAD]
                wave = waves[n * SPREAD : (n + 1) * SPREAD]
                wr, wi = wave[:, :width], wave[:, width:]
                sums[0] += xr * wr + xi * wi
                sums[1] += xr * wi - xi * wr
                sums[2] += xr * xr + xi * xi
                far_side = wide_lane >= qs
                for c in range(2):
                    grad = pr * wr + pi * wi if c == 0 else pr * wi - pi * wr
                    grad = grad.astype(jnp.bfloat16).astype(jnp.float32)
                    rolled = [
                        pltpu.roll(grad[:, j * LANES : (j + 1) * LANES], qs, 1)
                        for j in range(wide)
                    ]
                    zero = jnp.zeros_like(rolled[0])
                    for j in range(wide + 1):
                        here = rolled[j] if j < wide else zero
                        before = rolled[j - 1] if j > 0 else zero
                        total[c, qb + j, pl.ds(r + start, SPREAD), :] += jnp.where(
                            far_side, here, before
                        )
            for k in range(3):
                sums_ref[k, start : start + SPREAD] += sums[k]

    count = count_ref[0, 0]
    group = GROUP

    @pl.loop(0, count // group)
    def _(i):
        some_frames([group * i + n for n in range(group)])

    done = count // group * group
    for size in (2, 1):
        left = (count - done) // size

        @pl.when(left > 0)
        def _(done=done, size=size):
            some_frames([done + n for n in range(size)])

        done = done + left * size

    pairs, chips, _, _ = chunks_ref.shape
    chunk = chunks_ref.shape[2] // (3 * tilts)
    for e in range(pairs):
        for c in range(chips):
            for t in range(tilts):
                start = ((e * chips + c) * tilts + t) * chunk
                for k in range(3):
                    chunks_ref[e, c, pl.ds((t * 3 + k) * chunk, chunk), :] = sums_ref[
                        k, start : start + chunk, :
                    ]


def frame_sums(reach, tilts, parts, positions, count, frames, band, probe, forward, inverse):
    vmem = pl.BlockSpec(memory_space=pltpu.VMEM)
    smem = pl.BlockSpec(memory_space=pltpu.SMEM)
    return pl.pallas_call(
        functools.partial(frames_kernel, reach, tilts),
        out_shape=[
            jax.ShapeDtypeStruct(band.shape, jnp.float32),
            jax.ShapeDtypeStruct(parts, jnp.float32),
        ],
        in_specs=[vmem, smem] + [vmem] * 5,
        out_specs=[vmem] * 2,
        scratch_shapes=[
            pltpu.VMEM((3,) + probe.shape[1:], jnp.float32),
            pltpu.VMEM((GROUP, 2) + probe.shape[1:], jnp.float32),
            pltpu.SMEM(positions.shape, jnp.int32),
            pltpu.SemaphoreType.DMA,
        ],
        compiler_params=pltpu.CompilerParams(vmem_limit_bytes=24 * 1024 * 1024),
    )(positions, count, frames, band, probe, forward, inverse)


def greet(tilts, devices, meanwhile=lambda: None):
    t, p = lax.axis_index("tilt"), lax.axis_index("pos")
    barrier = pltpu.get_barrier_semaphore()
    for k in range(1, devices):
        pl.semaphore_signal(
            barrier,
            inc=1,
            device_id=(t, lax.rem(p + k, devices)),
            device_id_type=pl.DeviceIdType.MESH,
        )
    for k in range(1, tilts):
        pl.semaphore_signal(
            barrier,
            inc=1,
            device_id=(lax.rem(t + k, tilts), p),
            device_id_type=pl.DeviceIdType.MESH,
        )
    meanwhile()
    pl.semaphore_wait(barrier, devices - 1 + tilts - 1)


def send(src, dst, sem_out, sem_in, tilt, pos):
    return pltpu.make_async_remote_copy(
        src_ref=src,
        dst_ref=dst,
        send_sem=sem_out,
        recv_sem=sem_in,
        device_id=(tilt, pos),
        device_id_type=pl.DeviceIdType.MESH,
    )


def relayed(devices):
    return devices == 8


def gather_kernel(
    devices,
    field_any,
    frames_any,
    probe_any,
    fwd_any,
    inv_any,
    pos_any,
    moves_any,
    band,
    frames_ref,
    probe_ref,
    fwd_ref,
    inv_ref,
    pos_ref,
    own,
    slots,
    stage,
    raw_ref,
    moves_ref,
    out_sem,
    in_sem,
    relay_out,
    relay_in,
    local_sem,
):
    t, p = lax.axis_index("tilt"), lax.axis_index("pos")
    chip, chips = p // 2, devices // 2
    rows = own.shape[1]
    groups = own.shape[2] // LANES

    own_copy = pltpu.make_async_copy(field_any.at[0], own, local_sem.at[0])
    own_copy.start()
    loads = [
        pltpu.make_async_copy(src, dst, local_sem.at[1 + n])
        for n, (src, dst) in enumerate(
            [
                (pos_any, pos_ref),
                (probe_any, probe_ref),
                (fwd_any, fwd_ref),
                (inv_any, inv_ref),
                (moves_any, moves_ref),
                (frames_any.at[0], raw_ref),
            ]
        )
    ]
    greet(1, devices)
    own_copy.wait()

    def place(src, b):
        for c in range(2):
            for g in range(groups):
                band[c, g, pl.ds(b * rows, rows), :] = src[
                    c, :, g * LANES : (g + 1) * LANES
                ].astype(jnp.float32)

    def reorder():
        slots_of, width = raw_ref.shape[0], raw_ref.shape[1]
        some = math.gcd(slots_of, 4)

        @pl.loop(0, slots_of // some)
        def _(i):
            moved = jnp.dot(
                jnp.concatenate([raw_ref[i * some + n] for n in range(some)], 0),
                moves_ref[1],
                preferred_element_type=jnp.float32,
            ).astype(jnp.bfloat16)
            for n in range(some):
                frames_ref[i * some + n] = jnp.dot(
                    moves_ref[0],
                    moved[n * width : (n + 1) * width],
                    preferred_element_type=jnp.float32,
                ).astype(frames_ref.dtype)

    def role(odd):
        partner = p - 1 if odd else p + 1
        has_left, has_right = chip > 0, chip < chips - 1
        near, far = (3, 4) if odd else (1, 0)
        onward = 4 if odd else 0
        from_partner = 1 if odd else 3
        opposite = 0 if odd else 4
        outer, inner = (has_right, has_left) if odd else (has_left, has_right)
        slot_left, slot_right = (4, 1) if odd else (3, 0)
        pos_left, pos_right = 2 * chip - 1, 2 * chip + 2

        def copy(src, slot, c, out, pos):
            return send(
                src.at[c], slots.at[slot, c], out_sem.at[out, c], in_sem.at[slot, c], t, pos
            )

        to_left = [copy(own, slot_left, c, 1, pos_left) for c in range(2)]
        to_right = [copy(own, slot_right, c, 2, pos_right) for c in range(2)]
        to_partner = [copy(own, 3 if odd else 1, c, 0, partner) for c in range(2)]
        forward = [copy(slots.at[near], onward, c, 3, partner) for c in range(2)]

        def arrived(slot, c):
            copy(own, slot, c, 0, partner).wait_recv()

        to_near, to_far = (to_right, to_left) if odd else (to_left, to_right)
        has_near, has_far = (has_right, has_left) if odd else (has_left, has_right)
        if relayed(devices):
            across = lax.rem(p + 4, 8)
            source, relay = (chip == 2, chip == 0) if odd else (chip == 1, chip == 3)
            slot_far, pos_far = (slot_left, 3) if odd else (slot_right, 4)
            direct = has_far & ~source
            to_stage = [
                send(own.at[c], stage.at[c], relay_out.at[0, c], relay_in.at[c], t, across)
                for c in range(2)
            ]
            staged = [
                send(
                    stage.at[c],
                    slots.at[slot_far, c],
                    relay_out.at[1, c],
                    in_sem.at[slot_far, c],
                    t,
                    pos_far,
                )
                for c in range(2)
            ]
        else:
            direct = has_far
        for c in range(2):
            if relayed(devices):
                pl.when(source)(to_stage[c].start)
            pl.when(has_near)(to_near[c].start)
        for c in range(2):
            pl.when(direct)(to_far[c].start)
        for c in range(2):
            to_partner[c].start()
        for load in loads:
            load.start()
        for c in range(2):
            band[c, groups] = jnp.zeros(band.shape[2:], jnp.float32)
        place(own, 2)
        for c in range(2):
            arrived(from_partner, c)
        place(slots.at[from_partner], from_partner)
        for load in loads:
            load.wait()
        reorder()
        if relayed(devices):

            @pl.when(relay)
            def _():
                for c in range(2):
                    to_stage[c].wait_recv()
                    staged[c].start()

        @pl.when(outer)
        def _():
            for c in range(2):
                arrived(near, c)
                forward[c].start()
            place(slots.at[near], near)
            for c in range(2):
                arrived(far, c)
            place(slots.at[far], far)

        @pl.when(inner)
        def _():
            for c in range(2):
                arrived(opposite, c)
            place(slots.at[opposite], opposite)

        for c in range(2):
            pl.when(has_near)(to_near[c].wait_send)
            pl.when(direct)(to_far[c].wait_send)
            if relayed(devices):
                pl.when(source)(to_stage[c].wait_send)
                pl.when(relay)(staged[c].wait_send)
        for c in range(2):
            to_partner[c].wait_send()
            pl.when(outer)(forward[c].wait_send)

    pl.when(lax.rem(p, 2) == 0)(lambda: role(False))
    pl.when(lax.rem(p, 2) == 1)(lambda: role(True))


def gather(devices, field, frames, probe, forward, inverse, positions, moves):
    hbm = pl.BlockSpec(memory_space=pltpu.HBM)
    vmem = pl.BlockSpec(memory_space=pltpu.VMEM)
    _, planes, rows, columns = field.shape
    block = (planes, rows, columns)
    groups = columns // LANES
    dma = pltpu.SemaphoreType.DMA
    held = 4 * planes * (groups + 1) * 5 * rows * LANES + sum(
        a.size * a.dtype.itemsize for a in (frames, probe, forward, inverse)
    )
    return pl.pallas_call(
        functools.partial(gather_kernel, devices),
        out_shape=[
            pltpu.VMEM((planes, groups + 1, 5 * rows, LANES), jnp.float32),
            pltpu.VMEM(frames.shape[1:], frames.dtype),
            pltpu.VMEM(probe.shape, probe.dtype),
            pltpu.VMEM(forward.shape, forward.dtype),
            pltpu.VMEM(inverse.shape, inverse.dtype),
            pltpu.VMEM(positions.shape, positions.dtype),
        ],
        in_specs=[hbm] * 7,
        out_specs=[vmem] * 6,
        scratch_shapes=[
            pltpu.VMEM(block, field.dtype),
            pltpu.VMEM((5,) + block, field.dtype),
            pltpu.VMEM(block, field.dtype),
            pltpu.VMEM(frames.shape[1:], frames.dtype),
            pltpu.VMEM(moves.shape, moves.dtype),
            dma((4, 2)),
            dma((5, 2)),
            dma((2, 2)),
            dma((2,)),
            dma((7,)),
        ],
        compiler_params=pltpu.CompilerParams(
            collective_id=1, has_side_effects=True, vmem_limit_bytes=62 * 1024 * 1024 - held
        ),
    )(field, frames, probe, forward, inverse, positions, moves)


def exchange_kernel(tilts, devices, *refs):
    grads, sums, mine, from_left, from_right, result = refs[:6]
    extra, near, distant, stage = refs[6:10]
    half, got0, got1, plane, column, got2 = refs[10:16]
    obj_out, obj_in, stage_out, stage_in = refs[16:20]
    out0, in0, out1, in1, out2, in2, out3, in3, out4, in4, out5, in5 = refs[20:]
    t, p = lax.axis_index("tilt"), lax.axis_index("pos")
    chip, chips = p // 2, devices // 2
    e = lax.rem(p, 2)
    partner = p + 1 - 2 * e
    groups, rows = mine.shape[1:3]
    chunk = column.shape[0] // 2
    relay = relayed(devices)

    def meanwhile():
        start = pl.multiple_of(4 * rows * e, 8)
        for c in range(2):
            distant[c] = grads[c, 0:groups, pl.ds(start, rows), :].astype(distant.dtype)

    greet(tilts, devices, meanwhile)

    def block(b):
        return grads.at[:, pl.ds(0, groups), pl.ds(b * rows, rows), :]

    chips_rows = half.shape[1]
    pieces = out0.shape[0]
    piece = chips_rows // pieces
    per = tilts // pieces

    def cut(n):
        return pl.ds(n * piece, piece)

    swap = [
        send(
            sums.at[1 - e, :, cut(n), :], got0.at[:, cut(n), :], out0.at[n], in0.at[n], t, partner
        )
        for n in range(pieces)
    ]

    def objects(odd, step):
        has = chip < chips - 1 if odd else chip > 0
        way = 1 if odd else -1
        middle = (chip == 1) if odd else (chip == 2)
        corner = (chip == 3) if odd else (chip == 0)
        lands = from_left if odd else from_right
        side = 0 if odd else 1
        across = lax.rem(p + 4, 8)

        def out(src, n, c, pos):
            return send(src.at[c], lands.at[c], obj_out.at[n, c], obj_in.at[side, c], t, pos)

        far = [out(distant, 0, c, p + 2 * way) for c in range(2)]
        close = [out(near, 1, c, p + way) for c in range(2)]
        to_extra = send(
            block(0 if odd else 4), extra, obj_out.at[2, 0], obj_in.at[2, 0], t, partner
        )
        to_mine = send(block(1 if odd else 3), mine, obj_out.at[2, 1], obj_in.at[2, 1], t, partner)
        if relay:
            up = [
                send(src.at[1], stage.at[n], stage_out.at[n], stage_in.at[n], t, across)
                for n, src in enumerate([distant, near])
            ]
            onto = [(5, 4), (2, 3)][side]
            on = [
                send(stage.at[n], lands.at[1], stage_out.at[2 + n], obj_in.at[side, 1], t, onto[n])
                for n in range(2)
            ]
        if step == 0:
            to_extra.start()
            if relay:
                pl.when(middle)(up[0].start)
        elif step == 1:
            if relay:
                pl.when(has)(far[0].start)
                pl.when(has & ~middle)(far[1].start)
            else:
                pl.when(has)(far[0].start)
                pl.when(has)(far[1].start)
            to_mine.start()
            to_extra.wait_recv()
            b = 3 if odd else 1
            for c in range(2):
                near[c] = (
                    grads[c, 0:groups, pl.ds(b * rows, rows), :] + extra[c]
                ).astype(near.dtype)
            pl.when(has)(close[0].start)
            if relay:
                pl.when(middle)(up[1].start)

                @pl.when(corner)
                def _():
                    up[0].wait_recv()
                    on[0].start()
        elif step == 2:
            if relay:
                pl.when(has & ~middle)(close[1].start)

                @pl.when(corner)
                def _():
                    up[1].wait_recv()
                    on[1].start()
            else:
                pl.when(has)(close[1].start)
        else:
            to_mine.wait_recv()
            to_extra.wait_send()
            to_mine.wait_send()
            pl.when(has)(far[0].wait_send)
            pl.when(has)(close[0].wait_send)
            if relay:
                for n, direct in enumerate([far[1], close[1]]):
                    pl.when(has & ~middle)(direct.wait_send)
                    pl.when(middle)(up[n].wait_send)
                    pl.when(corner)(on[n].wait_send)
            else:
                pl.when(has)(far[1].wait_send)
                pl.when(has)(close[1].wait_send)

    def both(step):
        pl.when(e == 0)(lambda: objects(False, step))
        pl.when(e == 1)(lambda: objects(True, step))

    for copy in swap:
        copy.start()
    both(0)
    round1 = []
    for n in range(pieces):
        swap[n].wait_recv()
        half[:, cut(n), :] = (sums[e, :, cut(n), :] + got0[:, cut(n), :]).astype(half.dtype)
        for k in range(1, chips):
            other = lax.rem(chip + k, chips)
            round1.append(
                send(
                    half.at[other, cut(n)],
                    got1.at[k - 1, cut(n)],
                    out1.at[n, k - 1],
                    in1.at[n, k - 1],
                    t,
                    2 * other + e,
                )
            )
            round1[-1].start()
    both(1)
    for n in range(pieces):
        total = sums[e, chip, cut(n)] + got0[chip, cut(n)]
        for k in range(1, chips):
            round1[n * (chips - 1) + k - 1].wait_recv()
            total = total + got1[k - 1, cut(n)].astype(jnp.float32)
        for s in range(per):
            other = n * per + s
            plane[other] = total[s * 3 * chunk : (s + 1) * 3 * chunk]

            @pl.when(t != other)
            def _(other=other):
                k = lax.rem(other - t + tilts, tilts) - 1
                send(plane.at[other], got2.at[k], out2.at[k], in2.at[k], other, p).start()

    total = plane[t]
    for k in range(1, tilts):
        send(plane.at[0], got2.at[k - 1], out2.at[k - 1], in2.at[k - 1], t, partner).wait_recv()
        total = total + got2[k - 1]
    below = total[2 * chunk :]
    column[...] = total[: 2 * chunk] / jnp.concatenate([below, below], 0)
    result[e, chip, t] = column[...]
    round3 = []
    for k in range(1, tilts):
        other = lax.rem(t + k, tilts)
        round3.append(
            send(column, result.at[e, chip, t], out3.at[k - 1], in3.at[k - 1], other, p)
        )
        round3[-1].start()
    order = sorted(range(tilts), key=lambda m: min(m, tilts - m))
    round4 = []
    for m in order:
        whose = lax.rem(t - m + tilts, tilts)
        if m > 0:
            round3[m - 1].wait_recv()
        for k in range(1, chips):
            other = lax.rem(chip + k, chips)
            round4.append(
                send(
                    result.at[e, chip, whose],
                    result.at[e, chip, whose],
                    out4.at[m, k - 1],
                    in4.at[m, k - 1],
                    t,
                    2 * other + e,
                )
            )
            round4[-1].start()
    both(2)
    back = []
    for n, m in enumerate(order):
        whose = lax.rem(t - m + tilts, tilts)
        for k in range(1, chips):
            round4[n * (chips - 1) + k - 1].wait_recv()
        back.append(
            send(result.at[e, :, whose], result.at[e, :, whose], out5.at[m], in5.at[m], t, partner)
        )
        back[-1].start()
    both(3)
    for side, has, landed in [(0, chip > 0, from_left), (1, chip < chips - 1, from_right)]:

        @pl.when(has)
        def _():
            for c in range(2):
                send(
                    near.at[c], landed.at[c], obj_out.at[1, c], obj_in.at[side, c], t, partner
                ).wait_recv()

    for copy in back:
        copy.wait_recv()
    for copy in swap + round1 + round3 + round4 + back:
        copy.wait_send()
    for k in range(1, tilts):
        send(plane.at[0], got2.at[k - 1], out2.at[k - 1], in2.at[k - 1], t, partner).wait_send()


def exchange(tilts, devices, width, rows, grads, sums):
    vmem = pl.BlockSpec(memory_space=pltpu.VMEM)
    planes, groups = grads.shape[0], grads.shape[1] - 1
    _, chips, part, _ = sums.shape
    third = part // tilts
    pieces = 2 if tilts % 2 == 0 and part % 32 == 0 else 1
    block = (planes, groups, rows, LANES)
    dma = pltpu.SemaphoreType.DMA
    f32, bf16 = jnp.float32, jnp.bfloat16
    return pl.pallas_call(
        functools.partial(exchange_kernel, tilts, devices),
        out_shape=[
            pltpu.VMEM(block, f32),
            pltpu.VMEM(block, bf16),
            pltpu.VMEM(block, bf16),
            pltpu.VMEM((2, chips, tilts, 2 * third // 3, width), f32),
        ],
        in_specs=[vmem] * 2,
        out_specs=[vmem] * 4,
        scratch_shapes=[pltpu.VMEM(block, f32)]
        + [pltpu.VMEM(block, bf16)] * 2
        + [
            pltpu.VMEM((2,) + block[1:], bf16),
            pltpu.VMEM((chips, part, width), bf16),
            pltpu.VMEM((chips, part, width), f32),
            pltpu.VMEM((chips - 1, part, width), bf16),
            pltpu.VMEM((tilts, third, width), f32),
            pltpu.VMEM((2 * third // 3, width), f32),
            pltpu.VMEM((tilts - 1, third, width), f32),
        ]
        + [dma((3, 2)), dma((3, 2)), dma((4,)), dma((2,))]
        + [dma((pieces,))] * 2
        + [dma((pieces, chips - 1))] * 2
        + [dma((tilts - 1,))] * 4
        + [dma((tilts, chips - 1))] * 2
        + [dma((tilts,))] * 2,
        compiler_params=pltpu.CompilerParams(
            collective_id=2, has_side_effects=True, vmem_limit_bytes=20 * 1024 * 1024
        ),
    )(grads, sums)


def finish_kernel(
    devices, total, mine, left, right, result, object_any, probe_any, object_ref, probe_ref, sems
):
    p = lax.axis_index("pos")
    has_left, has_right = p >= 2, p < devices - 2
    groups, rows = mine.shape[1:3]
    pairs, chips, tilts, part, _ = result.shape
    chunk = part // 2
    copies = []

    def leave(src, dst):
        copies.append(pltpu.make_async_copy(src, dst, sems.at[len(copies)]))
        copies[-1].start()

    for k in range(2):
        for i in range(pairs):
            for c in range(chips):
                for s in range(tilts):
                    start = ((i * chips + c) * tilts + s) * chunk
                    probe_ref[k, start : start + chunk, :] = result[
                        i, c, s, k * chunk : (k + 1) * chunk, :
                    ]
        leave(probe_ref.at[k], probe_any.at[k])
    for c in range(2):
        for g in range(groups):
            object_ref[c, :, g * LANES : (g + 1) * LANES] = (
                total[c, g, pl.ds(2 * rows, rows), :]
                + mine[c, g]
                + jnp.where(has_left, left[c, g].astype(jnp.float32), 0.0)
                + jnp.where(has_right, right[c, g].astype(jnp.float32), 0.0)
            )
        leave(object_ref.at[c], object_any.at[0, c])
    for copy in copies:
        copy.wait()


def finish(devices, width, total, mine, left, right, result):
    planes, groups, rows, _ = mine.shape
    vmem = pl.BlockSpec(memory_space=pltpu.VMEM)
    hbm = pl.BlockSpec(memory_space=pltpu.HBM)
    f32 = jnp.float32
    shapes = [(planes, rows, groups * LANES), (2, width, width)]
    return pl.pallas_call(
        functools.partial(finish_kernel, devices),
        out_shape=[
            jax.ShapeDtypeStruct((1,) + shapes[0], f32),
            jax.ShapeDtypeStruct(shapes[1], f32),
        ],
        in_specs=[vmem] * 5,
        out_specs=[hbm] * 2,
        scratch_shapes=[pltpu.VMEM(shape, f32) for shape in shapes]
        + [pltpu.SemaphoreType.DMA((4,))],
        compiler_params=pltpu.CompilerParams(vmem_limit_bytes=16 * 1024 * 1024),
    )(total, mine, left, right, result)


def local(tilts, devices, intensity, positions, counts, object_field, probe):
    width = probe.shape[-1]
    rows = object_field.shape[2]
    reach = width // rows
    assert reach == 2 and devices % 2 == 0
    forward, inverse = dft_tables(width)
    row_order, column_order = orders(width)
    identity = np.eye(width, dtype=np.float32)
    moves = jnp.asarray(
        np.stack([identity[row_order], identity[column_order].T]).astype(ml_dtypes.bfloat16)
    )
    band, frames, probe_v, forward, inverse, places = gather(
        devices, object_field, intensity, probe, forward, inverse, positions[0].T, moves
    )
    parts = (2, devices // 2, 3 * width // devices, width)
    grads, sums = frame_sums(
        reach, tilts, parts, places, counts, frames, band, probe_v, forward, inverse
    )
    parts = exchange(tilts, devices, width, rows, grads, sums)
    return tuple(finish(devices, width, grads, *parts))


def solution(mesh):
    placed = (
        P("tilt", "pos", None, None),
        P("tilt", "pos", None),
        P("tilt", "pos"),
        P("tilt", None, "pos", None),
        P(),
    )
    return jax.shard_map(
        functools.partial(local, mesh.shape["tilt"], mesh.shape["pos"]),
        mesh=mesh,
        in_specs=placed,
        out_specs=(P("tilt", None, "pos", None), P()),
        check_vma=False,
    )
```
